32 devices in a mesh: seq: 8 (over y, x, core), wt: 4 (over z).
Axes of the slice: x: 2, y: 2, z: 4, core: 2. Of those that a mesh axis runs over, the one named last changes fastest.
Arguments:
- tokens: bfloat16 [8, 224, 112, 128], P(None, 'seq', 'wt'), may hold values from -6 to 6
- region: int32 [8, 224, 112], P(None, 'seq', 'wt'), may hold values from 0 to 3
- rel_index: int32 [49, 49], replicated, may hold values from 0 to 168
- norm_gain: float32 [2, 2, 128], replicated, may hold values from 0.5 to 1.5
- norm_bias: float32 [2, 2, 128], replicated, may hold values from -3 to 3
- w_qkv: bfloat16 [2, 128, 384], P(None, 'wt'), may hold values from -0.5 to 0.5
- qv_bias: float32 [2, 2, 128], replicated, may hold values from -3 to 3
- pos_table: float32 [2, 169, 4], replicated, may hold values from -4 to 4
- w_proj: bfloat16 [2, 128, 128], P(None, 'wt'), may hold values from -1 to 1
- out_bias: float32 [2, 2, 128], replicated, may hold values from -2 to 2
- w_fc1: bfloat16 [2, 128, 512], P(None, 'wt'), may hold values from -0.5 to 0.5
- fc1_bias: float32 [2, 512], replicated, may hold values from -3 to 3
- w_fc2: bfloat16 [2, 512, 128], P(None, 'wt'), may hold values from -0.375 to 0.375
- cotangent: bfloat16 [8, 224, 112, 128], P(None, 'seq', 'wt'), may hold values from -6 to 6
Outputs:
- mixed: bfloat16 [8, 224, 112, 128], P(None, 'seq', 'wt')
- tokens_grad: float32 [8, 224, 112, 128], P(None, 'seq', 'wt')
- norm_gain_grad: float32 [2, 2, 128], replicated
- norm_bias_grad: float32 [2, 2, 128], replicated
- w_qkv_grad: float32 [2, 128, 384], P(None, 'wt')
- qv_bias_grad: float32 [2, 2, 128], replicated
- pos_table_grad: float32 [2, 169, 4], replicated
- w_proj_grad: float32 [2, 128, 128], P(None, 'wt')
- out_bias_grad: float32 [2, 2, 128], replicated
- w_fc1_grad: float32 [2, 128, 512], P(None, 'wt')
- fc1_bias_grad: float32 [2, 512], replicated
- w_fc2_grad: float32 [2, 512, 128], P(None, 'wt')
The draws below stay inside these ranges and needn't reach their ends.
Inputs may be any that keep to these rules, and one draw needn't show every extreme that they name: `region`: region ids of the shifted layer's tokens, in shifted coordinates.
All inputs are finite; a program needn't handle non-finite values.
Results may differ from the reference program's by a relative error of at most 0.019.
Values may be sent and summed in bfloat16 or wider, within the bound.
No kernel may reach another device: no remote copies, remote signals or barrier semaphores. Data moves between devices by JAX's collectives and lax.ppermute only.
A program may use at most 320 MiB of HBM per device.

```python
import math
import jax
import jax.numpy as jnp
from jax import lax

D = 128
HEADS = 4
FF = 512
WIN = 7
SHIFT = 3
BATCH = 8
HEAD_DIM = 32
TABLE = 169
HEIGHT = 224
WIDTH = 112


def plant(values, stream_key, least, largest):
    place = [jax.random.randint(jax.random.fold_in(stream_key, axis), (), 0, length) for axis, length in enumerate(values.shape)]
    widest = values.shape.index(max(values.shape))
    next_to = place[:widest] + [(place[widest] + 1) % values.shape[widest]] + place[widest + 1:]
    return values.at[tuple(place)].set(least).at[tuple(next_to)].set(largest)


def block_levels(stream_key, extent, cuts, least, top_value):
    gain = 1.0
    for dim, parts in cuts:
        heights = jax.random.uniform(jax.random.fold_in(jax.random.fold_in(stream_key, 6), dim), (parts,), jnp.float32, least / len(cuts), top_value / len(cuts))
        gain = gain * jnp.repeat(jnp.exp(heights), extent[dim] // parts).reshape((-1,) + (1,) * (len(extent) - 1 - dim))
    return gain


def gaussian(stream_key, shape, spread, reach, cuts=(), dtype=jnp.bfloat16):
    loudness = block_levels(stream_key, shape, cuts, -0.22, 0.18) if cuts else 1.0
    drawn = jax.random.normal(stream_key, shape, jnp.float32) * spread * loudness
    return jnp.minimum(jnp.maximum(drawn, -reach), reach).astype(dtype)


def setup_inputs(seed: int = 0) -> dict:
    keys = jax.random.split(jax.random.key(seed), 15)
    return {
        "tokens": gaussian(keys[0], (BATCH, HEIGHT, WIDTH, D), 1.0, 6.0, ((1, 8), (2, 4))),
        "region": plant(jax.random.randint(keys[1], (BATCH, HEIGHT, WIDTH), 0, 4), jax.random.fold_in(keys[1], 1), 0, 3).astype(jnp.int32),
        "rel_index": plant(jax.random.randint(keys[2], (WIN * WIN, WIN * WIN), 0, TABLE), jax.random.fold_in(keys[2], 1), 0, TABLE - 1).astype(jnp.int32),
        "norm_gain": jnp.clip(1.0 + 0.1 * jax.random.normal(keys[3], (2, 2, D), jnp.float32), 0.5, 1.5),
        "norm_bias": gaussian(keys[4], (2, 2, D), 0.5, 3.0, (), jnp.float32),
        "w_qkv": gaussian(keys[5], (2, D, 3 * D), D ** -0.5, 0.5, ((1, 4),)),
        "qv_bias": gaussian(keys[6], (2, 2, D), 0.5, 3.0, (), jnp.float32),
        "pos_table": gaussian(keys[7], (2, TABLE, HEADS), 1.0, 4.0, (), jnp.float32),
        "w_proj": gaussian(keys[8], (2, D, D), (D // 4) ** -0.5, 1.0, ((1, 4),)),
        "out_bias": gaussian(keys[9], (2, 2, D), 0.3, 2.0, (), jnp.float32),
        "w_fc1": gaussian(keys[10], (2, D, FF), D ** -0.5, 0.5, ((1, 4),)),
        "fc1_bias": gaussian(keys[11], (2, FF), 0.5, 3.0, (), jnp.float32),
        "w_fc2": gaussian(keys[12], (2, FF, D), (FF // 2) ** -0.5, 0.375, ((1, 4),)),
        "cotangent": gaussian(keys[13], (BATCH, HEIGHT, WIDTH, D), 1.0, 6.0, ((1, 8), (2, 4))),
    }


@jax.custom_vjp
def low(v):
    return lax.optimization_barrier(v.astype(jnp.bfloat16)).astype(jnp.float32)

@jax.custom_vjp
def low_back(v):
    return v

def low_keep(v):
    return (low(v), None)

def low_pass(kept, grad):
    return (grad,)

def back_keep(v):
    return (v, None)

def back_low(kept, grad):
    return (low(grad),)
low.defvjp(low_keep, low_pass)
low_back.defvjp(back_keep, back_low)
EPSILON = 1e-05
HIGH = lax.Precision.HIGHEST

def matmul(left, right):
    return jnp.matmul(left, right, precision=HIGH)

def layer_norm(field, norm_scale, norm_shift):
    average = lax.optimization_barrier(jnp.mean(field, -1, keepdims=True))
    centred = field - average
    variance = lax.optimization_barrier(jnp.mean(centred * centred, -1, keepdims=True))
    return centred * lax.rsqrt(variance + EPSILON) * norm_scale + norm_shift

def to_windows(field):
    window_rows = field.shape[0] // WIN
    window_cols = field.shape[1] // WIN
    blocks = field.reshape(window_rows, WIN, window_cols, WIN, field.shape[-1])
    return blocks.transpose(0, 2, 1, 3, 4).reshape(window_rows * window_cols, WIN * WIN, field.shape[-1])

def from_windows(blocks, height, width):
    window_rows = height // WIN
    window_cols = width // WIN
    field = blocks.reshape(window_rows, window_cols, WIN, WIN, blocks.shape[-1])
    return field.transpose(0, 2, 1, 3, 4).reshape(height, width, blocks.shape[-1])

def swin_layer(stream, params, layer, shifted, mask_add, rel_index):
    norm_gain, norm_bias, w_qkv, qv_bias, pos_table, w_proj, out_bias, w_fc1, fc1_bias, w_fc2 = params
    height, width = (stream.shape[0], stream.shape[1])
    hidden = low(layer_norm(stream, norm_gain[layer, 0], norm_bias[layer, 0]))
    if shifted:
        hidden = low_back(hidden)
        hidden = jnp.roll(hidden, (-SHIFT, -SHIFT), (0, 1))
    windows = to_windows(hidden)
    window_count = windows.shape[0]
    zeros = jnp.zeros((D,), jnp.float32)
    projected = matmul(windows, w_qkv[layer]) + jnp.concatenate([qv_bias[layer, 0], zeros, qv_bias[layer, 1]])
    heads_shape = (window_count, WIN * WIN, HEADS, HEAD_DIM)
    query_heads = low_back(low(projected[..., :D])).reshape(heads_shape)
    key_heads = low_back(low(projected[..., D:2 * D])).reshape(heads_shape)
    value_heads = low_back(low(projected[..., 2 * D:])).reshape(heads_shape)
    rel_bias = pos_table[layer][rel_index].transpose(2, 0, 1)
    scale = 1.0 / math.sqrt(HEAD_DIM)
    scores = jnp.einsum('wihd,wjhd->whij', query_heads, key_heads, precision=HIGH) * scale + rel_bias[None]
    if shifted:
        scores = scores + mask_add[:, None]
    scores = low_back(scores)
    attention = low(jax.nn.softmax(scores, -1))
    attended = jnp.einsum('whij,wjhd->wihd', attention, value_heads, precision=HIGH).reshape(window_count, WIN * WIN, D)
    attended = low_back(low(attended))
    attended = from_windows(attended, height, width)
    if shifted:
        attended = jnp.roll(attended, (SHIFT, SHIFT), (0, 1))
    branch = low_back(matmul(attended, w_proj[layer]) + out_bias[layer, 0])
    middle = stream + branch
    inner = low(layer_norm(middle, norm_gain[layer, 1], norm_bias[layer, 1]))
    expanded = low_back(matmul(inner, w_fc1[layer]) + fc1_bias[layer])
    activated = low(jax.nn.gelu(expanded, approximate=False))
    return middle + low_back(matmul(activated, w_fc2[layer]) + out_bias[layer, 1])

def reference(tokens, region, rel_index, norm_gain, norm_bias, w_qkv, qv_bias, pos_table, w_proj, out_bias, w_fc1, fc1_bias, w_fc2, cotangent):
    params = (norm_gain, norm_bias, w_qkv.astype(jnp.float32), qv_bias, pos_table, w_proj.astype(jnp.float32), out_bias, w_fc1.astype(jnp.float32), fc1_bias, w_fc2.astype(jnp.float32))

    def image_step(totals, inputs):
        image, region_map, seed_grad = inputs
        region_ids = to_windows(region_map[..., None])[..., 0]
        mask_add = jnp.where(region_ids[:, :, None] == region_ids[:, None, :], 0.0, -100.0).astype(jnp.float32)

        def forward(field, weights):
            middle = swin_layer(field, weights, 0, False, mask_add, rel_index)
            return swin_layer(middle, weights, 1, True, mask_add, rel_index)
        output, pullback = jax.vjp(forward, image.astype(jnp.float32), params)
        image_grad, weight_grads = pullback(seed_grad.astype(jnp.float32))
        totals = jax.tree.map(lambda left, right: left + right, totals, weight_grads)
        return (totals, (output.astype(jnp.bfloat16), image_grad))
    starting = jax.tree.map(jnp.zeros_like, params)
    totals, (outputs, gradients) = lax.scan(image_step, starting, (tokens, region, cotangent))
    return (outputs, gradients, totals[0], totals[1], totals[2], totals[3], totals[4], totals[5], totals[6], totals[7], totals[8], totals[9])
```

```python
import math

import jax
import jax.numpy as jnp
from jax import lax
from jax.experimental import pallas as pl
from jax.experimental.pallas import tpu as pltpu
from jax.sharding import PartitionSpec as P

HEADS = 4
WIN = 7
SHIFT = 3
HEAD_DIM = 32
EPSILON = 1e-05
POS = WIN * WIN
SLOT = 64
LOG2E = math.log2(math.e)
SCALE = 1.0 / math.sqrt(HEAD_DIM)
OFF = -1e30
BF = jnp.bfloat16
F32 = jnp.float32
VMEM_LIMIT = 56 * 1024 * 1024


def mm(left, right):
    return lax.dot_general(left, right, (((1,), (0,)), ((), ())), preferred_element_type=F32)


def mm_nt(left, right):
    return lax.dot_general(left, right, (((1,), (1,)), ((), ())), preferred_element_type=F32)


def mm_tn(left, right):
    return lax.dot_general(left, right, (((0,), (0,)), ((), ())), preferred_element_type=F32)


def norm_parts(field):
    centred = field - jnp.mean(field, -1, keepdims=True)
    inverse = lax.rsqrt(jnp.mean(centred * centred, -1, keepdims=True) + EPSILON)
    return centred * inverse, inverse


def norm_backward(upstream, normed, inverse, gain):
    scaled = upstream * gain
    return inverse * (
        scaled
        - jnp.mean(scaled, -1, keepdims=True)
        - normed * jnp.mean(scaled * normed, -1, keepdims=True)
    )


def fold_rows(field):
    rows, cols = field.shape
    return jnp.sum(field.reshape(rows // 8, 8, cols), 0)


def tokens_of(ref):
    block = ref[...].astype(F32)
    return block.reshape(-1, block.shape[-1])


def put_tokens(ref, field):
    ref[...] = field.reshape(ref.shape).astype(ref.dtype)


def head_blocks(field):
    head = lax.broadcasted_iota(jnp.int32, field.shape, 1) >> 5
    return jnp.concatenate(
        [jnp.where(head == h, field, 0.0).astype(BF) for h in range(HEADS)], 0
    )


def gather_heads(stacked):
    head = lax.broadcasted_iota(jnp.int32, (SLOT, stacked.shape[1]), 1) >> 5
    total = stacked[:SLOT]
    for h in range(1, HEADS):
        total = jnp.where(head == h, stacked[h * SLOT : (h + 1) * SLOT], total)
    return total


def lane_segments():
    row = lax.broadcasted_iota(jnp.int32, (HEADS * SLOT, HEADS * SLOT), 0) >> 6
    col = lax.broadcasted_iota(jnp.int32, (HEADS * SLOT, HEADS * SLOT), 1) >> 6
    return jnp.where(row == col, 1.0, 0.0).astype(BF)


def head_lanes():
    row = lax.broadcasted_iota(jnp.int32, (HEADS * SLOT, HEADS * HEAD_DIM), 0) >> 6
    col = lax.broadcasted_iota(jnp.int32, (HEADS * SLOT, HEADS * HEAD_DIM), 1) >> 5
    return jnp.where(row == col, 1.0, 0.0).astype(BF)


def segment_max(scores):
    low = lax.broadcasted_iota(jnp.int32, (SLOT, 2 * SLOT), 1) < SLOT
    parts = []
    for start in (0, 2 * SLOT):
        pair = scores[:, start : start + 2 * SLOT]
        first = jnp.max(jnp.where(low, pair, OFF), 1, keepdims=True)
        second = jnp.max(jnp.where(low, OFF, pair), 1, keepdims=True)
        parts.append(jnp.where(low, first, second))
    return jnp.concatenate(parts, 1)


def zero_tails(first_step, count, *refs):
    @pl.when(first_step)
    def _():
        for ref in refs:
            ref[count:, :] = jnp.zeros((ref.shape[0] - count, ref.shape[1]), F32)


def first_of_grid():
    return (pl.program_id(0) == 0) & (pl.program_id(1) == 0)


def window(ref, image, images):
    return ref[pl.ds(image, SLOT, stride=images), :]


def attention_forward(images, parts, bias, masks, probs_ref, out_ref):
    sc_q, sc_k, sc_v = parts
    segments = lane_segments()
    everything = range(images)
    scores = [
        mm_nt(window(sc_q, i, images).astype(BF), head_blocks(window(sc_k, i, images)))
        * (SCALE * LOG2E)
        + bias
        for i in everything
    ]
    if masks is not None:
        apart = [masks[0, 0, i].astype(F32) * (-100.0 * LOG2E) for i in everything]
        scores = [scores[i] + jnp.concatenate([apart[i], apart[i]], 1) for i in everything]
    powers = [jnp.exp2(s - segment_max(s)) for s in scores]
    sums = [mm(p.astype(BF), segments) for p in powers]
    probs = [(p / s).astype(BF) for p, s in zip(powers, sums)]
    for i in everything:
        probs_ref[0, 0, i] = probs[i]
        out_ref[pl.ds(i, SLOT, stride=images), :] = mm(
            probs[i], head_blocks(window(sc_v, i, images))
        )


def attention_backward(images, parts, sc_grad, sc_out, probs_ref, grads, bias_acc):
    sc_q, sc_k, sc_v = parts
    sc_dq, sc_dk, sc_dv = grads
    lanes = head_lanes()
    everything = range(images)
    upstream = [window(sc_grad, i, images) for i in everything]
    centred = [
        mm_nt(
            jnp.concatenate(
                [
                    upstream[i].astype(BF),
                    (-(upstream[i] * window(sc_out, i, images))).astype(BF),
                ],
                1,
            ),
            jnp.concatenate([head_blocks(window(sc_v, i, images)), lanes], 1),
        )
        for i in everything
    ]
    probs = [probs_ref[0, 0, i] for i in everything]
    score_grads = [(probs[i].astype(F32) * centred[i]).astype(BF) for i in everything]
    total = score_grads[0].astype(F32)
    for i in everything[1:]:
        total = total + score_grads[i].astype(F32)
    bias_acc[...] += total
    for i in everything:
        place = pl.ds(i, SLOT, stride=images)
        sc_dq[place, :] = mm(score_grads[i], head_blocks(window(sc_k, i, images))) * SCALE
        sc_dk[place, :] = (
            gather_heads(mm_tn(score_grads[i], window(sc_q, i, images).astype(BF))) * SCALE
        )
        sc_dv[place, :] = gather_heads(mm_tn(probs[i], upstream[i].astype(BF)))


def split_projection(hidden, w_qkv, qkv_bias, parts, count):
    projected = mm(hidden, w_qkv) + qkv_bias
    projected = projected.astype(BF).astype(F32)
    depth = hidden.shape[1]
    for n, ref in enumerate(parts):
        ref[:count, :] = projected[:, n * depth : (n + 1) * depth]


def gelu_parts(expanded):
    cumulative = 0.5 + 0.5 * lax.erf(expanded * (1.0 / math.sqrt(2.0)))
    density = jnp.exp(expanded * expanded * -0.5) * (1.0 / math.sqrt(2.0 * math.pi))
    return expanded * cumulative, cumulative + expanded * density


def kernel_first_layer(
    images, x_ref, w_qkv, w_proj, w_fc1, w_fc2, vecs, qkv_bias, fc1_bias, bias,
    stream_out, hidden_out, middle_out, out_out, probs_out, act_out, slope_out,
    sc_q, sc_k, sc_v, sc_out,
):
    count = POS * images
    zero_tails(first_of_grid(), count, sc_q, sc_k, sc_v)
    stream = tokens_of(x_ref)
    normed, _ = norm_parts(stream)
    hidden = (normed * vecs[0:1] + vecs[1:2]).astype(BF)
    split_projection(hidden, w_qkv[...], qkv_bias[...], (sc_q, sc_k, sc_v), count)
    attention_forward(images, (sc_q, sc_k, sc_v), bias[...], None, probs_out, sc_out)
    attended = sc_out[:count, :].astype(BF)
    out_out[0, 0] = attended
    middle = stream + (mm(attended, w_proj[...]) + vecs[4:5])
    middle_out[0, 0] = middle
    normed, _ = norm_parts(middle)
    inner = (normed * vecs[2:3] + vecs[3:4]).astype(BF)
    activated, slope = gelu_parts(mm(inner, w_fc1[...]) + fc1_bias[...])
    activated = activated.astype(BF)
    act_out[0, 0] = activated
    slope_out[0, 0] = slope.astype(BF)
    stream = middle + mm(activated, w_fc2[...]) + vecs[5:6]
    stream_out[0, 0] = stream
    normed, _ = norm_parts(stream)
    put_tokens(hidden_out, normed * vecs[6:7] + vecs[7:8])


def kernel_shifted_forward(
    images, hidden_ref, w_qkv, qkv_bias, bias, masks, out_out, probs_out, sc_q, sc_k, sc_v, sc_out
):
    count = POS * images
    zero_tails(first_of_grid(), count, sc_q, sc_k, sc_v)
    hidden = tokens_of(hidden_ref).astype(BF)
    split_projection(hidden, w_qkv[...], qkv_bias[...], (sc_q, sc_k, sc_v), count)
    attention_forward(images, (sc_q, sc_k, sc_v), bias[...], masks, probs_out, sc_out)
    put_tokens(out_out, sc_out[:count, :])


def feed_forward_backward(out_low, inner, activated, slope, w_fc1, w_fc2):
    expanded_low = (slope * mm_nt(out_low, w_fc2)).astype(BF)
    inner_grad = mm_nt(expanded_low, w_fc1)
    return expanded_low, inner_grad


def start_sums(refs):
    @pl.when(first_of_grid())
    def _():
        for ref in refs:
            ref[...] = jnp.zeros_like(ref)


def kernel_middle(
    images, stream_ref, out_ref, cot_ref, w_proj, w_fc1, w_fc2, vecs, fc1_bias,
    mixed_out, grad_out, low_out, g_proj, g_fc1, g_fc2, sums, fc1_sums,
):
    start_sums((g_proj, g_fc1, g_fc2, sums, fc1_sums))
    stream = stream_ref[0, 0]
    attended = tokens_of(out_ref).astype(BF)
    middle = stream + (mm(attended, w_proj[...]) + vecs[4:5])
    normed, inverse = norm_parts(middle)
    inner = (normed * vecs[2:3] + vecs[3:4]).astype(BF)
    activated, slope = gelu_parts(mm(inner, w_fc1[...]) + fc1_bias[...])
    activated = activated.astype(BF)
    put_tokens(mixed_out, middle + mm(activated, w_fc2[...]) + vecs[5:6])
    gradient = tokens_of(cot_ref)
    out_low = gradient.astype(BF)
    expanded_low, inner_grad = feed_forward_backward(
        out_low, inner, activated, slope, w_fc1[...], w_fc2[...]
    )
    g_fc2[...] += mm_tn(out_low, activated)
    g_fc1[...] += mm_tn(inner, expanded_low)
    fc1_sums[...] += fold_rows(expanded_low.astype(F32))
    norm_term = norm_backward(inner_grad, normed, inverse, vecs[2:3])
    updated = gradient + norm_term
    grad_out[0, 0] = updated
    branch_low = updated.astype(BF)
    g_proj[...] += mm_tn(attended, branch_low)
    put_tokens(low_out, mm_nt(branch_low, w_proj[...]))
    sums[0] += fold_rows(gradient)
    sums[1] += fold_rows(inner_grad * normed)
    sums[2] += fold_rows(inner_grad)
    sums[3] += fold_rows(branch_low.astype(F32))


def joined_gradients(count, grads, qv_sums):
    pieces = [ref[:count, :].astype(BF) for ref in grads]
    qv_sums[0] += fold_rows(pieces[0].astype(F32))
    qv_sums[1] += fold_rows(pieces[2].astype(F32))
    return jnp.concatenate(pieces, 1)


def kernel_shifted_backward(
    images, hidden_ref, out_ref, low_ref, probs_ref, w_qkv, qkv_bias,
    hidden_grad_out, g_qkv, qv_sums, bias_acc,
    sc_q, sc_k, sc_v, sc_out, sc_grad, sc_dq, sc_dk, sc_dv,
):
    count = POS * images
    start_sums((g_qkv, qv_sums, bias_acc))
    zero_tails(first_of_grid(), count, sc_q, sc_k, sc_v, sc_out, sc_grad)
    hidden = tokens_of(hidden_ref).astype(BF)
    split_projection(hidden, w_qkv[...], qkv_bias[...], (sc_q, sc_k, sc_v), count)
    sc_out[:count, :] = tokens_of(out_ref)
    sc_grad[:count, :] = tokens_of(low_ref)
    grads = (sc_dq, sc_dk, sc_dv)
    attention_backward(images, (sc_q, sc_k, sc_v), sc_grad, sc_out, probs_ref, grads, bias_acc)
    joined = joined_gradients(count, grads, qv_sums)
    g_qkv[...] += mm_tn(hidden, joined)
    put_tokens(hidden_grad_out, mm_nt(joined, w_qkv[...]))


def kernel_first_feed_backward(
    images, hidden_grad_ref, stream_ref, grad_ref, middle_ref, act_ref, slope_ref, att_ref,
    w_proj, w_fc1, w_fc2, vecs,
    grad_out, low_out, g_proj, g_fc1, g_fc2, sums, fc1_sums,
):
    start_sums((g_proj, g_fc1, g_fc2, sums, fc1_sums))
    upstream = tokens_of(hidden_grad_ref)
    normed, inverse = norm_parts(stream_ref[0, 0])
    gradient = grad_ref[0, 0] + norm_backward(upstream, normed, inverse, vecs[6:7])
    sums[4] += fold_rows(upstream * normed)
    sums[5] += fold_rows(upstream)
    out_low = gradient.astype(BF)
    normed, inverse = norm_parts(middle_ref[0, 0])
    inner = (normed * vecs[2:3] + vecs[3:4]).astype(BF)
    activated = act_ref[0, 0]
    expanded_low, inner_grad = feed_forward_backward(
        out_low, inner, activated, slope_ref[0, 0].astype(F32), w_fc1[...], w_fc2[...]
    )
    g_fc2[...] += mm_tn(out_low, activated)
    g_fc1[...] += mm_tn(inner, expanded_low)
    fc1_sums[...] += fold_rows(expanded_low.astype(F32))
    updated = gradient + norm_backward(inner_grad, normed, inverse, vecs[2:3])
    grad_out[0, 0] = updated
    branch_low = updated.astype(BF)
    g_proj[...] += mm_tn(att_ref[0, 0], branch_low)
    low_out[0, 0] = mm_nt(branch_low, w_proj[...]).astype(BF)
    sums[0] += fold_rows(out_low.astype(F32))
    sums[1] += fold_rows(inner_grad * normed)
    sums[2] += fold_rows(inner_grad)
    sums[3] += fold_rows(branch_low.astype(F32))


def kernel_first_attention_backward(
    images, x_ref, grad_ref, low_ref, att_ref, probs_ref, w_qkv, vecs, qkv_bias,
    tokens_grad_out, g_qkv, qv_sums, bias_acc, sums,
    sc_q, sc_k, sc_v, sc_out, sc_grad, sc_dq, sc_dk, sc_dv,
):
    count = POS * images
    start_sums((g_qkv, qv_sums, bias_acc, sums))
    zero_tails(first_of_grid(), count, sc_q, sc_k, sc_v, sc_out, sc_grad)
    normed, inverse = norm_parts(tokens_of(x_ref))
    hidden = (normed * vecs[0:1] + vecs[1:2]).astype(BF)
    split_projection(hidden, w_qkv[...], qkv_bias[...], (sc_q, sc_k, sc_v), count)
    sc_out[:count, :] = att_ref[0, 0].astype(F32)
    sc_grad[:count, :] = low_ref[0, 0].astype(F32)
    grads = (sc_dq, sc_dk, sc_dv)
    attention_backward(images, (sc_q, sc_k, sc_v), sc_grad, sc_out, probs_ref, grads, bias_acc)
    joined = joined_gradients(count, grads, qv_sums)
    g_qkv[...] += mm_tn(hidden, joined)
    upstream = mm_nt(joined, w_qkv[...])
    put_tokens(tokens_grad_out, grad_ref[0, 0] + norm_backward(upstream, normed, inverse, vecs[0:1]))
    sums[0] += fold_rows(upstream * normed)
    sums[1] += fold_rows(upstream)


def shift_by(array, axis, by):
    count = lax.axis_size(axis)
    return lax.ppermute(array, axis, [(i, (i + by) % count) for i in range(count)])


def shift_both(array, by):
    rows, cols = lax.axis_size("seq"), lax.axis_size("wt")
    pairs = [
        (r * cols + c, ((r + by) % rows) * cols + (c + by) % cols)
        for r in range(rows)
        for c in range(cols)
    ]
    return lax.ppermute(array, ("seq", "wt"), pairs)


def roll_ahead(field):
    rim_rows = shift_by(field[:SHIFT], "seq", -1)
    rim_cols = shift_by(field[:, :SHIFT], "wt", -1)
    corner = shift_both(field[:SHIFT, :SHIFT], -1)
    upper = jnp.concatenate([field[SHIFT:, SHIFT:], rim_cols[SHIFT:]], 1)
    lower = jnp.concatenate([rim_rows[:, SHIFT:], corner], 1)
    return jnp.concatenate([upper, lower], 0)


def roll_behind(field):
    rim_rows = shift_by(field[-SHIFT:], "seq", 1)
    rim_cols = shift_by(field[:, -SHIFT:], "wt", 1)
    corner = shift_both(field[-SHIFT:, -SHIFT:], 1)
    upper = jnp.concatenate([corner, rim_rows[:, :-SHIFT]], 1)
    lower = jnp.concatenate([rim_cols[:-SHIFT], field[:-SHIFT, :-SHIFT]], 1)
    return jnp.concatenate([upper, lower], 0)


def pack_second(w_fc2):
    rows, depth = w_fc2.shape
    blocks = w_fc2.reshape(4, rows // 4, depth)
    return blocks.transpose(1, 0, 2).reshape(rows // 4, 4 * depth)


def unpack_second(packed, parts):
    rows, wide = packed.shape
    depth = wide // 4
    blocks = packed.reshape(parts, rows // parts, 4, depth)
    return blocks.transpose(0, 2, 1, 3).reshape(rows * 4, depth)


def per_device(
    tokens, region, rel_index, norm_gain, norm_bias, w_qkv, qv_bias, pos_table, w_proj, out_bias,
    w_fc1, fc1_bias, w_fc2, cotangent,
):
    images, height, width, depth = tokens.shape
    wide = w_fc1.shape[-1]
    parts = lax.axis_size("wt")
    rows, cols = height // WIN, width // WIN
    count = POS * images
    table_size = pos_table.shape[1]

    weights = []
    for layer in range(2):
        packed = jnp.concatenate(
            [w_qkv[layer], w_proj[layer], w_fc1[layer], pack_second(w_fc2[layer])], 1
        )
        whole = lax.all_gather(packed, "wt", axis=0, tiled=True)
        cuts = [3 * depth, 4 * depth, 4 * depth + wide]
        qkv, proj, fc1, fc2 = jnp.split(whole, cuts, 1)
        weights.append((qkv, proj, fc1, unpack_second(fc2, parts)))

    x = tokens.transpose(1, 2, 0, 3)
    cot = cotangent.transpose(1, 2, 0, 3)
    selector = (
        rel_index.reshape(-1)[:, None] == jnp.arange(table_size, dtype=jnp.int32)[None, :]
    ).astype(F32)
    tables = jnp.dot(
        selector,
        pos_table.transpose(1, 0, 2).reshape(table_size, 2 * HEADS) * LOG2E,
        precision=lax.Precision.HIGHEST,
    ).reshape(POS, POS, 2, HEADS)
    padded = jnp.pad(
        jnp.pad(tables.transpose(2, 0, 3, 1), ((0, 0), (0, SLOT - POS), (0, 0), (0, 0))),
        ((0, 0), (0, 0), (0, 0), (0, SLOT - POS)),
        constant_values=OFF,
    )
    biases = padded.reshape(2, SLOT, HEADS * SLOT)
    ids = region.reshape(images, rows, WIN, cols, WIN).transpose(1, 3, 0, 2, 4)
    ids = ids.reshape(rows, cols, images, POS)
    apart = (ids[..., :, None] != ids[..., None, :]).astype(BF)
    apart = jnp.pad(apart, [(0, 0)] * 3 + [(0, SLOT - POS)] * 2)
    masks = jnp.concatenate([apart, apart], -1)

    zeros = jnp.zeros((depth,), F32)
    qkv_biases = [
        jnp.concatenate([qv_bias[l, 0], zeros, qv_bias[l, 1]])[None] for l in range(2)
    ]

    def vectors(layer):
        after = norm_gain[1, 0], norm_bias[1, 0]
        return jnp.stack(
            [
                norm_gain[layer, 0], norm_bias[layer, 0], norm_gain[layer, 1], norm_bias[layer, 1],
                out_bias[layer, 0], out_bias[layer, 1], *after,
            ]
        )

    vecs = [vectors(0), vectors(1)]

    field = pl.BlockSpec((WIN, WIN, images, depth), lambda r, c: (r, c, 0, 0))
    probs_spec = pl.BlockSpec((1, 1, images, SLOT, HEADS * SLOT), lambda r, c: (r, c, 0, 0, 0))
    mask_spec = pl.BlockSpec((1, 1, images, SLOT, 2 * SLOT), lambda r, c: (r, c, 0, 0, 0))

    def flat(columns):
        return pl.BlockSpec((1, 1, count, columns), lambda r, c: (r, c, 0, 0))

    def whole_of(shape):
        return pl.BlockSpec(tuple(shape), lambda r, c: (0,) * len(shape))

    field_shape = (height, width, images, depth)

    def flat_type(columns, dtype):
        return jax.ShapeDtypeStruct((rows, cols, count, columns), dtype)

    probs_type = jax.ShapeDtypeStruct((rows, cols, images, SLOT, HEADS * SLOT), BF)

    def run(kernel, inputs, outputs, slots):
        def body(*refs):
            kernel(images, *refs)

        return pl.pallas_call(
            body,
            grid=(rows, cols),
            in_specs=[spec if spec is not None else whole_of(a.shape) for a, spec in inputs],
            out_specs=[spec if spec is not None else whole_of(t.shape) for t, spec in outputs],
            out_shape=[t for t, _ in outputs],
            scratch_shapes=[pltpu.VMEM((SLOT * images, depth), F32)] * slots,
            compiler_params=pltpu.CompilerParams(vmem_limit_bytes=VMEM_LIMIT),
        )(*[a for a, _ in inputs])

    def total(*shape):
        return (jax.ShapeDtypeStruct(shape, F32), None)

    qkv0, proj0, fc10, fc20 = weights[0]
    qkv1, proj1, fc11, fc21 = weights[1]
    stream1, hidden1, middle0, att0, probs0, act0, slope0 = run(
        kernel_first_layer,
        [
            (x, field), (qkv0, None), (proj0, None), (fc10, None), (fc20, None), (vecs[0], None),
            (qkv_biases[0], None), (fc1_bias[0:1], None), (biases[0], None),
        ],
        [
            (flat_type(depth, F32), flat(depth)),
            (jax.ShapeDtypeStruct(field_shape, BF), field),
            (flat_type(depth, F32), flat(depth)),
            (flat_type(depth, BF), flat(depth)),
            (probs_type, probs_spec),
            (flat_type(wide, BF), flat(wide)),
            (flat_type(wide, BF), flat(wide)),
        ],
        4,
    )
    hidden1 = roll_ahead(hidden1)
    att1, probs1 = run(
        kernel_shifted_forward,
        [
            (hidden1, field), (qkv1, None), (qkv_biases[1], None), (biases[1], None),
            (masks, mask_spec),
        ],
        [(jax.ShapeDtypeStruct(field_shape, BF), field), (probs_type, probs_spec)],
        4,
    )
    mixed, grad1, low1, g_proj1, g_fc11, g_fc21, sums1, fc1_sums1 = run(
        kernel_middle,
        [
            (stream1, flat(depth)), (roll_behind(att1), field), (cot, field), (proj1, None),
            (fc11, None), (fc21, None), (vecs[1], None), (fc1_bias[1:2], None),
        ],
        [
            (jax.ShapeDtypeStruct(field_shape, BF), field),
            (flat_type(depth, F32), flat(depth)),
            (jax.ShapeDtypeStruct(field_shape, BF), field),
            total(depth, depth), total(depth, wide), total(depth, wide), total(4, 8, depth),
            total(8, wide),
        ],
        0,
    )
    hidden_grad1, g_qkv1, qv_sums1, bias_sums1 = run(
        kernel_shifted_backward,
        [
            (hidden1, field), (att1, field), (roll_ahead(low1), field), (probs1, probs_spec),
            (qkv1, None), (qkv_biases[1], None),
        ],
        [
            (jax.ShapeDtypeStruct(field_shape, BF), field),
            total(depth, 3 * depth), total(2, 8, depth), total(SLOT, HEADS * SLOT),
        ],
        8,
    )
    grad0, low0, g_proj0, g_fc10, g_fc20, sums0, fc1_sums0 = run(
        kernel_first_feed_backward,
        [
            (roll_behind(hidden_grad1), field), (stream1, flat(depth)), (grad1, flat(depth)),
            (middle0, flat(depth)), (act0, flat(wide)), (slope0, flat(wide)), (att0, flat(depth)),
            (proj0, None), (fc10, None), (fc20, None), (vecs[0], None),
        ],
        [
            (flat_type(depth, F32), flat(depth)), (flat_type(depth, BF), flat(depth)),
            total(depth, depth), total(depth, wide), total(depth, wide), total(6, 8, depth),
            total(8, wide),
        ],
        0,
    )
    tokens_grad, g_qkv0, qv_sums0, bias_sums0, sums00 = run(
        kernel_first_attention_backward,
        [
            (x, field), (grad0, flat(depth)), (low0, flat(depth)), (att0, flat(depth)),
            (probs0, probs_spec), (qkv0, None), (vecs[0], None), (qkv_biases[0], None),
        ],
        [
            (jax.ShapeDtypeStruct(field_shape, F32), field),
            total(depth, 3 * depth), total(2, 8, depth), total(SLOT, HEADS * SLOT),
            total(2, 8, depth),
        ],
        8,
    )

    owned = []
    for g_qkv, g_proj, g_fc1, g_fc2 in (
        (g_qkv0, g_proj0, g_fc10, g_fc20), (g_qkv1, g_proj1, g_fc11, g_fc21)
    ):
        packed = jnp.concatenate(
            [g_qkv, g_proj, g_fc1, g_fc2.reshape(depth, parts, -1).transpose(1, 2, 0).reshape(parts, wide // parts, depth).reshape(parts, 4, -1, depth).transpose(0, 2, 1, 3).reshape(depth, wide)], 1
        ).astype(BF)
        mine = lax.psum_scatter(packed, "wt", scatter_dimension=0, tiled=True)
        mine = lax.psum(mine, "seq").astype(F32)
        a, b, c, d = jnp.split(mine, [3 * depth, 4 * depth, 4 * depth + wide], 1)
        owned.append((a, b, c, unpack_second(d, 1)))

    def one(sums):
        return jnp.sum(sums, -2)

    sums0, sums1, sums00 = one(sums0), one(sums1), one(sums00)
    bias_sums = jnp.stack([bias_sums0, bias_sums1]).reshape(2, SLOT, HEADS, SLOT)
    bias_sums = bias_sums[:, :POS, :, :POS].transpose(1, 3, 0, 2).reshape(POS * POS, 2 * HEADS)
    table_grads = jnp.dot(selector.T, bias_sums, precision=lax.Precision.HIGHEST)
    table_grads = table_grads.reshape(table_size, 2, HEADS).transpose(1, 0, 2)
    small = lax.psum(
        (
            jnp.stack([jnp.stack([sums00[0], sums0[1]]), jnp.stack([sums0[4], sums1[1]])]),
            jnp.stack([jnp.stack([sums00[1], sums0[2]]), jnp.stack([sums0[5], sums1[2]])]),
            jnp.stack([one(qv_sums0), one(qv_sums1)]),
            table_grads,
            jnp.stack([jnp.stack([sums0[3], sums0[0]]), jnp.stack([sums1[3], sums1[0]])]),
            jnp.stack([one(fc1_sums0), one(fc1_sums1)]),
        ),
        ("seq", "wt"),
    )

    def both(index):
        return jnp.stack([owned[0][index], owned[1][index]])

    return (
        mixed.transpose(2, 0, 1, 3),
        tokens_grad.transpose(2, 0, 1, 3),
        small[0],
        small[1],
        both(0),
        small[2],
        small[3],
        both(1),
        small[4],
        both(2),
        small[5],
        both(3),
    )


def solution(mesh):
    field = P(None, "seq", "wt", None)
    shared = P(None, "wt", None)
    return jax.shard_map(
        per_device,
        mesh=mesh,
        in_specs=(
            field, P(None, "seq", "wt"), P(), P(), P(), shared, P(), P(), shared, P(), shared, P(),
            shared, field,
        ),
        out_specs=(
            field, field, P(), P(), shared, P(), P(), shared, P(), shared, P(), shared,
        ),
        check_vma=False,
    )
```

```python
import math

import jax
import jax.numpy as jnp
from jax import lax
from jax.experimental import pallas as pl
from jax.experimental.pallas import tpu as pltpu
from jax.sharding import PartitionSpec as P

HEADS = 4
WIN = 7
SHIFT = 3
HEAD_DIM = 32
EPSILON = 1e-05
POS = WIN * WIN
SLOT = 64
LOG2E = math.log2(math.e)
SCALE = 1.0 / math.sqrt(HEAD_DIM)
OFF = -1e30
BF = jnp.bfloat16
F32 = jnp.float32
VMEM_LIMIT = 56 * 1024 * 1024


def mm(left, right):
    return lax.dot_general(left, right, (((1,), (0,)), ((), ())), preferred_element_type=F32)


def mm_nt(left, right):
    return lax.dot_general(left, right, (((1,), (1,)), ((), ())), preferred_element_type=F32)


def mm_tn(left, right):
    return lax.dot_general(left, right, (((0,), (0,)), ((), ())), preferred_element_type=F32)


def norm_parts(field):
    centred = field - jnp.mean(field, -1, keepdims=True)
    inverse = lax.rsqrt(jnp.mean(centred * centred, -1, keepdims=True) + EPSILON)
    return centred * inverse, inverse


def norm_backward(upstream, normed, inverse, gain):
    scaled = upstream * gain
    return inverse * (
        scaled
        - jnp.mean(scaled, -1, keepdims=True)
        - normed * jnp.mean(scaled * normed, -1, keepdims=True)
    )


def fold_rows(field):
    rows, cols = field.shape
    return jnp.sum(field.reshape(rows // 8, 8, cols), 0)


def tokens_of_block(block):
    return block.astype(F32).reshape(-1, block.shape[-1])


def tokens_of(ref):
    return tokens_of_block(ref[...])


def put_tokens(ref, field):
    block = field.reshape(ref.shape).astype(ref.dtype)
    ref[...] = block
    return block


def head_blocks(field):
    head = lax.broadcasted_iota(jnp.int32, field.shape, 1) >> 5
    return jnp.concatenate(
        [jnp.where(head == h, field, 0.0).astype(BF) for h in range(HEADS)], 0
    )


def gather_heads(stacked):
    head = lax.broadcasted_iota(jnp.int32, (SLOT, stacked.shape[1]), 1) >> 5
    total = stacked[:SLOT]
    for h in range(1, HEADS):
        total = jnp.where(head == h, stacked[h * SLOT : (h + 1) * SLOT], total)
    return total


def lane_segments():
    row = lax.broadcasted_iota(jnp.int32, (HEADS * SLOT, HEADS * SLOT), 0) >> 6
    col = lax.broadcasted_iota(jnp.int32, (HEADS * SLOT, HEADS * SLOT), 1) >> 6
    return jnp.where(row == col, 1.0, 0.0).astype(BF)


def head_lanes():
    row = lax.broadcasted_iota(jnp.int32, (HEADS * SLOT, HEADS * HEAD_DIM), 0) >> 6
    col = lax.broadcasted_iota(jnp.int32, (HEADS * SLOT, HEADS * HEAD_DIM), 1) >> 5
    return jnp.where(row == col, 1.0, 0.0).astype(BF)


def segment_max(scores):
    low = lax.broadcasted_iota(jnp.int32, (SLOT, 2 * SLOT), 1) < SLOT
    parts = []
    for start in (0, 2 * SLOT):
        pair = scores[:, start : start + 2 * SLOT]
        first = jnp.max(jnp.where(low, pair, OFF), 1, keepdims=True)
        second = jnp.max(jnp.where(low, OFF, pair), 1, keepdims=True)
        parts.append(jnp.where(low, first, second))
    return jnp.concatenate(parts, 1)


def zero_tails(first_step, count, *refs):
    @pl.when(first_step)
    def _():
        for ref in refs:
            ref[count:, :] = jnp.zeros((ref.shape[0] - count, ref.shape[1]), F32)


def first_of_grid():
    return pl.program_id(0) == 0


def window(ref, image, images):
    return ref[pl.ds(image, SLOT, stride=images), :]


def attention_forward(images, parts, bias, masks, probs_ref, out_ref):
    sc_q, sc_k, sc_v = parts
    segments = lane_segments()
    everything = range(images)
    scores = [
        mm_nt(window(sc_q, i, images).astype(BF), head_blocks(window(sc_k, i, images)))
        * (SCALE * LOG2E)
        + bias
        for i in everything
    ]
    if masks is not None:
        apart = [masks[0, 0, i].astype(F32) * (-100.0 * LOG2E) for i in everything]
        scores = [scores[i] + jnp.concatenate([apart[i], apart[i]], 1) for i in everything]
    powers = [jnp.exp2(s - segment_max(s)) for s in scores]
    sums = [mm(p.astype(BF), segments) for p in powers]
    probs = [(p / s).astype(BF) for p, s in zip(powers, sums)]
    for i in everything:
        probs_ref[0, 0, i] = probs[i]
        out_ref[pl.ds(i, SLOT, stride=images), :] = mm(
            probs[i], head_blocks(window(sc_v, i, images))
        )


def attention_backward(images, parts, sc_grad, sc_out, probs_ref, grads, bias_acc):
    sc_q, sc_k, sc_v = parts
    sc_dq, sc_dk, sc_dv = grads
    lanes = head_lanes()
    everything = range(images)
    upstream = [window(sc_grad, i, images) for i in everything]
    centred = [
        mm_nt(
            jnp.concatenate(
                [
                    upstream[i].astype(BF),
                    (-(upstream[i] * window(sc_out, i, images))).astype(BF),
                ],
                1,
            ),
            jnp.concatenate([head_blocks(window(sc_v, i, images)), lanes], 1),
        )
        for i in everything
    ]
    probs = [probs_ref[0, 0, i] for i in everything]
    score_grads = [(probs[i].astype(F32) * centred[i]).astype(BF) for i in everything]
    total = score_grads[0].astype(F32)
    for i in everything[1:]:
        total = total + score_grads[i].astype(F32)
    bias_acc[...] += total
    for i in everything:
        place = pl.ds(i, SLOT, stride=images)
        sc_dq[place, :] = mm(score_grads[i], head_blocks(window(sc_k, i, images))) * SCALE
        sc_dk[place, :] = (
            gather_heads(mm_tn(score_grads[i], window(sc_q, i, images).astype(BF))) * SCALE
        )
        sc_dv[place, :] = gather_heads(mm_tn(probs[i], upstream[i].astype(BF)))


def split_projection(hidden, w_qkv, qkv_bias, parts, count):
    projected = mm(hidden, w_qkv) + qkv_bias
    projected = projected.astype(BF).astype(F32)
    depth = hidden.shape[1]
    for n, ref in enumerate(parts):
        ref[:count, :] = projected[:, n * depth : (n + 1) * depth]


def gelu_parts(expanded):
    cumulative = 0.5 + 0.5 * lax.erf(expanded * (1.0 / math.sqrt(2.0)))
    density = jnp.exp(expanded * expanded * -0.5) * (1.0 / math.sqrt(2.0 * math.pi))
    return expanded * cumulative, cumulative + expanded * density


def kernel_first_layer(
    images, place, rims, x_ref, w_qkv, w_proj, w_fc1, w_fc2, vecs, qkv_bias, fc1_bias, bias,
    stream_out, hidden_out, middle_out, out_out, probs_out, act_out, slope_out,
    sc_q, sc_k, sc_v, sc_out,
):
    count = POS * images
    zero_tails(first_of_grid(), count, sc_q, sc_k, sc_v)
    stream = tokens_of(x_ref)
    normed, _ = norm_parts(stream)
    hidden = (normed * vecs[0:1] + vecs[1:2]).astype(BF)
    split_projection(hidden, w_qkv[...], qkv_bias[...], (sc_q, sc_k, sc_v), count)
    attention_forward(images, (sc_q, sc_k, sc_v), bias[...], None, probs_out, sc_out)
    attended = sc_out[:count, :].astype(BF)
    out_out[0, 0] = attended
    middle = stream + (mm(attended, w_proj[...]) + vecs[4:5])
    middle_out[0, 0] = middle
    normed, _ = norm_parts(middle)
    inner = (normed * vecs[2:3] + vecs[3:4]).astype(BF)
    activated, slope = gelu_parts(mm(inner, w_fc1[...]) + fc1_bias[...])
    activated = activated.astype(BF)
    act_out[0, 0] = activated
    slope_out[0, 0] = slope.astype(BF)
    stream = middle + mm(activated, w_fc2[...]) + vecs[5:6]
    stream_out[0, 0] = stream
    normed, _ = norm_parts(stream)
    block = put_tokens(hidden_out, normed * vecs[6:7] + vecs[7:8])
    if rims is not None:
        put_rims(block, rims, place, "first")


def kernel_shifted_forward(
    images, place, rims, hidden_ref, *refs
):
    halo, refs = (None, refs) if rims is None else (refs[:3], refs[3:])
    w_qkv, qkv_bias, bias, masks, out_out, probs_out, held, sc_q, sc_k, sc_v, sc_out = refs
    count = POS * images
    zero_tails(first_of_grid(), count, sc_q, sc_k, sc_v)
    hidden = ahead_window(hidden_ref, halo, held, place).astype(BF)
    split_projection(hidden, w_qkv[...], qkv_bias[...], (sc_q, sc_k, sc_v), count)
    attention_forward(images, (sc_q, sc_k, sc_v), bias[...], masks, probs_out, sc_out)
    block = put_tokens(out_out, sc_out[:count, :])
    if rims is not None:
        put_rims(block, rims, place, "last")


def feed_forward_backward(out_low, inner, activated, slope, w_fc1, w_fc2):
    expanded_low = (slope * mm_nt(out_low, w_fc2)).astype(BF)
    inner_grad = mm_nt(expanded_low, w_fc1)
    return expanded_low, inner_grad


def put_rims(block, rims, place, edge):
    rim_rows, rim_cols, corner = rims
    row, col, rows, cols = place
    start = 0 if edge == "first" else WIN - SHIFT
    keep = slice(start, start + SHIFT)
    row_rim = row == (0 if edge == "first" else rows - 1)
    col_rim = col == (0 if edge == "first" else cols - 1)

    @pl.when(row_rim)
    def _():
        rim_rows[:, pl.ds(col * WIN, WIN)] = block[keep]

    @pl.when(col_rim)
    def _():
        rim_cols[pl.ds(row * WIN, WIN)] = block[:, keep]

    @pl.when(row_rim & col_rim)
    def _():
        corner[...] = block[keep, keep]


def ahead_window(field, rims, held, place):
    row, col, rows, cols = place
    top, left = row * WIN + SHIFT, col * WIN + SHIFT
    if rims is None:
        return tokens_of_block(field[pl.ds(top, WIN), pl.ds(left, WIN)])
    rim_rows, rim_cols, corner = rims
    own = WIN - SHIFT
    low, far = row == rows - 1, col == cols - 1
    held[:own, :own] = field[pl.ds(top, own), pl.ds(left, own)]

    @pl.when(low)
    def _():
        held[own:, :own] = rim_rows[:, pl.ds(left, own)]

    @pl.when(jnp.logical_not(low))
    def _():
        held[own:, :own] = field[pl.ds(top + own, SHIFT), pl.ds(left, own)]

    @pl.when(far)
    def _():
        held[:own, own:] = rim_cols[pl.ds(top, own)]

    @pl.when(jnp.logical_not(far))
    def _():
        held[:own, own:] = field[pl.ds(top, own), pl.ds(left + own, SHIFT)]

    @pl.when(low & far)
    def _():
        held[own:, own:] = corner[...]

    @pl.when(low & jnp.logical_not(far))
    def _():
        held[own:, own:] = rim_rows[:, pl.ds(left + own, SHIFT)]

    @pl.when(jnp.logical_not(low) & far)
    def _():
        held[own:, own:] = rim_cols[pl.ds(top + own, SHIFT)]

    return tokens_of_block(held[...])


def behind_window(field, rims, held, place):
    row, col, _, _ = place
    top, left = row * WIN, col * WIN
    if rims is None:
        return tokens_of_block(field[pl.ds(top - SHIFT, WIN), pl.ds(left - SHIFT, WIN)])
    rim_rows, rim_cols, corner = rims
    own = WIN - SHIFT
    high, near = row == 0, col == 0
    held[SHIFT:, SHIFT:] = field[pl.ds(top, own), pl.ds(left, own)]

    @pl.when(high)
    def _():
        held[:SHIFT, SHIFT:] = rim_rows[:, pl.ds(left, own)]

    @pl.when(jnp.logical_not(high))
    def _():
        held[:SHIFT, SHIFT:] = field[pl.ds(top - SHIFT, SHIFT), pl.ds(left, own)]

    @pl.when(near)
    def _():
        held[SHIFT:, :SHIFT] = rim_cols[pl.ds(top, own)]

    @pl.when(jnp.logical_not(near))
    def _():
        held[SHIFT:, :SHIFT] = field[pl.ds(top, own), pl.ds(left - SHIFT, SHIFT)]

    @pl.when(high & near)
    def _():
        held[:SHIFT, :SHIFT] = corner[...]

    @pl.when(high & jnp.logical_not(near))
    def _():
        held[:SHIFT, :SHIFT] = rim_rows[:, pl.ds(left - SHIFT, SHIFT)]

    @pl.when(jnp.logical_not(high) & near)
    def _():
        held[:SHIFT, :SHIFT] = rim_cols[pl.ds(top - SHIFT, SHIFT)]

    @pl.when(jnp.logical_not(high) & jnp.logical_not(near))
    def _():
        held[:SHIFT, :SHIFT] = field[pl.ds(top - SHIFT, SHIFT), pl.ds(left - SHIFT, SHIFT)]

    return tokens_of_block(held[...])


def kernel_middle(images, place, rims, out_ref, *refs):
    halo, refs = (None, refs) if rims is None else (refs[:3], refs[3:])
    (
        stream_ref, cot_ref, w_proj, w_fc1, w_fc2, vecs, fc1_bias,
        mixed_out, grad_out, low_out, g_proj, g_fc1, g_fc2, sums, fc1_sums, held,
    ) = refs
    stream = stream_ref[0, 0]
    attended = behind_window(out_ref, halo, held, place).astype(BF)
    middle = stream + (mm(attended, w_proj[...]) + vecs[4:5])
    normed, inverse = norm_parts(middle)
    inner = (normed * vecs[2:3] + vecs[3:4]).astype(BF)
    activated, slope = gelu_parts(mm(inner, w_fc1[...]) + fc1_bias[...])
    activated = activated.astype(BF)
    put_tokens(mixed_out, middle + mm(activated, w_fc2[...]) + vecs[5:6])
    gradient = tokens_of(cot_ref)
    out_low = gradient.astype(BF)
    expanded_low, inner_grad = feed_forward_backward(
        out_low, inner, activated, slope, w_fc1[...], w_fc2[...]
    )
    g_fc2[...] += mm_tn(out_low, activated)
    g_fc1[...] += mm_tn(inner, expanded_low)
    fc1_sums[...] += fold_rows(expanded_low.astype(F32))
    norm_term = norm_backward(inner_grad, normed, inverse, vecs[2:3])
    updated = gradient + norm_term
    grad_out[0, 0] = updated
    branch_low = updated.astype(BF)
    g_proj[...] += mm_tn(attended, branch_low)
    block = put_tokens(low_out, mm_nt(branch_low, w_proj[...]))
    if rims is not None:
        put_rims(block, rims, place, "first")
    sums[0] += fold_rows(gradient)
    sums[1] += fold_rows(inner_grad * normed)
    sums[2] += fold_rows(inner_grad)
    sums[3] += fold_rows(branch_low.astype(F32))


def joined_gradients(count, grads, qv_sums):
    pieces = [ref[:count, :].astype(BF) for ref in grads]
    qv_sums[0] += fold_rows(pieces[0].astype(F32))
    qv_sums[1] += fold_rows(pieces[2].astype(F32))
    return jnp.concatenate(pieces, 1)


def kernel_shifted_backward(images, place, rims, hidden_ref, low_ref, *refs):
    halo, low_halo, refs = (
        (None, None, refs) if rims is None else (refs[:3], refs[3:6], refs[6:])
    )
    (
        out_ref, probs_ref, w_qkv, qkv_bias, hidden_grad_out, g_qkv, qv_sums, bias_acc,
        held, sc_q, sc_k, sc_v, sc_out, sc_grad, sc_dq, sc_dk, sc_dv,
    ) = refs
    count = POS * images
    zero_tails(first_of_grid(), count, sc_q, sc_k, sc_v, sc_out, sc_grad)
    hidden = ahead_window(hidden_ref, halo, held, place).astype(BF)
    split_projection(hidden, w_qkv[...], qkv_bias[...], (sc_q, sc_k, sc_v), count)
    sc_out[:count, :] = tokens_of(out_ref)
    sc_grad[:count, :] = ahead_window(low_ref, low_halo, held, place)
    grads = (sc_dq, sc_dk, sc_dv)
    attention_backward(images, (sc_q, sc_k, sc_v), sc_grad, sc_out, probs_ref, grads, bias_acc)
    joined = joined_gradients(count, grads, qv_sums)
    g_qkv[...] += mm_tn(hidden, joined)
    block = put_tokens(hidden_grad_out, mm_nt(joined, w_qkv[...]))
    if rims is not None:
        put_rims(block, rims, place, "last")


def kernel_first_feed_backward(
    images, place, rims, hidden_grad_ref, rim_rows, rim_cols, corner, stream_ref, grad_ref, middle_ref, act_ref, slope_ref, att_ref,
    w_proj, w_fc1, w_fc2, vecs,
    grad_out, low_out, g_proj, g_fc1, g_fc2, sums, fc1_sums, held,
):
    upstream = behind_window(hidden_grad_ref, (rim_rows, rim_cols, corner), held, place)
    normed, inverse = norm_parts(stream_ref[0, 0])
    gradient = grad_ref[0, 0] + norm_backward(upstream, normed, inverse, vecs[6:7])
    sums[4] += fold_rows(upstream * normed)
    sums[5] += fold_rows(upstream)
    out_low = gradient.astype(BF)
    normed, inverse = norm_parts(middle_ref[0, 0])
    inner = (normed * vecs[2:3] + vecs[3:4]).astype(BF)
    activated = act_ref[0, 0]
    expanded_low, inner_grad = feed_forward_backward(
        out_low, inner, activated, slope_ref[0, 0].astype(F32), w_fc1[...], w_fc2[...]
    )
    g_fc2[...] += mm_tn(out_low, activated)
    g_fc1[...] += mm_tn(inner, expanded_low)
    fc1_sums[...] += fold_rows(expanded_low.astype(F32))
    updated = gradient + norm_backward(inner_grad, normed, inverse, vecs[2:3])
    grad_out[0, 0] = updated
    branch_low = updated.astype(BF)
    g_proj[...] += mm_tn(att_ref[0, 0], branch_low)
    low_out[0, 0] = mm_nt(branch_low, w_proj[...]).astype(BF)
    sums[0] += fold_rows(out_low.astype(F32))
    sums[1] += fold_rows(inner_grad * normed)
    sums[2] += fold_rows(inner_grad)
    sums[3] += fold_rows(branch_low.astype(F32))


def kernel_first_attention_backward(
    images, place, rims, x_ref, grad_ref, low_ref, att_ref, probs_ref, w_qkv, vecs, qkv_bias,
    tokens_grad_out, g_qkv, qv_sums, bias_acc, sums,
    sc_q, sc_k, sc_v, sc_out, sc_grad, sc_dq, sc_dk, sc_dv,
):
    count = POS * images
    zero_tails(first_of_grid(), count, sc_q, sc_k, sc_v, sc_out, sc_grad)
    normed, inverse = norm_parts(tokens_of(x_ref))
    hidden = (normed * vecs[0:1] + vecs[1:2]).astype(BF)
    split_projection(hidden, w_qkv[...], qkv_bias[...], (sc_q, sc_k, sc_v), count)
    sc_out[:count, :] = att_ref[0, 0].astype(F32)
    sc_grad[:count, :] = low_ref[0, 0].astype(F32)
    grads = (sc_dq, sc_dk, sc_dv)
    attention_backward(images, (sc_q, sc_k, sc_v), sc_grad, sc_out, probs_ref, grads, bias_acc)
    joined = joined_gradients(count, grads, qv_sums)
    g_qkv[...] += mm_tn(hidden, joined)
    upstream = mm_nt(joined, w_qkv[...])
    put_tokens(tokens_grad_out, grad_ref[0, 0] + norm_backward(upstream, normed, inverse, vecs[0:1]))
    sums[0] += fold_rows(upstream * normed)
    sums[1] += fold_rows(upstream)


def shift_by(array, axis, by):
    count = lax.axis_size(axis)
    return lax.ppermute(array, axis, [(i, (i + by) % count) for i in range(count)])


def shift_both(array, by):
    rows, cols = lax.axis_size("seq"), lax.axis_size("wt")
    pairs = [
        (r * cols + c, ((r + by) % rows) * cols + (c + by) % cols)
        for r in range(rows)
        for c in range(cols)
    ]
    return lax.ppermute(array, ("seq", "wt"), pairs)


def send_rims(rims, by):
    rim_rows, rim_cols, corner = rims
    return (
        shift_by(rim_rows, "seq", by),
        shift_by(rim_cols, "wt", by),
        shift_both(corner, by),
    )


def window_order(part, rows, cols):
    if part == "all":
        return rows * cols, lambda i: (i // cols, i % cols)
    edge, rim = part
    if rim:
        base = 0 if edge == "first" else rows - 1
        side = 0 if edge == "first" else cols - 1
        skip = 1 if edge == "first" else 0
        return rows + cols - 1, lambda i: (
            jnp.where(i < cols, base, i - cols + skip),
            jnp.where(i < cols, i, side),
        )
    skip = 1 if edge == "first" else 0
    return (rows - 1) * (cols - 1), lambda i: (
        i // (cols - 1) + skip,
        i % (cols - 1) + skip,
    )


def axis_sizes():
    return lax.axis_size("seq"), lax.axis_size("wt")


def blocks_of(matrix):
    return [matrix[:, i : i + 128] for i in range(0, matrix.shape[1], 128)]


def pack_slices(w_qkv, w_proj, w_fc1, w_fc2):
    return jnp.concatenate([*blocks_of(w_qkv), w_proj, *blocks_of(w_fc1), w_fc2], 0)


def kernel_weights(parts, place_ref, *refs):
    pieces, (qkv, proj, fc1, fc2), (s_qkv, s_proj, s_fc1, s_fc2) = (
        refs[:parts], refs[parts : parts + 4], refs[parts + 4 :]
    )
    rows = s_qkv.shape[0] // parts
    for k in range(parts):
        owner = lax.rem(place_ref[0] + k, parts)
        piece = pieces[k][...].astype(F32)
        near = pl.ds(pl.multiple_of(owner * rows, rows), rows)
        at = 0
        for target in (s_qkv, s_proj, s_fc1):
            for i in range(0, target.shape[1], 128):
                target[near, i : i + 128] = piece[at : at + rows]
                at += rows
        far = s_fc2.shape[0] // parts
        s_fc2[pl.ds(pl.multiple_of(owner * far, far), far), :] = piece[at : at + far]
    for out, held in ((qkv, s_qkv), (proj, s_proj), (fc1, s_fc1), (fc2, s_fc2)):
        out[...] = held[...].astype(BF)


def whole_weights(place, packed, depth, wide):
    parts = lax.axis_size("wt")
    pieces = [packed] + [shift_by(packed, "wt", -k) for k in range(1, parts)]
    shapes = [(depth, 3 * depth), (depth, depth), (depth, wide), (wide, depth)]

    def body(*refs):
        kernel_weights(parts, *refs)

    full = pl.BlockSpec(memory_space=pltpu.VMEM)
    return pl.pallas_call(
        body,
        in_specs=[pl.BlockSpec(memory_space=pltpu.SMEM)] + [full] * parts,
        out_specs=[full] * 4,
        out_shape=[jax.ShapeDtypeStruct(shape, BF) for shape in shapes],
        scratch_shapes=[pltpu.VMEM(shape, F32) for shape in shapes],
    )(place, *pieces)


SMALL_ROWS = 8


def split_high(field):
    high = field.astype(BF)
    return high, (field - high.astype(F32)).astype(BF)


def small_rows(refs):
    (sums00, sums0, sums1, qv0, qv1, fc1_0, fc1_1, table) = refs

    def one(ref, k):
        return jnp.sum(ref[k], 0, keepdims=True)

    rows = [
        one(sums00, 0), one(sums0, 1), one(sums0, 4), one(sums1, 1),
        one(sums00, 1), one(sums0, 2), one(sums0, 5), one(sums1, 2),
        one(qv0, 0), one(qv0, 1), one(qv1, 0), one(qv1, 1),
        one(sums0, 3), one(sums0, 0), one(sums1, 3), one(sums1, 0),
    ]
    for ref in (fc1_0, fc1_1):
        line = jnp.sum(ref[...], 0, keepdims=True)
        rows += [line[:, i : i + 128] for i in range(0, line.shape[1], 128)]
    return rows + [table[:, i : i + 128] for i in range(0, table.shape[1], 128)]


def kernel_pack(seqs, parts, each, *refs):
    grads, smalls, out, held, lines = refs[:8], refs[8:16], refs[16], refs[17], refs[18]
    depth = grads[0].shape[0]
    rows = depth // parts
    lines[...] = jnp.zeros_like(lines)
    at = 0
    for row in small_rows(smalls):
        lines[at : at + row.shape[0], :] = row
        at += row.shape[0]
    per = -(-at // seqs)
    turned = [grads[3][...].T, grads[7][...].T]
    for w in range(parts):
        near = slice(w * rows, (w + 1) * rows)
        at = 0
        for layer in range(2):
            for grad in grads[4 * layer : 4 * layer + 3]:
                for i in range(0, grad.shape[1], 128):
                    held[at : at + rows, :] = grad[near, i : i + 128]
                    at += rows
            far = turned[layer].shape[0] // parts
            held[at : at + far, :] = turned[layer][w * far : (w + 1) * far]
            at += far
        for s in range(seqs):
            mine = held[s * each : s * each + out.shape[1] - 2 * SMALL_ROWS, :]
            high, low = split_high(lines[s * per : s * per + SMALL_ROWS, :])
            out[s * parts + w] = jnp.concatenate(
                [mine, high.astype(F32), low.astype(F32)], 0
            ).astype(BF)


def kernel_reduce(packet_ref, out_ref):
    total = packet_ref[0].astype(F32)
    for i in range(1, packet_ref.shape[0]):
        total = total + packet_ref[i].astype(F32)
    rows = total.shape[0] - 2 * SMALL_ROWS
    high, low = split_high(total[rows : rows + SMALL_ROWS] + total[rows + SMALL_ROWS :])
    out_ref[...] = jnp.concatenate(
        [total[:rows], high.astype(F32), low.astype(F32)], 0
    ).astype(BF)


def kernel_unpack(each, per, packets, *refs):
    (gains, shifts, qkv, qv, table, proj, outs, fc1, fc1_bias, fc2, held, lines) = refs
    seqs, size, _ = packets.shape
    for s in range(seqs):
        packet = packets[s].astype(F32)
        start = size - 2 * SMALL_ROWS
        held[s * each : (s + 1) * each, :] = packet[:each]
        both = packet[start : start + SMALL_ROWS] + packet[start + SMALL_ROWS :]
        lines[s * per : (s + 1) * per, :] = both[:per]
    at = 0
    for layer in range(2):
        for target in (qkv, proj, fc1):
            rows = target.shape[1]
            for i in range(0, target.shape[2], 128):
                target[layer, :, i : i + 128] = held[at : at + rows, :]
                at += rows
        far = fc2.shape[1]
        fc2[layer] = held[at : at + far, :]
        at += far
    at = 0
    for target in (gains, shifts, qv, outs):
        for layer in range(2):
            target[layer] = lines[at : at + 2, :]
            at += 2
    for layer in range(2):
        for i in range(0, fc1_bias.shape[1], 128):
            fc1_bias[layer : layer + 1, i : i + 128] = lines[at : at + 1, :]
            at += 1
    for i in range(0, table.shape[1], 128):
        table[:, i : i + 128] = lines[at : at + table.shape[0], :]
        at += table.shape[0]


def whole_kernel(body, inputs, outputs, scratch=()):
    full = pl.BlockSpec(memory_space=pltpu.VMEM)
    return pl.pallas_call(
        body,
        in_specs=[full] * len(inputs),
        out_specs=[full] * len(outputs),
        out_shape=[jax.ShapeDtypeStruct(*out) for out in outputs],
        scratch_shapes=[pltpu.VMEM(shape, F32) for shape in scratch],
        compiler_params=pltpu.CompilerParams(vmem_limit_bytes=VMEM_LIMIT),
    )(*inputs)


def sum_everywhere(grads, smalls, depth, wide):
    seqs, parts = axis_sizes()
    rows = depth // parts
    held = 2 * (4 * depth + 2 * wide) // parts
    each = held // seqs
    size = -(-each // 16) * 16 + 2 * SMALL_ROWS
    count = 16 + 2 * (wide // 128) + 2 * HEADS * (smalls[-1].shape[1] // 128)
    per = -(-count // seqs)
    tail = (seqs * per + SMALL_ROWS, 128)

    def pack(*refs):
        kernel_pack(seqs, parts, each, *refs)

    def unpack(*refs):
        kernel_unpack(each, per, *refs)

    (packets,) = whole_kernel(
        pack,
        [*grads, *smalls],
        [((seqs * parts, size, 128), BF)],
        [(held + 16, 128), tail],
    )
    packets = lax.all_to_all(packets, ("seq", "wt"), 0, 0, tiled=True)
    (mine,) = whole_kernel(kernel_reduce, [packets], [((size, 128), BF)])
    mine = lax.all_gather(mine, "seq", axis=0)
    return whole_kernel(
        unpack,
        [mine],
        [
            ((2, 2, depth), F32), ((2, 2, depth), F32), ((2, rows, 3 * depth), F32),
            ((2, 2, depth), F32), (smalls[-1].shape, F32), ((2, rows, depth), F32),
            ((2, 2, depth), F32), ((2, rows, wide), F32), ((2, wide), F32),
            ((2, wide // parts, depth), F32),
        ],
        [(held, 128), tail],
    )


def per_device(
    tokens, region, rel_index, norm_gain, norm_bias, w_qkv, qv_bias, pos_table, w_proj, out_bias,
    w_fc1, fc1_bias, w_fc2, cotangent,
):
    images, height, width, depth = tokens.shape
    wide = w_fc1.shape[-1]
    rows, cols = height // WIN, width // WIN
    count = POS * images
    table_size = pos_table.shape[1]

    place = lax.axis_index("wt").astype(jnp.int32)[None]
    slices = [pack_slices(w_qkv[l], w_proj[l], w_fc1[l], w_fc2[l]) for l in range(2)]
    first_weights = whole_weights(place, slices[0], depth, wide)
    x = tokens.transpose(1, 2, 0, 3)
    cot = cotangent.transpose(1, 2, 0, 3)
    selector = (
        rel_index.reshape(-1)[:, None] == jnp.arange(table_size, dtype=jnp.int32)[None, :]
    ).astype(F32)
    tables = jnp.dot(
        selector,
        pos_table.transpose(1, 0, 2).reshape(table_size, 2 * HEADS) * LOG2E,
        precision=lax.Precision.HIGHEST,
    ).reshape(POS, POS, 2, HEADS)
    padded = jnp.pad(
        jnp.pad(tables.transpose(2, 0, 3, 1), ((0, 0), (0, SLOT - POS), (0, 0), (0, 0))),
        ((0, 0), (0, 0), (0, 0), (0, SLOT - POS)),
        constant_values=OFF,
    )
    biases = padded.reshape(2, SLOT, HEADS * SLOT)
    ids = region.reshape(images, rows, WIN, cols, WIN).transpose(1, 3, 0, 2, 4)
    ids = ids.reshape(rows, cols, images, POS)
    apart = (ids[..., :, None] != ids[..., None, :]).astype(BF)
    apart = jnp.pad(apart, [(0, 0)] * 3 + [(0, SLOT - POS)] * 2)
    masks = jnp.concatenate([apart, apart], -1)

    first_weights, later, masks = lax.optimization_barrier((first_weights, slices[1], masks))
    weights = [first_weights, whole_weights(place, later, depth, wide)]

    zeros = jnp.zeros((depth,), F32)
    qkv_biases = [
        jnp.concatenate([qv_bias[l, 0], zeros, qv_bias[l, 1]])[None] for l in range(2)
    ]

    def vectors(layer):
        after = norm_gain[1, 0], norm_bias[1, 0]
        return jnp.stack(
            [
                norm_gain[layer, 0], norm_bias[layer, 0], norm_gain[layer, 1], norm_bias[layer, 1],
                out_bias[layer, 0], out_bias[layer, 1], *after,
            ]
        )

    vecs = [vectors(0), vectors(1)]

    field_shape = (height, width, images, depth)
    field = ((WIN, WIN, images, depth), lambda r, c: (r, c, 0, 0))
    probs_spec = ((1, 1, images, SLOT, HEADS * SLOT), lambda r, c: (r, c, 0, 0, 0))
    mask_spec = ((1, 1, images, SLOT, 2 * SLOT), lambda r, c: (r, c, 0, 0, 0))

    def flat(columns):
        return (1, 1, count, columns), lambda r, c: (r, c, 0, 0)

    def flat_type(columns, dtype):
        return jax.ShapeDtypeStruct((rows, cols, count, columns), dtype)

    probs_type = jax.ShapeDtypeStruct((rows, cols, images, SLOT, HEADS * SLOT), BF)
    rim_types = [
        jax.ShapeDtypeStruct((SHIFT, width, images, depth), BF),
        jax.ShapeDtypeStruct((height, SHIFT, images, depth), BF),
        jax.ShapeDtypeStruct((SHIFT, SHIFT, images, depth), BF),
    ]

    def run(kernel, part, inputs, outputs, slots, earlier=None, held=False):
        steps, order = window_order(part, rows, cols)

        def spec_of(spec, shape):
            if spec is None:
                return pl.BlockSpec(tuple(shape), lambda i: (0,) * len(shape))
            block, index = spec
            return pl.BlockSpec(block, lambda i: index(*order(i)))

        with_rims = part != "all" and part[1]
        n_in, n_out = len(inputs), len(outputs)
        ins = [a for a, _ in inputs]
        in_specs = [spec_of(spec, a.shape) for a, spec in inputs]
        aliases = {}
        if earlier is not None:
            for n, (array, (_, spec)) in enumerate(zip(earlier, outputs)):
                if spec is not None:
                    aliases[len(ins)] = n
                ins.append(array)
                in_specs.append(
                    spec_of(None, array.shape)
                    if spec is None
                    else pl.BlockSpec(memory_space=pl.ANY)
                )
        n_all = len(ins)
        types = [t for t, _ in outputs] + (rim_types if with_rims else [])
        out_specs = [spec_of(spec, t.shape) for t, spec in outputs]
        out_specs += [spec_of(None, t.shape) for t in rim_types] if with_rims else []

        def body(*refs):
            place = (*order(pl.program_id(0)), rows, cols)
            outs = refs[n_all : n_all + n_out]
            rims = refs[n_all + n_out : n_all + n_out + 3] if with_rims else None
            rest = refs[n_all + len(types) :]

            @pl.when(first_of_grid())
            def _():
                for n, (_, spec) in enumerate(outputs):
                    if spec is None:
                        if earlier is None:
                            outs[n][...] = jnp.zeros_like(outs[n])
                        else:
                            outs[n][...] = refs[n_in + n][...]

            kernel(images, place, rims, *refs[:n_in], *outs, *rest)

        scratch = [pltpu.VMEM((WIN, WIN, images, depth), BF)] if held else []
        scratch += [pltpu.VMEM((SLOT * images, depth), F32)] * slots
        results = pl.pallas_call(
            body,
            grid=(steps,),
            in_specs=in_specs,
            out_specs=out_specs,
            out_shape=types,
            scratch_shapes=scratch,
            input_output_aliases=aliases,
            compiler_params=pltpu.CompilerParams(vmem_limit_bytes=VMEM_LIMIT),
            cost_estimate=pl.CostEstimate(
                flops=steps * 10**9, bytes_accessed=10**7, transcendentals=0
            ),
        )(*ins)
        return results[:n_out], results[n_out:]

    def run_both(kernel, edge, inputs, halos, outputs, slots, by, held=False):
        lead = len(halos)
        rim_inputs = [(a, None) for halo in halos for a in halo]
        inputs_a = inputs[:lead] + rim_inputs + inputs[lead:]
        first, rims = run(kernel, (edge, True), inputs_a, outputs, slots, held=held)
        rims = send_rims(rims, by)
        return run(kernel, (edge, False), inputs, outputs, slots, first, held=held)[0], rims

    def total(*shape):
        return (jax.ShapeDtypeStruct(shape, F32), None)

    qkv0, proj0, fc10, fc20 = weights[0]
    qkv1, proj1, fc11, fc21 = weights[1]
    (stream1, hidden1, middle0, att0, probs0, act0, slope0), halo = run_both(
        kernel_first_layer,
        "first",
        [
            (x, field), (qkv0, None), (proj0, None), (fc10, None), (fc20, None), (vecs[0], None),
            (qkv_biases[0], None), (fc1_bias[0:1], None), (biases[0], None),
        ],
        [],
        [
            (flat_type(depth, F32), flat(depth)),
            (jax.ShapeDtypeStruct(field_shape, BF), field),
            (flat_type(depth, F32), flat(depth)),
            (flat_type(depth, BF), flat(depth)),
            (probs_type, probs_spec),
            (flat_type(wide, BF), flat(wide)),
            (flat_type(wide, BF), flat(wide)),
        ],
        4,
        -1,
    )
    (att1, probs1), out_halo = run_both(
        kernel_shifted_forward,
        "last",
        [
            (hidden1, None), (qkv1, None), (qkv_biases[1], None), (biases[1], None),
            (masks, mask_spec),
        ],
        [halo],
        [(jax.ShapeDtypeStruct(field_shape, BF), field), (probs_type, probs_spec)],
        4,
        1,
        held=True,
    )
    (mixed, grad1, low1, g_proj1, g_fc11, g_fc21, sums1, fc1_sums1), low_halo = run_both(
        kernel_middle,
        "first",
        [
            (att1, None), (stream1, flat(depth)), (cot, field), (proj1, None),
            (fc11, None), (fc21, None), (vecs[1], None), (fc1_bias[1:2], None),
        ],
        [out_halo],
        [
            (jax.ShapeDtypeStruct(field_shape, BF), field),
            (flat_type(depth, F32), flat(depth)),
            (jax.ShapeDtypeStruct(field_shape, BF), field),
            total(depth, depth), total(depth, wide), total(depth, wide), total(4, 8, depth),
            total(8, wide),
        ],
        0,
        -1,
        held=True,
    )
    (hidden_grad1, g_qkv1, qv_sums1, bias_sums1), grad_halo = run_both(
        kernel_shifted_backward,
        "last",
        [
            (hidden1, None), (low1, None), (att1, field), (probs1, probs_spec),
            (qkv1, None), (qkv_biases[1], None),
        ],
        [halo, low_halo],
        [
            (jax.ShapeDtypeStruct(field_shape, BF), field),
            total(depth, 3 * depth), total(2, 8, depth), total(SLOT, HEADS * SLOT),
        ],
        8,
        1,
        held=True,
    )
    (grad0, low0, g_proj0, g_fc10, g_fc20, sums0, fc1_sums0), _ = run(
        kernel_first_feed_backward,
        "all",
        [
            (hidden_grad1, None), *[(a, None) for a in grad_halo],
            (stream1, flat(depth)), (grad1, flat(depth)),
            (middle0, flat(depth)), (act0, flat(wide)), (slope0, flat(wide)), (att0, flat(depth)),
            (proj0, None), (fc10, None), (fc20, None), (vecs[0], None),
        ],
        [
            (flat_type(depth, F32), flat(depth)), (flat_type(depth, BF), flat(depth)),
            total(depth, depth), total(depth, wide), total(depth, wide), total(6, 8, depth),
            total(8, wide),
        ],
        0,
        held=True,
    )
    (tokens_grad, g_qkv0, qv_sums0, bias_sums0, sums00), _ = run(
        kernel_first_attention_backward,
        "all",
        [
            (x, field), (grad0, flat(depth)), (low0, flat(depth)), (att0, flat(depth)),
            (probs0, probs_spec), (qkv0, None), (vecs[0], None), (qkv_biases[0], None),
        ],
        [
            (jax.ShapeDtypeStruct(field_shape, F32), field),
            total(depth, 3 * depth), total(2, 8, depth), total(SLOT, HEADS * SLOT),
            total(2, 8, depth),
        ],
        8,
    )

    bias_sums = jnp.stack([bias_sums0, bias_sums1]).reshape(2, SLOT, HEADS, SLOT)
    bias_sums = bias_sums[:, :POS, :, :POS].transpose(0, 2, 1, 3).reshape(2 * HEADS, POS * POS)
    table = jnp.dot(bias_sums, selector, precision=lax.Precision.HIGHEST)
    table = jnp.pad(table, ((0, 0), (0, -table_size % 128)))
    gains, shifts, d_qkv, d_qv, d_table, d_proj, d_out, d_fc1, d_fc1_bias, d_fc2 = sum_everywhere(
        [g_qkv0, g_proj0, g_fc10, g_fc20, g_qkv1, g_proj1, g_fc11, g_fc21],
        [sums00, sums0, sums1, qv_sums0, qv_sums1, fc1_sums0, fc1_sums1, table],
        depth,
        wide,
    )
    d_table = d_table[:, :table_size].reshape(2, HEADS, table_size).transpose(0, 2, 1)
    return (
        mixed.transpose(2, 0, 1, 3), tokens_grad.transpose(2, 0, 1, 3), gains, shifts, d_qkv,
        d_qv, d_table, d_proj, d_out, d_fc1, d_fc1_bias, d_fc2,
    )


def solution(mesh):
    field = P(None, "seq", "wt", None)
    shared = P(None, "wt", None)
    return jax.shard_map(
        per_device,
        mesh=mesh,
        in_specs=(
            field, P(None, "seq", "wt"), P(), P(), P(), shared, P(), P(), shared, P(), shared, P(),
            shared, field,
        ),
        out_specs=(
            field, field, P(), P(), shared, P(), P(), shared, P(), shared, P(), shared,
        ),
        check_vma=False,
    )
```

```python
import math

import jax
import jax.numpy as jnp
from jax import lax
from jax.experimental import pallas as pl
from jax.experimental.pallas import tpu as pltpu
from jax.sharding import PartitionSpec as P

HEADS = 4
WIN = 7
SHIFT = 3
HEAD_DIM = 32
EPSILON = 1e-05
POS = WIN * WIN
SLOT = 64
LOG2E = math.log2(math.e)
SCALE = 1.0 / math.sqrt(HEAD_DIM)
OFF = -1e30
BF = jnp.bfloat16
F32 = jnp.float32
MIB = 1024 * 1024
VMEM_LIMIT = 56 * MIB
LIMITS = ((56, 56), (16, 16), (16, 16), (16, 16), 56)


def mm(left, right):
    return lax.dot_general(left, right, (((1,), (0,)), ((), ())), preferred_element_type=F32)


def mm_nt(left, right):
    return lax.dot_general(left, right, (((1,), (1,)), ((), ())), preferred_element_type=F32)


def mm_tn(left, right):
    return lax.dot_general(left, right, (((0,), (0,)), ((), ())), preferred_element_type=F32)


def norm_parts(field):
    centred = field - jnp.mean(field, -1, keepdims=True)
    inverse = lax.rsqrt(jnp.mean(centred * centred, -1, keepdims=True) + EPSILON)
    return centred * inverse, inverse


def norm_backward(upstream, normed, inverse, gain):
    scaled = upstream * gain
    return inverse * (
        scaled
        - jnp.mean(scaled, -1, keepdims=True)
        - normed * jnp.mean(scaled * normed, -1, keepdims=True)
    )


def fold_rows(field):
    rows, cols = field.shape
    return jnp.sum(field.reshape(rows // 8, 8, cols), 0)


def tokens_of_block(block):
    return block.astype(F32).reshape(-1, block.shape[-1])


def tokens_of(ref):
    return tokens_of_block(ref[...])


def put_tokens(ref, field):
    block = field.reshape(ref.shape).astype(ref.dtype)
    ref[...] = block
    return block


def head_blocks(field):
    head = lax.broadcasted_iota(jnp.int32, field.shape, 1) >> 5
    return jnp.concatenate(
        [jnp.where(head == h, field, 0.0).astype(BF) for h in range(HEADS)], 0
    )


def gather_heads(stacked):
    head = lax.broadcasted_iota(jnp.int32, (SLOT, stacked.shape[1]), 1) >> 5
    total = stacked[:SLOT]
    for h in range(1, HEADS):
        total = jnp.where(head == h, stacked[h * SLOT : (h + 1) * SLOT], total)
    return total


def head_lanes():
    row = lax.broadcasted_iota(jnp.int32, (HEADS * SLOT, HEADS * HEAD_DIM), 0) >> 6
    col = lax.broadcasted_iota(jnp.int32, (HEADS * SLOT, HEADS * HEAD_DIM), 1) >> 5
    return jnp.where(row == col, 1.0, 0.0).astype(BF)


def segment_max(every):
    low = lax.broadcasted_iota(jnp.int32, (SLOT, 2 * SLOT), 1) < SLOT
    pairs = [s[:, start : start + 2 * SLOT] for s in every for start in (0, 2 * SLOT)]
    first = [jnp.max(jnp.where(low, pair, OFF), 1, keepdims=True) for pair in pairs]
    second = [jnp.max(jnp.where(low, OFF, pair), 1, keepdims=True) for pair in pairs]
    highest = [jnp.where(low, a, b) for a, b in zip(first, second)]
    return [jnp.concatenate(highest[n : n + 2], 1) for n in range(0, len(highest), 2)]


def zero_tails(first_step, count, *refs):
    @pl.when(first_step)
    def _():
        for ref in refs:
            ref[count:, :] = jnp.zeros((ref.shape[0] - count, ref.shape[1]), F32)


def first_of_grid():
    return pl.program_id(0) == 0


def window(ref, image, images):
    return ref[pl.ds(image, SLOT, stride=images), :]


def attention_forward(images, parts, bias, masks, powers_ref, out_ref, share_ref):
    sc_q, sc_k, sc_v = parts
    lanes = head_lanes()
    everything = range(images)
    scores = [
        mm_nt(window(sc_q, i, images).astype(BF), head_blocks(window(sc_k, i, images)))
        * (SCALE * LOG2E)
        + bias
        for i in everything
    ]
    if masks is not None:
        apart = [masks[0, 0, i].astype(F32) * (-100.0 * LOG2E) for i in everything]
        scores = [scores[i] + jnp.concatenate([apart[i], apart[i]], 1) for i in everything]
    powers = [jnp.exp2(s - top) for s, top in zip(scores, segment_max(scores))]
    powers = [p.astype(BF) for p in powers]
    both = [
        mm(powers[i], jnp.concatenate([head_blocks(window(sc_v, i, images)), lanes], 1))
        for i in everything
    ]
    depth = lanes.shape[1]
    shares = [1.0 / one[:, depth:] for one in both]
    for i in everything:
        place = pl.ds(i, SLOT, stride=images)
        powers_ref[0, 0, i] = powers[i]
        out_ref[place, :] = both[i][:, :depth] * shares[i]
        share_ref[place, :] = shares[i]


def attention_backward(images, parts, sc_grad, sc_out, powers_ref, grads, bias_acc):
    sc_q, sc_k, sc_v = parts
    sc_dq, sc_dk, sc_dv = grads
    lanes = head_lanes()
    depth = lanes.shape[1]
    everything = range(images)
    upstream = [window(sc_grad, i, images).astype(BF) for i in everything]
    centred = [
        mm_nt(
            jnp.concatenate([upstream[i], window(sc_out, i, images).astype(BF)], 1),
            jnp.concatenate([head_blocks(window(sc_v, i, images)), lanes], 1),
        )
        for i in everything
    ]
    powers = [powers_ref[0, 0, i] for i in everything]
    score_grads = [(powers[i].astype(F32) * centred[i]).astype(BF) for i in everything]
    total = score_grads[0].astype(F32)
    for i in everything[1:]:
        total = total + score_grads[i].astype(F32)
    bias_acc[...] += total
    d_queries = [mm(score_grads[i], head_blocks(window(sc_k, i, images))) for i in everything]
    empty = jnp.zeros((SLOT, depth), BF)
    d_both = [
        mm_tn(
            jnp.concatenate([score_grads[i], powers[i]], 0),
            jnp.concatenate(
                [
                    jnp.concatenate([window(sc_q, i, images).astype(BF), empty], 1),
                    jnp.concatenate([empty, upstream[i]], 1),
                ],
                0,
            ),
        )
        for i in everything
    ]
    for i in everything:
        place = pl.ds(i, SLOT, stride=images)
        sc_dq[place, :] = d_queries[i] * SCALE
        sc_dk[place, :] = gather_heads(d_both[i][:, :depth]) * SCALE
        sc_dv[place, :] = gather_heads(d_both[i][:, depth:])


def put_upstream(count, sc_grad, sc_out, gradient, out, share):
    shared = gradient * share
    sc_grad[:count, :] = shared
    sc_out[:count, :] = -(shared * out)


def put_norm(refs, normed, inverse):
    normed_ref, inverse_ref = refs
    normed_ref[0, 0] = normed.astype(BF)
    inverse_ref[0, 0] = jnp.broadcast_to(inverse, normed.shape).astype(BF)


def get_norm(refs):
    normed_ref, inverse_ref = refs
    return normed_ref[0, 0].astype(F32), inverse_ref[0, 0].astype(F32)


def split_projection(hidden, w_qkv, qkv_bias, parts, count):
    projected = mm(hidden, w_qkv) + qkv_bias
    projected = projected.astype(BF).astype(F32)
    depth = hidden.shape[1]
    for n, ref in enumerate(parts):
        ref[:count, :] = projected[:, n * depth : (n + 1) * depth]


def gelu_parts(expanded):
    cumulative = 0.5 + 0.5 * lax.erf(expanded * (1.0 / math.sqrt(2.0)))
    density = jnp.exp(expanded * expanded * -0.5) * (1.0 / math.sqrt(2.0 * math.pi))
    return expanded * cumulative, cumulative + expanded * density


def kernel_first_layer(
    images, place, rims, x_ref, w_qkv, w_proj, w_fc1, w_fc2, vecs, qkv_bias, fc1_bias, bias,
    stream_out, hidden_out, out_out, share_out, powers_out, act_out, slope_out,
    n_one, r_one, n_two, r_two, n_next, r_next,
    sc_q, sc_k, sc_v, sc_out, sc_share,
):
    count = POS * images
    zero_tails(first_of_grid(), count, sc_q, sc_k, sc_v)
    stream = tokens_of(x_ref)
    normed, inverse = norm_parts(stream)
    put_norm((n_one, r_one), normed, inverse)
    hidden = (normed * vecs[0:1] + vecs[1:2]).astype(BF)
    split_projection(hidden, w_qkv[...], qkv_bias[...], (sc_q, sc_k, sc_v), count)
    attention_forward(images, (sc_q, sc_k, sc_v), bias[...], None, powers_out, sc_out, sc_share)
    attended = sc_out[:count, :].astype(BF)
    out_out[0, 0] = attended
    share_out[0, 0] = sc_share[:count, :]
    middle = stream + (mm(attended, w_proj[...]) + vecs[4:5])
    normed, inverse = norm_parts(middle)
    put_norm((n_two, r_two), normed, inverse)
    inner = (normed * vecs[2:3] + vecs[3:4]).astype(BF)
    activated, slope = gelu_parts(mm(inner, w_fc1[...]) + fc1_bias[...])
    activated = activated.astype(BF)
    act_out[0, 0] = activated
    slope_out[0, 0] = slope.astype(BF)
    stream = middle + mm(activated, w_fc2[...]) + vecs[5:6]
    stream_out[0, 0] = stream
    normed, inverse = norm_parts(stream)
    put_norm((n_next, r_next), normed, inverse)
    block = put_tokens(hidden_out, normed * vecs[6:7] + vecs[7:8])
    if rims is not None:
        put_rims(block, rims, place, "first")


def kernel_shifted_forward(
    images, place, rims, hidden_ref, *refs
):
    halo, refs = (None, refs) if rims is None else (refs[:3], refs[3:])
    (
        w_qkv, qkv_bias, bias, masks, out_out, share_out, powers_out,
        held, sc_q, sc_k, sc_v, sc_out, sc_share,
    ) = refs
    count = POS * images
    zero_tails(first_of_grid(), count, sc_q, sc_k, sc_v)
    hidden = ahead_window(hidden_ref, halo, held, place).astype(BF)
    split_projection(hidden, w_qkv[...], qkv_bias[...], (sc_q, sc_k, sc_v), count)
    attention_forward(images, (sc_q, sc_k, sc_v), bias[...], masks, powers_out, sc_out, sc_share)
    share_out[0, 0] = sc_share[:count, :]
    block = put_tokens(out_out, sc_out[:count, :])
    if rims is not None:
        put_rims(block, rims, place, "last")


def feed_forward_backward(out_low, inner, activated, slope, w_fc1, w_fc2):
    expanded_low = (slope * mm_nt(out_low, w_fc2)).astype(BF)
    inner_grad = mm_nt(expanded_low, w_fc1)
    return expanded_low, inner_grad


def put_rims(block, rims, place, edge):
    rim_rows, rim_cols, corner = rims
    row, col, rows, cols = place
    start = 0 if edge == "first" else WIN - SHIFT
    keep = slice(start, start + SHIFT)
    row_rim = row == (0 if edge == "first" else rows - 1)
    col_rim = col == (0 if edge == "first" else cols - 1)

    @pl.when(row_rim)
    def _():
        rim_rows[:, pl.ds(col * WIN, WIN)] = block[keep]

    @pl.when(col_rim)
    def _():
        rim_cols[pl.ds(row * WIN, WIN)] = block[:, keep]

    @pl.when(row_rim & col_rim)
    def _():
        corner[...] = block[keep, keep]


def ahead_window(field, rims, held, place):
    row, col, rows, cols = place
    top, left = row * WIN + SHIFT, col * WIN + SHIFT
    if rims is None:
        return tokens_of_block(field[pl.ds(top, WIN), pl.ds(left, WIN)])
    rim_rows, rim_cols, corner = rims
    own = WIN - SHIFT
    low, far = row == rows - 1, col == cols - 1
    held[:own, :own] = field[pl.ds(top, own), pl.ds(left, own)]

    @pl.when(low)
    def _():
        held[own:, :own] = rim_rows[:, pl.ds(left, own)]

    @pl.when(jnp.logical_not(low))
    def _():
        held[own:, :own] = field[pl.ds(top + own, SHIFT), pl.ds(left, own)]

    @pl.when(far)
    def _():
        held[:own, own:] = rim_cols[pl.ds(top, own)]

    @pl.when(jnp.logical_not(far))
    def _():
        held[:own, own:] = field[pl.ds(top, own), pl.ds(left + own, SHIFT)]

    @pl.when(low & far)
    def _():
        held[own:, own:] = corner[...]

    @pl.when(low & jnp.logical_not(far))
    def _():
        held[own:, own:] = rim_rows[:, pl.ds(left + own, SHIFT)]

    @pl.when(jnp.logical_not(low) & far)
    def _():
        held[own:, own:] = rim_cols[pl.ds(top + own, SHIFT)]

    return tokens_of_block(held[...])


def behind_window(field, rims, held, place):
    row, col, _, _ = place
    top, left = row * WIN, col * WIN
    if rims is None:
        return tokens_of_block(field[pl.ds(top - SHIFT, WIN), pl.ds(left - SHIFT, WIN)])
    rim_rows, rim_cols, corner = rims
    own = WIN - SHIFT
    high, near = row == 0, col == 0
    held[SHIFT:, SHIFT:] = field[pl.ds(top, own), pl.ds(left, own)]

    @pl.when(high)
    def _():
        held[:SHIFT, SHIFT:] = rim_rows[:, pl.ds(left, own)]

    @pl.when(jnp.logical_not(high))
    def _():
        held[:SHIFT, SHIFT:] = field[pl.ds(top - SHIFT, SHIFT), pl.ds(left, own)]

    @pl.when(near)
    def _():
        held[SHIFT:, :SHIFT] = rim_cols[pl.ds(top, own)]

    @pl.when(jnp.logical_not(near))
    def _():
        held[SHIFT:, :SHIFT] = field[pl.ds(top, own), pl.ds(left - SHIFT, SHIFT)]

    @pl.when(high & near)
    def _():
        held[:SHIFT, :SHIFT] = corner[...]

    @pl.when(high & jnp.logical_not(near))
    def _():
        held[:SHIFT, :SHIFT] = rim_rows[:, pl.ds(left - SHIFT, SHIFT)]

    @pl.when(jnp.logical_not(high) & near)
    def _():
        held[:SHIFT, :SHIFT] = rim_cols[pl.ds(top - SHIFT, SHIFT)]

    @pl.when(jnp.logical_not(high) & jnp.logical_not(near))
    def _():
        held[:SHIFT, :SHIFT] = field[pl.ds(top - SHIFT, SHIFT), pl.ds(left - SHIFT, SHIFT)]

    return tokens_of_block(held[...])


def kernel_middle(images, place, rims, out_ref, *refs):
    halo, refs = (None, refs) if rims is None else (refs[:3], refs[3:])
    (
        stream_ref, cot_ref, w_proj, w_fc1, w_fc2, vecs, fc1_bias,
        mixed_out, grad_out, low_out, g_proj, g_fc1, g_fc2, sums, fc1_sums, held,
    ) = refs
    stream = stream_ref[0, 0]
    attended = behind_window(out_ref, halo, held, place).astype(BF)
    middle = stream + (mm(attended, w_proj[...]) + vecs[4:5])
    normed, inverse = norm_parts(middle)
    inner = (normed * vecs[2:3] + vecs[3:4]).astype(BF)
    activated, slope = gelu_parts(mm(inner, w_fc1[...]) + fc1_bias[...])
    activated = activated.astype(BF)
    put_tokens(mixed_out, middle + mm(activated, w_fc2[...]) + vecs[5:6])
    gradient = tokens_of(cot_ref)
    out_low = gradient.astype(BF)
    expanded_low, inner_grad = feed_forward_backward(
        out_low, inner, activated, slope, w_fc1[...], w_fc2[...]
    )
    g_fc2[...] += mm_tn(out_low, activated)
    g_fc1[...] += mm_tn(inner, expanded_low)
    fc1_sums[...] += fold_rows(expanded_low.astype(F32))
    norm_term = norm_backward(inner_grad, normed, inverse, vecs[2:3])
    updated = gradient + norm_term
    grad_out[0, 0] = updated
    branch_low = updated.astype(BF)
    g_proj[...] += mm_tn(attended, branch_low)
    block = put_tokens(low_out, mm_nt(branch_low, w_proj[...]))
    if rims is not None:
        put_rims(block, rims, place, "first")
    sums[0] += fold_rows(gradient)
    sums[1] += fold_rows(inner_grad * normed)
    sums[2] += fold_rows(inner_grad)
    sums[3] += fold_rows(branch_low.astype(F32))


def joined_gradients(count, grads, qv_sums):
    pieces = [ref[:count, :].astype(BF) for ref in grads]
    qv_sums[0] += fold_rows(pieces[0].astype(F32))
    qv_sums[1] += fold_rows(pieces[2].astype(F32))
    return jnp.concatenate(pieces, 1)


def kernel_shifted_backward(images, place, rims, hidden_ref, low_ref, *refs):
    halo, low_halo, refs = (
        (None, None, refs) if rims is None else (refs[:3], refs[3:6], refs[6:])
    )
    (
        out_ref, share_ref, powers_ref, w_qkv, qkv_bias, hidden_grad_out, g_qkv, qv_sums, bias_acc,
        held, sc_q, sc_k, sc_v, sc_out, sc_grad, sc_dq, sc_dk, sc_dv,
    ) = refs
    count = POS * images
    zero_tails(first_of_grid(), count, sc_q, sc_k, sc_v, sc_out, sc_grad)
    hidden = ahead_window(hidden_ref, halo, held, place).astype(BF)
    split_projection(hidden, w_qkv[...], qkv_bias[...], (sc_q, sc_k, sc_v), count)
    gradient = ahead_window(low_ref, low_halo, held, place)
    put_upstream(count, sc_grad, sc_out, gradient, tokens_of(out_ref), share_ref[0, 0])
    grads = (sc_dq, sc_dk, sc_dv)
    attention_backward(images, (sc_q, sc_k, sc_v), sc_grad, sc_out, powers_ref, grads, bias_acc)
    joined = joined_gradients(count, grads, qv_sums)
    g_qkv[...] += mm_tn(hidden, joined)
    block = put_tokens(hidden_grad_out, mm_nt(joined, w_qkv[...]))
    if rims is not None:
        put_rims(block, rims, place, "last")


def kernel_first_backward(
    images, place, rims, hidden_grad_ref, rim_rows, rim_cols, corner, grad_ref,
    n_one, r_one, n_two, r_two, n_next, r_next, act_ref, slope_ref, att_ref, share_ref, powers_ref,
    w_qkv, w_proj, w_fc1, w_fc2, vecs, qkv_bias,
    tokens_grad_out, g_qkv, g_proj, g_fc1, g_fc2, sums, fc1_sums, qv_sums, bias_acc,
    held, sc_q, sc_k, sc_v, sc_out, sc_grad, sc_dq, sc_dk, sc_dv,
):
    count = POS * images
    zero_tails(first_of_grid(), count, sc_q, sc_k, sc_v, sc_out, sc_grad)
    upstream = behind_window(hidden_grad_ref, (rim_rows, rim_cols, corner), held, place)
    normed_one, inverse_one = get_norm((n_one, r_one))
    hidden = (normed_one * vecs[0:1] + vecs[1:2]).astype(BF)
    split_projection(hidden, w_qkv[...], qkv_bias[...], (sc_q, sc_k, sc_v), count)
    normed, inverse = get_norm((n_next, r_next))
    gradient = grad_ref[0, 0] + norm_backward(upstream, normed, inverse, vecs[6:7])
    sums[4] += fold_rows(upstream * normed)
    sums[5] += fold_rows(upstream)
    out_low = gradient.astype(BF)
    normed, inverse = get_norm((n_two, r_two))
    inner = (normed * vecs[2:3] + vecs[3:4]).astype(BF)
    activated = act_ref[0, 0]
    expanded_low, inner_grad = feed_forward_backward(
        out_low, inner, activated, slope_ref[0, 0].astype(F32), w_fc1[...], w_fc2[...]
    )
    updated = gradient + norm_backward(inner_grad, normed, inverse, vecs[2:3])
    branch_low = updated.astype(BF)
    low = mm_nt(branch_low, w_proj[...]).astype(BF).astype(F32)
    attended = att_ref[0, 0]
    put_upstream(count, sc_grad, sc_out, low, attended.astype(F32), share_ref[0, 0])
    grads = (sc_dq, sc_dk, sc_dv)
    attention_backward(images, (sc_q, sc_k, sc_v), sc_grad, sc_out, powers_ref, grads, bias_acc)
    g_fc2[...] += mm_tn(out_low, activated)
    g_fc1[...] += mm_tn(inner, expanded_low)
    g_proj[...] += mm_tn(attended, branch_low)
    fc1_sums[...] += fold_rows(expanded_low.astype(F32))
    sums[0] += fold_rows(out_low.astype(F32))
    sums[1] += fold_rows(inner_grad * normed)
    sums[2] += fold_rows(inner_grad)
    sums[3] += fold_rows(branch_low.astype(F32))
    joined = joined_gradients(count, grads, qv_sums)
    g_qkv[...] += mm_tn(hidden, joined)
    upstream = mm_nt(joined, w_qkv[...])
    term = norm_backward(upstream, normed_one, inverse_one, vecs[0:1])
    put_tokens(tokens_grad_out, updated + term)
    sums[6] += fold_rows(upstream * normed_one)
    sums[7] += fold_rows(upstream)


def shift_by(array, axis, by):
    count = lax.axis_size(axis)
    return lax.ppermute(array, axis, [(i, (i + by) % count) for i in range(count)])


def shift_both(array, by):
    rows, cols = lax.axis_size("seq"), lax.axis_size("wt")
    pairs = [
        (r * cols + c, ((r + by) % rows) * cols + (c + by) % cols)
        for r in range(rows)
        for c in range(cols)
    ]
    return lax.ppermute(array, ("seq", "wt"), pairs)


def send_rims(rims, by):
    rim_rows, rim_cols, corner = rims
    return (
        shift_by(rim_rows, "seq", by),
        shift_by(rim_cols, "wt", by),
        shift_both(corner, by),
    )


def window_order(part, rows, cols):
    if part == "all":
        return rows * cols, lambda i: (i // cols, i % cols)
    edge, rim = part
    if rim:
        base = 0 if edge == "first" else rows - 1
        side = 0 if edge == "first" else cols - 1
        skip = 1 if edge == "first" else 0
        return rows + cols - 1, lambda i: (
            jnp.where(i < cols, base, i - cols + skip),
            jnp.where(i < cols, i, side),
        )
    skip = 1 if edge == "first" else 0
    return (rows - 1) * (cols - 1), lambda i: (
        i // (cols - 1) + skip,
        i % (cols - 1) + skip,
    )


def axis_sizes():
    return lax.axis_size("seq"), lax.axis_size("wt")


def blocks_of(matrix):
    return [matrix[:, i : i + 128] for i in range(0, matrix.shape[1], 128)]


def pack_slices(w_qkv, w_proj, w_fc1, w_fc2):
    return jnp.concatenate([*blocks_of(w_qkv), w_proj, *blocks_of(w_fc1), w_fc2], 0)


def kernel_weights(parts, place_ref, *refs):
    pieces, (qkv, proj, fc1, fc2), (s_qkv, s_proj, s_fc1, s_fc2) = (
        refs[:parts], refs[parts : parts + 4], refs[parts + 4 :]
    )
    rows = s_qkv.shape[0] // parts
    for k in range(parts):
        owner = lax.rem(place_ref[0] + k, parts)
        piece = pieces[k][...].astype(F32)
        near = pl.ds(pl.multiple_of(owner * rows, rows), rows)
        at = 0
        for target in (s_qkv, s_proj, s_fc1):
            for i in range(0, target.shape[1], 128):
                target[near, i : i + 128] = piece[at : at + rows]
                at += rows
        far = s_fc2.shape[0] // parts
        s_fc2[pl.ds(pl.multiple_of(owner * far, far), far), :] = piece[at : at + far]
    for out, held in ((qkv, s_qkv), (proj, s_proj), (fc1, s_fc1), (fc2, s_fc2)):
        out[...] = held[...].astype(BF)


def whole_weights(place, packed, depth, wide):
    parts = lax.axis_size("wt")
    pieces = [packed] + [shift_by(packed, "wt", -k) for k in range(1, parts)]
    shapes = [(depth, 3 * depth), (depth, depth), (depth, wide), (wide, depth)]

    def body(*refs):
        kernel_weights(parts, *refs)

    full = pl.BlockSpec(memory_space=pltpu.VMEM)
    return pl.pallas_call(
        body,
        in_specs=[pl.BlockSpec(memory_space=pltpu.SMEM)] + [full] * parts,
        out_specs=[full] * 4,
        out_shape=[jax.ShapeDtypeStruct(shape, BF) for shape in shapes],
        scratch_shapes=[pltpu.VMEM(shape, F32) for shape in shapes],
    )(place, *pieces)


SMALL_ROWS = 8


def split_high(field):
    high = field.astype(BF)
    return high, (field - high.astype(F32)).astype(BF)


def small_rows(refs):
    (sums0, sums1, qv0, qv1, fc1_0, fc1_1, table) = refs

    def one(ref, k):
        return jnp.sum(ref[k], 0, keepdims=True)

    rows = [
        one(sums0, 6), one(sums0, 1), one(sums0, 4), one(sums1, 1),
        one(sums0, 7), one(sums0, 2), one(sums0, 5), one(sums1, 2),
        one(qv0, 0), one(qv0, 1), one(qv1, 0), one(qv1, 1),
        one(sums0, 3), one(sums0, 0), one(sums1, 3), one(sums1, 0),
    ]
    for ref in (fc1_0, fc1_1):
        line = jnp.sum(ref[...], 0, keepdims=True)
        rows += [line[:, i : i + 128] for i in range(0, line.shape[1], 128)]
    return rows + [table[:, i : i + 128] for i in range(0, table.shape[1], 128)]


def kernel_pack(seqs, parts, each, *refs):
    grads, smalls, out, held, lines = refs[:8], refs[8:15], refs[15], refs[16], refs[17]
    depth = grads[0].shape[0]
    rows = depth // parts
    lines[...] = jnp.zeros_like(lines)
    at = 0
    for row in small_rows(smalls):
        lines[at : at + row.shape[0], :] = row
        at += row.shape[0]
    per = -(-at // seqs)
    turned = [grads[3][...].T, grads[7][...].T]
    for w in range(parts):
        near = slice(w * rows, (w + 1) * rows)
        at = 0
        for layer in range(2):
            for grad in grads[4 * layer : 4 * layer + 3]:
                for i in range(0, grad.shape[1], 128):
                    held[at : at + rows, :] = grad[near, i : i + 128]
                    at += rows
            far = turned[layer].shape[0] // parts
            held[at : at + far, :] = turned[layer][w * far : (w + 1) * far]
            at += far
        for s in range(seqs):
            mine = held[s * each : s * each + out.shape[1] - 2 * SMALL_ROWS, :]
            high, low = split_high(lines[s * per : s * per + SMALL_ROWS, :])
            out[s * parts + w] = jnp.concatenate(
                [mine, high.astype(F32), low.astype(F32)], 0
            ).astype(BF)


def kernel_reduce(packet_ref, out_ref):
    total = packet_ref[0].astype(F32)
    for i in range(1, packet_ref.shape[0]):
        total = total + packet_ref[i].astype(F32)
    rows = total.shape[0] - 2 * SMALL_ROWS
    high, low = split_high(total[rows : rows + SMALL_ROWS] + total[rows + SMALL_ROWS :])
    out_ref[...] = jnp.concatenate(
        [total[:rows], high.astype(F32), low.astype(F32)], 0
    ).astype(BF)


def kernel_unpack(each, per, packets, *refs):
    (gains, shifts, qkv, qv, table, proj, outs, fc1, fc1_bias, fc2, held, lines) = refs
    seqs, size, _ = packets.shape
    for s in range(seqs):
        packet = packets[s].astype(F32)
        start = size - 2 * SMALL_ROWS
        held[s * each : (s + 1) * each, :] = packet[:each]
        both = packet[start : start + SMALL_ROWS] + packet[start + SMALL_ROWS :]
        lines[s * per : (s + 1) * per, :] = both[:per]
    at = 0
    for layer in range(2):
        for target in (qkv, proj, fc1):
            rows = target.shape[1]
            for i in range(0, target.shape[2], 128):
                target[layer, :, i : i + 128] = held[at : at + rows, :]
                at += rows
        far = fc2.shape[1]
        fc2[layer] = held[at : at + far, :]
        at += far
    at = 0
    for target in (gains, shifts, qv, outs):
        for layer in range(2):
            target[layer] = lines[at : at + 2, :]
            at += 2
    for layer in range(2):
        for i in range(0, fc1_bias.shape[1], 128):
            fc1_bias[layer : layer + 1, i : i + 128] = lines[at : at + 1, :]
            at += 1
    for i in range(0, table.shape[1], 128):
        table[:, i : i + 128] = lines[at : at + table.shape[0], :]
        at += table.shape[0]


def whole_kernel(body, inputs, outputs, scratch=()):
    full = pl.BlockSpec(memory_space=pltpu.VMEM)
    return pl.pallas_call(
        body,
        in_specs=[full] * len(inputs),
        out_specs=[full] * len(outputs),
        out_shape=[jax.ShapeDtypeStruct(*out) for out in outputs],
        scratch_shapes=[pltpu.VMEM(shape, F32) for shape in scratch],
        compiler_params=pltpu.CompilerParams(vmem_limit_bytes=VMEM_LIMIT),
    )(*inputs)


def sum_everywhere(grads, smalls, depth, wide):
    seqs, parts = axis_sizes()
    rows = depth // parts
    held = 2 * (4 * depth + 2 * wide) // parts
    each = held // seqs
    size = -(-each // 16) * 16 + 2 * SMALL_ROWS
    count = 16 + 2 * (wide // 128) + 2 * HEADS * (smalls[-1].shape[1] // 128)
    per = -(-count // seqs)
    tail = (seqs * per + SMALL_ROWS, 128)

    def pack(*refs):
        kernel_pack(seqs, parts, each, *refs)

    def unpack(*refs):
        kernel_unpack(each, per, *refs)

    (packets,) = whole_kernel(
        pack,
        [*grads, *smalls],
        [((seqs * parts, size, 128), BF)],
        [(held + 16, 128), tail],
    )
    packets = lax.all_to_all(packets, ("seq", "wt"), 0, 0, tiled=True)
    (mine,) = whole_kernel(kernel_reduce, [packets], [((size, 128), BF)])
    mine = lax.all_gather(mine, "seq", axis=0)
    return whole_kernel(
        unpack,
        [mine],
        [
            ((2, 2, depth), F32), ((2, 2, depth), F32), ((2, rows, 3 * depth), F32),
            ((2, 2, depth), F32), (smalls[-1].shape, F32), ((2, rows, depth), F32),
            ((2, 2, depth), F32), ((2, rows, wide), F32), ((2, wide), F32),
            ((2, wide // parts, depth), F32),
        ],
        [(held, 128), tail],
    )


def per_device(
    tokens, region, rel_index, norm_gain, norm_bias, w_qkv, qv_bias, pos_table, w_proj, out_bias,
    w_fc1, fc1_bias, w_fc2, cotangent,
):
    images, height, width, depth = tokens.shape
    wide = w_fc1.shape[-1]
    rows, cols = height // WIN, width // WIN
    count = POS * images
    table_size = pos_table.shape[1]

    place = lax.axis_index("wt").astype(jnp.int32)[None]
    slices = [pack_slices(w_qkv[l], w_proj[l], w_fc1[l], w_fc2[l]) for l in range(2)]
    first_weights = whole_weights(place, slices[0], depth, wide)
    x = tokens.transpose(1, 2, 0, 3)
    cot = cotangent.transpose(1, 2, 0, 3)
    selector = (
        rel_index.reshape(-1)[:, None] == jnp.arange(table_size, dtype=jnp.int32)[None, :]
    ).astype(F32)
    tables = jnp.dot(
        selector,
        pos_table.transpose(1, 0, 2).reshape(table_size, 2 * HEADS) * LOG2E,
        precision=lax.Precision.HIGHEST,
    ).reshape(POS, POS, 2, HEADS)
    padded = jnp.pad(
        jnp.pad(tables.transpose(2, 0, 3, 1), ((0, 0), (0, SLOT - POS), (0, 0), (0, 0))),
        ((0, 0), (0, 0), (0, 0), (0, SLOT - POS)),
        constant_values=OFF,
    )
    biases = padded.reshape(2, SLOT, HEADS * SLOT)
    ids = region.reshape(images, rows, WIN, cols, WIN).transpose(1, 3, 0, 2, 4)
    ids = ids.reshape(rows, cols, images, POS)
    apart = (ids[..., :, None] != ids[..., None, :]).astype(BF)
    apart = jnp.pad(apart, [(0, 0)] * 3 + [(0, SLOT - POS)] * 2)
    masks = jnp.concatenate([apart, apart], -1)

    first_weights, later, masks = lax.optimization_barrier((first_weights, slices[1], masks))
    weights = [first_weights, whole_weights(place, later, depth, wide)]

    zeros = jnp.zeros((depth,), F32)
    qkv_biases = [
        jnp.concatenate([qv_bias[l, 0], zeros, qv_bias[l, 1]])[None] for l in range(2)
    ]

    def vectors(layer):
        after = norm_gain[1, 0], norm_bias[1, 0]
        return jnp.stack(
            [
                norm_gain[layer, 0], norm_bias[layer, 0], norm_gain[layer, 1], norm_bias[layer, 1],
                out_bias[layer, 0], out_bias[layer, 1], *after,
            ]
        )

    vecs = [vectors(0), vectors(1)]

    field_shape = (height, width, images, depth)
    field = ((WIN, WIN, images, depth), lambda r, c: (r, c, 0, 0))
    probs_spec = ((1, 1, images, SLOT, HEADS * SLOT), lambda r, c: (r, c, 0, 0, 0))
    mask_spec = ((1, 1, images, SLOT, 2 * SLOT), lambda r, c: (r, c, 0, 0, 0))

    def flat(columns):
        return (1, 1, count, columns), lambda r, c: (r, c, 0, 0)

    def flat_type(columns, dtype):
        return jax.ShapeDtypeStruct((rows, cols, count, columns), dtype)

    probs_type = jax.ShapeDtypeStruct((rows, cols, images, SLOT, HEADS * SLOT), BF)
    rim_types = [
        jax.ShapeDtypeStruct((SHIFT, width, images, depth), BF),
        jax.ShapeDtypeStruct((height, SHIFT, images, depth), BF),
        jax.ShapeDtypeStruct((SHIFT, SHIFT, images, depth), BF),
    ]

    def run(kernel, part, inputs, outputs, slots, limit, earlier=None, held=False):
        steps, order = window_order(part, rows, cols)

        def spec_of(spec, shape):
            if spec is None:
                return pl.BlockSpec(tuple(shape), lambda i: (0,) * len(shape))
            block, index = spec
            return pl.BlockSpec(block, lambda i: index(*order(i)))

        with_rims = part != "all" and part[1]
        n_in, n_out = len(inputs), len(outputs)
        ins = [a for a, _ in inputs]
        in_specs = [spec_of(spec, a.shape) for a, spec in inputs]
        aliases = {}
        if earlier is not None:
            for n, (array, (_, spec)) in enumerate(zip(earlier, outputs)):
                if spec is not None:
                    aliases[len(ins)] = n
                ins.append(array)
                in_specs.append(
                    spec_of(None, array.shape)
                    if spec is None
                    else pl.BlockSpec(memory_space=pl.ANY)
                )
        n_all = len(ins)
        types = [t for t, _ in outputs] + (rim_types if with_rims else [])
        out_specs = [spec_of(spec, t.shape) for t, spec in outputs]
        out_specs += [spec_of(None, t.shape) for t in rim_types] if with_rims else []

        def body(*refs):
            place = (*order(pl.program_id(0)), rows, cols)
            outs = refs[n_all : n_all + n_out]
            rims = refs[n_all + n_out : n_all + n_out + 3] if with_rims else None
            rest = refs[n_all + len(types) :]

            @pl.when(first_of_grid())
            def _():
                for n, (_, spec) in enumerate(outputs):
                    if spec is None:
                        if earlier is None:
                            outs[n][...] = jnp.zeros_like(outs[n])
                        else:
                            outs[n][...] = refs[n_in + n][...]

            kernel(images, place, rims, *refs[:n_in], *outs, *rest)

        scratch = [pltpu.VMEM((WIN, WIN, images, depth), BF)] if held else []
        scratch += [pltpu.VMEM((SLOT * images, depth), F32)] * slots
        results = pl.pallas_call(
            body,
            grid=(steps,),
            in_specs=in_specs,
            out_specs=out_specs,
            out_shape=types,
            scratch_shapes=scratch,
            input_output_aliases=aliases,
            compiler_params=pltpu.CompilerParams(vmem_limit_bytes=limit * MIB),
            cost_estimate=pl.CostEstimate(
                flops=steps * 10**9, bytes_accessed=10**7, transcendentals=0
            ),
        )(*ins)
        return results[:n_out], results[n_out:]

    def run_both(kernel, edge, inputs, halos, outputs, slots, by, limits, held=False):
        lead = len(halos)
        rim_inputs = [(a, None) for halo in halos for a in halo]
        inputs_a = inputs[:lead] + rim_inputs + inputs[lead:]
        first, rims = run(
            kernel, (edge, True), inputs_a, outputs, slots, limits[0], held=held
        )
        rims = send_rims(rims, by)
        second, _ = run(
            kernel, (edge, False), inputs, outputs, slots, limits[1], first, held=held
        )
        return second, rims

    def total(*shape):
        return (jax.ShapeDtypeStruct(shape, F32), None)

    qkv0, proj0, fc10, fc20 = weights[0]
    qkv1, proj1, fc11, fc21 = weights[1]
    (stream1, hidden1, att0, share0, powers0, act0, slope0, *norms0), halo = run_both(
        kernel_first_layer,
        "first",
        [
            (x, field), (qkv0, None), (proj0, None), (fc10, None), (fc20, None), (vecs[0], None),
            (qkv_biases[0], None), (fc1_bias[0:1], None), (biases[0], None),
        ],
        [],
        [
            (flat_type(depth, F32), flat(depth)),
            (jax.ShapeDtypeStruct(field_shape, BF), field),
            (flat_type(depth, BF), flat(depth)),
            (flat_type(depth, F32), flat(depth)),
            (probs_type, probs_spec),
            (flat_type(wide, BF), flat(wide)),
            (flat_type(wide, BF), flat(wide)),
            *[(flat_type(depth, BF), flat(depth))] * 6,
        ],
        5,
        -1,
        LIMITS[0],
    )
    (att1, share1, powers1), out_halo = run_both(
        kernel_shifted_forward,
        "last",
        [
            (hidden1, None), (qkv1, None), (qkv_biases[1], None), (biases[1], None),
            (masks, mask_spec),
        ],
        [halo],
        [
            (jax.ShapeDtypeStruct(field_shape, BF), field),
            (flat_type(depth, F32), flat(depth)),
            (probs_type, probs_spec),
        ],
        5,
        1,
        LIMITS[1],
        held=True,
    )
    (mixed, grad1, low1, g_proj1, g_fc11, g_fc21, sums1, fc1_sums1), low_halo = run_both(
        kernel_middle,
        "first",
        [
            (att1, None), (stream1, flat(depth)), (cot, field), (proj1, None),
            (fc11, None), (fc21, None), (vecs[1], None), (fc1_bias[1:2], None),
        ],
        [out_halo],
        [
            (jax.ShapeDtypeStruct(field_shape, BF), field),
            (flat_type(depth, F32), flat(depth)),
            (jax.ShapeDtypeStruct(field_shape, BF), field),
            total(depth, depth), total(depth, wide), total(depth, wide), total(4, 8, depth),
            total(8, wide),
        ],
        0,
        -1,
        LIMITS[2],
        held=True,
    )
    (hidden_grad1, g_qkv1, qv_sums1, bias_sums1), grad_halo = run_both(
        kernel_shifted_backward,
        "last",
        [
            (hidden1, None), (low1, None), (att1, field), (share1, flat(depth)),
            (powers1, probs_spec),
            (qkv1, None), (qkv_biases[1], None),
        ],
        [halo, low_halo],
        [
            (jax.ShapeDtypeStruct(field_shape, BF), field),
            total(depth, 3 * depth), total(2, 8, depth), total(SLOT, HEADS * SLOT),
        ],
        8,
        1,
        LIMITS[3],
        held=True,
    )
    (
        tokens_grad, g_qkv0, g_proj0, g_fc10, g_fc20, sums0, fc1_sums0, qv_sums0, bias_sums0
    ), _ = run(
        kernel_first_backward,
        "all",
        [
            (hidden_grad1, None), *[(a, None) for a in grad_halo], (grad1, flat(depth)),
            *[(a, flat(depth)) for a in norms0], (act0, flat(wide)), (slope0, flat(wide)),
            (att0, flat(depth)), (share0, flat(depth)), (powers0, probs_spec),
            (qkv0, None), (proj0, None), (fc10, None), (fc20, None), (vecs[0], None),
            (qkv_biases[0], None),
        ],
        [
            (jax.ShapeDtypeStruct(field_shape, F32), field),
            total(depth, 3 * depth), total(depth, depth), total(depth, wide), total(depth, wide),
            total(8, 8, depth), total(8, wide), total(2, 8, depth), total(SLOT, HEADS * SLOT),
        ],
        8,
        LIMITS[4],
        held=True,
    )

    bias_sums = jnp.stack([bias_sums0, bias_sums1]).reshape(2, SLOT, HEADS, SLOT)
    bias_sums = bias_sums[:, :POS, :, :POS].transpose(0, 2, 1, 3).reshape(2 * HEADS, POS * POS)
    table = jnp.dot(bias_sums, selector, precision=lax.Precision.HIGHEST)
    table = jnp.pad(table, ((0, 0), (0, -table_size % 128)))
    gains, shifts, d_qkv, d_qv, d_table, d_proj, d_out, d_fc1, d_fc1_bias, d_fc2 = sum_everywhere(
        [g_qkv0, g_proj0, g_fc10, g_fc20, g_qkv1, g_proj1, g_fc11, g_fc21],
        [sums0, sums1, qv_sums0, qv_sums1, fc1_sums0, fc1_sums1, table],
        depth,
        wide,
    )
    d_table = d_table[:, :table_size].reshape(2, HEADS, table_size).transpose(0, 2, 1)
    return (
        mixed.transpose(2, 0, 1, 3), tokens_grad.transpose(2, 0, 1, 3), gains, shifts, d_qkv,
        d_qv, d_table, d_proj, d_out, d_fc1, d_fc1_bias, d_fc2,
    )


def solution(mesh):
    field = P(None, "seq", "wt", None)
    shared = P(None, "wt", None)
    return jax.shard_map(
        per_device,
        mesh=mesh,
        in_specs=(
            field, P(None, "seq", "wt"), P(), P(), P(), shared, P(), P(), shared, P(), shared, P(),
            shared, field,
        ),
        out_specs=(
            field, field, P(), P(), shared, P(), P(), shared, P(), shared, P(), shared,
        ),
        check_vma=False,
    )
```

```python
import math

import jax
import jax.numpy as jnp
from jax import lax
from jax.experimental import pallas as pl
from jax.experimental.pallas import tpu as pltpu
from jax.sharding import PartitionSpec as P

HEADS = 4
WIN = 7
SHIFT = 3
HEAD_DIM = 32
EPSILON = 1e-05
POS = WIN * WIN
SLOT = 64
ASKED = 56
LOG2E = math.log2(math.e)
SCALE = 1.0 / math.sqrt(HEAD_DIM)
OFF = -1e30
BF = jnp.bfloat16
F32 = jnp.float32
MIB = 1024 * 1024
VMEM_LIMIT = 56 * MIB
GROUP = 1
LIMITS = ((56, 56), (16, 16), (16, 16), (16, 16), 56)


def mm(left, right):
    return lax.dot_general(left, right, (((1,), (0,)), ((), ())), preferred_element_type=F32)


def mm_nt(left, right):
    return lax.dot_general(left, right, (((1,), (1,)), ((), ())), preferred_element_type=F32)


def mm_tn(left, right):
    return lax.dot_general(left, right, (((0,), (0,)), ((), ())), preferred_element_type=F32)


def norm_parts(field):
    centred = field - jnp.mean(field, -1, keepdims=True)
    inverse = lax.rsqrt(jnp.mean(centred * centred, -1, keepdims=True) + EPSILON)
    return centred * inverse, inverse


def norm_backward(upstream, normed, inverse, gain):
    scaled = upstream * gain
    return inverse * (
        scaled
        - jnp.mean(scaled, -1, keepdims=True)
        - normed * jnp.mean(scaled * normed, -1, keepdims=True)
    )


def fold_rows(field):
    rows, cols = field.shape
    return jnp.sum(field.reshape(rows // 8, 8, cols), 0)


def tokens_of_block(block):
    return block.astype(F32).reshape(-1, block.shape[-1])


def tokens_of(ref):
    return tokens_of_block(ref[...])


def put_tokens(ref, field):
    block = field.reshape(ref.shape).astype(ref.dtype)
    ref[...] = block
    return block


def head_blocks(field):
    head = lax.broadcasted_iota(jnp.int32, field.shape, 1) >> 5
    return jnp.concatenate(
        [jnp.where(head == h, field, 0.0).astype(BF) for h in range(HEADS)], 0
    )


def gather_heads(stacked):
    head = lax.broadcasted_iota(jnp.int32, (SLOT, stacked.shape[1]), 1) >> 5
    total = stacked[:SLOT]
    for h in range(1, HEADS):
        total = jnp.where(head == h, stacked[h * SLOT : (h + 1) * SLOT], total)
    return total


def head_lanes():
    row = lax.broadcasted_iota(jnp.int32, (HEADS * SLOT, HEADS * HEAD_DIM), 0) >> 6
    col = lax.broadcasted_iota(jnp.int32, (HEADS * SLOT, HEADS * HEAD_DIM), 1) >> 5
    return jnp.where(row == col, 1.0, 0.0).astype(BF)


def segment_max(every):
    low = lax.broadcasted_iota(jnp.int32, (ASKED, 2 * SLOT), 1) < SLOT
    pairs = [s[:, start : start + 2 * SLOT] for s in every for start in (0, 2 * SLOT)]
    first = [jnp.max(jnp.where(low, pair, OFF), 1, keepdims=True) for pair in pairs]
    second = [jnp.max(jnp.where(low, OFF, pair), 1, keepdims=True) for pair in pairs]
    highest = [jnp.where(low, a, b) for a, b in zip(first, second)]
    return [jnp.concatenate(highest[n : n + 2], 1) for n in range(0, len(highest), 2)]


def zero_tails(first_step, count, *refs):
    @pl.when(first_step)
    def _():
        for ref in refs:
            ref[count:, :] = jnp.zeros((ref.shape[0] - count, ref.shape[1]), F32)


def first_of_grid():
    return pl.program_id(0) == 0


def window(ref, image, images, rows=SLOT):
    return ref[pl.ds(image, rows, stride=images), :]


def attention_forward(images, parts, bias, masks, powers_ref, out_ref, share_ref):
    sc_q, sc_k, sc_v = parts
    lanes = head_lanes()
    everything = range(images)
    scores = [
        mm_nt(window(sc_q, i, images, ASKED).astype(BF), head_blocks(window(sc_k, i, images)))
        * (SCALE * LOG2E)
        + bias
        for i in everything
    ]
    if masks is not None:
        apart = [masks[0, 0, i].astype(F32) * (-100.0 * LOG2E) for i in everything]
        scores = [scores[i] + jnp.concatenate([apart[i], apart[i]], 1) for i in everything]
    powers = [jnp.exp2(s - top) for s, top in zip(scores, segment_max(scores))]
    powers = [p.astype(BF) for p in powers]
    both = [
        mm(powers[i], jnp.concatenate([head_blocks(window(sc_v, i, images)), lanes], 1))
        for i in everything
    ]
    depth = lanes.shape[1]
    shares = [1.0 / one[:, depth:] for one in both]
    for i in everything:
        place = pl.ds(i, ASKED, stride=images)
        powers_ref[0, 0, i] = powers[i]
        out_ref[place, :] = both[i][:, :depth] * shares[i]
        share_ref[place, :] = shares[i]


def attention_backward(images, parts, sc_grad, sc_out, powers_ref, grads, bias_acc):
    sc_q, sc_k, sc_v = parts
    sc_dq, sc_dk, sc_dv = grads
    lanes = head_lanes()
    depth = lanes.shape[1]
    everything = range(images)
    upstream = [window(sc_grad, i, images, ASKED) for i in everything]
    centred = [
        mm_nt(
            jnp.concatenate([upstream[i], window(sc_out, i, images, ASKED)], 1).astype(BF),
            jnp.concatenate([head_blocks(window(sc_v, i, images)), lanes], 1),
        )
        for i in everything
    ]
    powers = [powers_ref[0, 0, i].astype(F32) for i in everything]
    score_grads = [powers[i] * centred[i] for i in everything]
    low_grads = [one.astype(BF) for one in score_grads]
    total = low_grads[0].astype(F32)
    for i in everything[1:]:
        total = total + low_grads[i].astype(F32)
    bias_acc[...] += total
    d_queries = [mm(low_grads[i], head_blocks(window(sc_k, i, images))) for i in everything]
    empty = jnp.zeros((ASKED, depth), F32)
    d_both = [
        mm_tn(
            jnp.concatenate([score_grads[i], powers[i]], 0).astype(BF),
            jnp.concatenate(
                [
                    jnp.concatenate([window(sc_q, i, images, ASKED), empty], 1),
                    jnp.concatenate([empty, upstream[i]], 1),
                ],
                0,
            ).astype(BF),
        )
        for i in everything
    ]
    for i in everything:
        place = pl.ds(i, SLOT, stride=images)
        sc_dq[pl.ds(i, ASKED, stride=images), :] = d_queries[i] * SCALE
        sc_dk[place, :] = gather_heads(d_both[i][:, :depth]) * SCALE
        sc_dv[place, :] = gather_heads(d_both[i][:, depth:])


def put_upstream(count, sc_grad, sc_out, gradient, out, share):
    shared = gradient * share
    sc_grad[:count, :] = shared
    sc_out[:count, :] = -(shared * out)


def put_norm(refs, normed, inverse):
    normed_ref, inverse_ref = refs
    normed_ref[0, 0] = normed.astype(BF)
    inverse_ref[0, 0] = jnp.broadcast_to(inverse, normed.shape).astype(BF)


def get_norm(refs):
    normed_ref, inverse_ref = refs
    return normed_ref[0, 0].astype(F32), inverse_ref[0, 0].astype(F32)


def split_projection(hidden, w_qkv, qv_ref, layer, parts, count):
    query_bias, value_bias = qv_ref[layer, 0:1], qv_ref[layer, 1:2]
    projected = mm(hidden, w_qkv) + jnp.concatenate(
        [query_bias, jnp.zeros_like(query_bias), value_bias], 1
    )
    projected = projected.astype(BF).astype(F32)
    depth = hidden.shape[1]
    for n, ref in enumerate(parts):
        ref[:count, :] = projected[:, n * depth : (n + 1) * depth]


def gelu_parts(expanded):
    cumulative = 0.5 + 0.5 * lax.erf(expanded * (1.0 / math.sqrt(2.0)))
    density = jnp.exp(expanded * expanded * -0.5) * (1.0 / math.sqrt(2.0 * math.pi))
    return expanded * cumulative, cumulative + expanded * density


def kernel_first_layer(
    images, place, rims, x_ref, w_qkv, w_proj, w_fc1, w_fc2, gains, shifts, outs, qkv_bias, fc1_bias, bias,
    stream_out, hidden_out, out_out, share_out, powers_out, expanded_out,
    n_one, r_one, n_two, r_two, n_next, r_next,
    sc_q, sc_k, sc_v, sc_out, sc_share,
):
    count = POS * images
    zero_tails(first_of_grid(), count, sc_q, sc_k, sc_v)
    stream = tokens_of(x_ref)
    normed, inverse = norm_parts(stream)
    put_norm((n_one, r_one), normed, inverse)
    hidden = (normed * gains[0, 0:1] + shifts[0, 0:1]).astype(BF)
    split_projection(hidden, w_qkv[...], qkv_bias, 0, (sc_q, sc_k, sc_v), count)
    attention_forward(images, (sc_q, sc_k, sc_v), bias[...], None, powers_out, sc_out, sc_share)
    attended = sc_out[:count, :].astype(BF)
    out_out[0, 0] = attended
    share_out[0, 0] = sc_share[:count, :]
    middle = stream + (mm(attended, w_proj[...]) + outs[0, 0:1])
    normed, inverse = norm_parts(middle)
    put_norm((n_two, r_two), normed, inverse)
    inner = (normed * gains[0, 1:2] + shifts[0, 1:2]).astype(BF)
    expanded = mm(inner, w_fc1[...]) + fc1_bias[0:1]
    expanded_out[0, 0] = expanded.astype(BF)
    activated = gelu_parts(expanded)[0].astype(BF)
    stream = middle + mm(activated, w_fc2[...]) + outs[0, 1:2]
    stream_out[0, 0] = stream
    normed, inverse = norm_parts(stream)
    put_norm((n_next, r_next), normed, inverse)
    block = put_tokens(hidden_out, normed * gains[1, 0:1] + shifts[1, 0:1])
    if rims is not None:
        put_rims(block, rims, place, "first")


def kernel_shifted_forward(
    images, place, rims, hidden_ref, *refs
):
    halo, refs = (None, refs) if rims is None else (refs[:3], refs[3:])
    (
        w_qkv, qkv_bias, bias, masks, out_out, share_out, powers_out,
        held, sc_q, sc_k, sc_v, sc_out, sc_share,
    ) = refs
    count = POS * images
    zero_tails(first_of_grid(), count, sc_q, sc_k, sc_v)
    hidden = ahead_window(hidden_ref, halo, held, place).astype(BF)
    split_projection(hidden, w_qkv[...], qkv_bias, 1, (sc_q, sc_k, sc_v), count)
    attention_forward(images, (sc_q, sc_k, sc_v), bias[...], masks, powers_out, sc_out, sc_share)
    share_out[0, 0] = sc_share[:count, :]
    block = put_tokens(out_out, sc_out[:count, :])
    if rims is not None:
        put_rims(block, rims, place, "last")


def feed_forward_backward(out_low, inner, activated, slope, w_fc1, w_fc2):
    expanded_low = (slope * mm_nt(out_low, w_fc2)).astype(BF)
    inner_grad = mm_nt(expanded_low, w_fc1)
    return expanded_low, inner_grad


def put_rims(block, rims, place, edge):
    rim_rows, rim_cols, corner = rims
    row, col, rows, cols = place
    start = 0 if edge == "first" else WIN - SHIFT
    keep = slice(start, start + SHIFT)
    row_rim = row == (0 if edge == "first" else rows - 1)
    col_rim = col == (0 if edge == "first" else cols - 1)

    @pl.when(row_rim)
    def _():
        rim_rows[:, pl.ds(col * WIN, WIN)] = block[keep]

    @pl.when(col_rim)
    def _():
        rim_cols[pl.ds(row * WIN, WIN)] = block[:, keep]

    @pl.when(row_rim & col_rim)
    def _():
        corner[...] = block[keep, keep]


def ahead_window(field, rims, held, place):
    row, col, rows, cols = place
    top, left = row * WIN + SHIFT, col * WIN + SHIFT
    if rims is None:
        return tokens_of_block(field[pl.ds(top, WIN), pl.ds(left, WIN)])
    rim_rows, rim_cols, corner = rims
    own = WIN - SHIFT
    low, far = row == rows - 1, col == cols - 1
    held[:own, :own] = field[pl.ds(top, own), pl.ds(left, own)]

    @pl.when(low)
    def _():
        held[own:, :own] = rim_rows[:, pl.ds(left, own)]

    @pl.when(jnp.logical_not(low))
    def _():
        held[own:, :own] = field[pl.ds(top + own, SHIFT), pl.ds(left, own)]

    @pl.when(far)
    def _():
        held[:own, own:] = rim_cols[pl.ds(top, own)]

    @pl.when(jnp.logical_not(far))
    def _():
        held[:own, own:] = field[pl.ds(top, own), pl.ds(left + own, SHIFT)]

    @pl.when(low & far)
    def _():
        held[own:, own:] = corner[...]

    @pl.when(low & jnp.logical_not(far))
    def _():
        held[own:, own:] = rim_rows[:, pl.ds(left + own, SHIFT)]

    @pl.when(jnp.logical_not(low) & far)
    def _():
        held[own:, own:] = rim_cols[pl.ds(top + own, SHIFT)]

    return tokens_of_block(held[...])


def behind_window(field, rims, held, place):
    row, col, _, _ = place
    top, left = row * WIN, col * WIN
    if rims is None:
        return tokens_of_block(field[pl.ds(top - SHIFT, WIN), pl.ds(left - SHIFT, WIN)])
    rim_rows, rim_cols, corner = rims
    own = WIN - SHIFT
    high, near = row == 0, col == 0
    held[SHIFT:, SHIFT:] = field[pl.ds(top, own), pl.ds(left, own)]

    @pl.when(high)
    def _():
        held[:SHIFT, SHIFT:] = rim_rows[:, pl.ds(left, own)]

    @pl.when(jnp.logical_not(high))
    def _():
        held[:SHIFT, SHIFT:] = field[pl.ds(top - SHIFT, SHIFT), pl.ds(left, own)]

    @pl.when(near)
    def _():
        held[SHIFT:, :SHIFT] = rim_cols[pl.ds(top, own)]

    @pl.when(jnp.logical_not(near))
    def _():
        held[SHIFT:, :SHIFT] = field[pl.ds(top, own), pl.ds(left - SHIFT, SHIFT)]

    @pl.when(high & near)
    def _():
        held[:SHIFT, :SHIFT] = corner[...]

    @pl.when(high & jnp.logical_not(near))
    def _():
        held[:SHIFT, :SHIFT] = rim_rows[:, pl.ds(left - SHIFT, SHIFT)]

    @pl.when(jnp.logical_not(high) & near)
    def _():
        held[:SHIFT, :SHIFT] = rim_cols[pl.ds(top - SHIFT, SHIFT)]

    @pl.when(jnp.logical_not(high) & jnp.logical_not(near))
    def _():
        held[:SHIFT, :SHIFT] = field[pl.ds(top - SHIFT, SHIFT), pl.ds(left - SHIFT, SHIFT)]

    return tokens_of_block(held[...])


def kernel_middle(images, place, rims, out_ref, *refs):
    halo, refs = (None, refs) if rims is None else (refs[:3], refs[3:])
    (
        stream_ref, cot_ref, w_proj, w_fc1, w_fc2, gains, shifts, outs, fc1_bias,
        mixed_out, grad_out, low_out, g_proj, g_fc1, g_fc2, sums, fc1_sums, held,
    ) = refs
    stream = stream_ref[0, 0]
    attended = behind_window(out_ref, halo, held, place).astype(BF)
    middle = stream + (mm(attended, w_proj[...]) + outs[1, 0:1])
    normed, inverse = norm_parts(middle)
    inner = (normed * gains[1, 1:2] + shifts[1, 1:2]).astype(BF)
    activated, slope = gelu_parts(mm(inner, w_fc1[...]) + fc1_bias[1:2])
    activated = activated.astype(BF)
    put_tokens(mixed_out, middle + mm(activated, w_fc2[...]) + outs[1, 1:2])
    gradient = tokens_of(cot_ref)
    out_low = gradient.astype(BF)
    expanded_low, inner_grad = feed_forward_backward(
        out_low, inner, activated, slope, w_fc1[...], w_fc2[...]
    )
    g_fc2[...] += mm_tn(out_low, activated)
    g_fc1[...] += mm_tn(inner, expanded_low)
    fc1_sums[...] += fold_rows(expanded_low.astype(F32))
    norm_term = norm_backward(inner_grad, normed, inverse, gains[1, 1:2])
    updated = gradient + norm_term
    grad_out[0, 0] = updated
    branch_low = updated.astype(BF)
    g_proj[...] += mm_tn(attended, branch_low)
    block = put_tokens(low_out, mm_nt(branch_low, w_proj[...]))
    if rims is not None:
        put_rims(block, rims, place, "first")
    sums[0] += fold_rows(gradient)
    sums[1] += fold_rows(inner_grad * normed)
    sums[2] += fold_rows(inner_grad)
    sums[3] += fold_rows(branch_low.astype(F32))


def joined_gradients(count, grads, qv_sums):
    pieces = [ref[:count, :].astype(BF) for ref in grads]
    qv_sums[0] += fold_rows(pieces[0].astype(F32))
    qv_sums[1] += fold_rows(pieces[2].astype(F32))
    return jnp.concatenate(pieces, 1)


def kernel_shifted_backward(images, place, rims, hidden_ref, low_ref, *refs):
    halo, low_halo, refs = (
        (None, None, refs) if rims is None else (refs[:3], refs[3:6], refs[6:])
    )
    (
        out_ref, share_ref, powers_ref, w_qkv, qkv_bias, hidden_grad_out, g_qkv, qv_sums, bias_acc,
        held, sc_q, sc_k, sc_v, sc_out, sc_grad, sc_dq, sc_dk, sc_dv,
    ) = refs
    count = POS * images
    zero_tails(first_of_grid(), count, sc_q, sc_k, sc_v, sc_out, sc_grad)
    hidden = ahead_window(hidden_ref, halo, held, place).astype(BF)
    split_projection(hidden, w_qkv[...], qkv_bias, 1, (sc_q, sc_k, sc_v), count)
    gradient = ahead_window(low_ref, low_halo, held, place)
    put_upstream(count, sc_grad, sc_out, gradient, tokens_of(out_ref), share_ref[0, 0])
    grads = (sc_dq, sc_dk, sc_dv)
    attention_backward(images, (sc_q, sc_k, sc_v), sc_grad, sc_out, powers_ref, grads, bias_acc)
    joined = joined_gradients(count, grads, qv_sums)
    g_qkv[...] += mm_tn(hidden, joined)
    block = put_tokens(hidden_grad_out, mm_nt(joined, w_qkv[...]))
    if rims is not None:
        put_rims(block, rims, place, "last")


def kernel_first_backward(
    images, place, rims, hidden_grad_ref, rim_rows, rim_cols, corner, grad_ref,
    n_one, r_one, n_two, r_two, n_next, r_next, expanded_ref, att_ref, share_ref, powers_ref,
    w_qkv, w_proj, w_fc1, w_fc2, gains, shifts, qkv_bias,
    tokens_grad_out, g_qkv, g_proj, g_fc1, g_fc2, sums, fc1_sums, qv_sums, bias_acc,
    held, sc_q, sc_k, sc_v, sc_out, sc_grad, sc_dq, sc_dk, sc_dv,
):
    count = POS * images
    zero_tails(first_of_grid(), count, sc_q, sc_k, sc_v, sc_out, sc_grad)
    upstream = behind_window(hidden_grad_ref, (rim_rows, rim_cols, corner), held, place)
    normed_one, inverse_one = get_norm((n_one, r_one))
    hidden = (normed_one * gains[0, 0:1] + shifts[0, 0:1]).astype(BF)
    split_projection(hidden, w_qkv[...], qkv_bias, 0, (sc_q, sc_k, sc_v), count)
    normed, inverse = get_norm((n_next, r_next))
    gradient = grad_ref[0, 0] + norm_backward(upstream, normed, inverse, gains[1, 0:1])
    sums[4] += fold_rows(upstream * normed)
    sums[5] += fold_rows(upstream)
    out_low = gradient.astype(BF)
    normed, inverse = get_norm((n_two, r_two))
    inner = (normed * gains[0, 1:2] + shifts[0, 1:2]).astype(BF)
    activated, slope = gelu_parts(expanded_ref[0, 0].astype(F32))
    activated = activated.astype(BF)
    expanded_low, inner_grad = feed_forward_backward(
        out_low, inner, activated, slope, w_fc1[...], w_fc2[...]
    )
    updated = gradient + norm_backward(inner_grad, normed, inverse, gains[0, 1:2])
    branch_low = updated.astype(BF)
    low = mm_nt(branch_low, w_proj[...]).astype(BF).astype(F32)
    attended = att_ref[0, 0]
    put_upstream(count, sc_grad, sc_out, low, attended.astype(F32), share_ref[0, 0])
    grads = (sc_dq, sc_dk, sc_dv)
    attention_backward(images, (sc_q, sc_k, sc_v), sc_grad, sc_out, powers_ref, grads, bias_acc)
    g_fc2[...] += mm_tn(out_low, activated)
    g_fc1[...] += mm_tn(inner, expanded_low)
    g_proj[...] += mm_tn(attended, branch_low)
    fc1_sums[...] += fold_rows(expanded_low.astype(F32))
    sums[0] += fold_rows(out_low.astype(F32))
    sums[1] += fold_rows(inner_grad * normed)
    sums[2] += fold_rows(inner_grad)
    sums[3] += fold_rows(branch_low.astype(F32))
    joined = joined_gradients(count, grads, qv_sums)
    g_qkv[...] += mm_tn(hidden, joined)
    upstream = mm_nt(joined, w_qkv[...])
    term = norm_backward(upstream, normed_one, inverse_one, gains[0, 0:1])
    put_tokens(tokens_grad_out, updated + term)
    sums[6] += fold_rows(upstream * normed_one)
    sums[7] += fold_rows(upstream)


def shift_by(array, axis, by):
    count = lax.axis_size(axis)
    return lax.ppermute(array, axis, [(i, (i + by) % count) for i in range(count)])


def shift_both(array, by):
    rows, cols = lax.axis_size("seq"), lax.axis_size("wt")
    pairs = [
        (r * cols + c, ((r + by) % rows) * cols + (c + by) % cols)
        for r in range(rows)
        for c in range(cols)
    ]
    return lax.ppermute(array, ("seq", "wt"), pairs)


def send_rims(rims, by):
    rim_rows, rim_cols, corner = rims
    return (
        shift_by(rim_rows, "seq", by),
        shift_by(rim_cols, "wt", by),
        shift_both(corner, by),
    )


def window_order(part, rows, cols):
    if part == "all":
        return rows * cols, lambda i: (i // cols, i % cols)
    edge, rim = part
    if rim:
        base = 0 if edge == "first" else rows - 1
        side = 0 if edge == "first" else cols - 1
        skip = 1 if edge == "first" else 0
        return rows + cols - 1, lambda i: (
            jnp.where(i < cols, base, i - cols + skip),
            jnp.where(i < cols, i, side),
        )
    skip = 1 if edge == "first" else 0
    return (rows - 1) * (cols - 1), lambda i: (
        i // (cols - 1) + skip,
        i % (cols - 1) + skip,
    )


def axis_sizes():
    return lax.axis_size("seq"), lax.axis_size("wt")


def blocks_of(matrix):
    return [matrix[:, i : i + 128] for i in range(0, matrix.shape[1], 128)]


def pack_slices(w_qkv, w_proj, w_fc1, w_fc2):
    return jnp.concatenate([*blocks_of(w_qkv), w_proj, *blocks_of(w_fc1), w_fc2], 0)


def kernel_weights(parts, place_ref, *refs):
    pieces, (qkv, proj, fc1, fc2), (s_qkv, s_proj, s_fc1, s_fc2) = (
        refs[:parts], refs[parts : parts + 4], refs[parts + 4 :]
    )
    rows = s_qkv.shape[0] // parts
    for k in range(parts):
        owner = lax.rem(place_ref[0] + k, parts)
        piece = pieces[k][...].astype(F32)
        near = pl.ds(pl.multiple_of(owner * rows, rows), rows)
        at = 0
        for target in (s_qkv, s_proj, s_fc1):
            for i in range(0, target.shape[1], 128):
                target[near, i : i + 128] = piece[at : at + rows]
                at += rows
        far = s_fc2.shape[0] // parts
        s_fc2[pl.ds(pl.multiple_of(owner * far, far), far), :] = piece[at : at + far]
    for out, held in ((qkv, s_qkv), (proj, s_proj), (fc1, s_fc1), (fc2, s_fc2)):
        out[...] = held[...].astype(BF)


def whole_weights(place, packed, depth, wide):
    parts = lax.axis_size("wt")
    pieces = [packed] + [shift_by(packed, "wt", -k) for k in range(1, parts)]
    shapes = [(depth, 3 * depth), (depth, depth), (depth, wide), (wide, depth)]

    def body(*refs):
        kernel_weights(parts, *refs)

    full = pl.BlockSpec(memory_space=pltpu.VMEM)
    return pl.pallas_call(
        body,
        in_specs=[pl.BlockSpec(memory_space=pltpu.SMEM)] + [full] * parts,
        out_specs=[full] * 4,
        out_shape=[jax.ShapeDtypeStruct(shape, BF) for shape in shapes],
        scratch_shapes=[pltpu.VMEM(shape, F32) for shape in shapes],
    )(place, *pieces)


SMALL_ROWS = 8


def split_high(field):
    high = field.astype(BF)
    return high, (field - high.astype(F32)).astype(BF)


def small_rows(refs):
    (sums0, sums1, qv0, qv1, fc1_0, fc1_1, table) = refs

    def one(ref, k):
        return jnp.sum(ref[k], 0, keepdims=True)

    rows = [
        one(sums0, 6), one(sums0, 1), one(sums0, 4), one(sums1, 1),
        one(sums0, 7), one(sums0, 2), one(sums0, 5), one(sums1, 2),
        one(qv0, 0), one(qv0, 1), one(qv1, 0), one(qv1, 1),
        one(sums0, 3), one(sums0, 0), one(sums1, 3), one(sums1, 0),
    ]
    for ref in (fc1_0, fc1_1):
        line = jnp.sum(ref[...], 0, keepdims=True)
        rows += [line[:, i : i + 128] for i in range(0, line.shape[1], 128)]
    return rows + [table[:, i : i + 128] for i in range(0, table.shape[1], 128)]


def kernel_pack(seqs, parts, each, *refs):
    grads, smalls, out, held, lines = refs[:8], refs[8:15], refs[15], refs[16], refs[17]
    depth = grads[0].shape[0]
    rows = depth // parts
    lines[...] = jnp.zeros_like(lines)
    at = 0
    for row in small_rows(smalls):
        lines[at : at + row.shape[0], :] = row
        at += row.shape[0]
    per = -(-at // seqs)
    turned = [grads[3][...].T, grads[7][...].T]
    for w in range(parts):
        near = slice(w * rows, (w + 1) * rows)
        at = 0
        for layer in range(2):
            for grad in grads[4 * layer : 4 * layer + 3]:
                for i in range(0, grad.shape[1], 128):
                    held[at : at + rows, :] = grad[near, i : i + 128]
                    at += rows
            far = turned[layer].shape[0] // parts
            held[at : at + far, :] = turned[layer][w * far : (w + 1) * far]
            at += far
        for s in range(seqs):
            mine = held[s * each : s * each + out.shape[1] - 2 * SMALL_ROWS, :]
            high, low = split_high(lines[s * per : s * per + SMALL_ROWS, :])
            out[s * parts + w] = jnp.concatenate(
                [mine, high.astype(F32), low.astype(F32)], 0
            ).astype(BF)


def kernel_reduce(packet_ref, out_ref):
    total = packet_ref[0].astype(F32)
    for i in range(1, packet_ref.shape[0]):
        total = total + packet_ref[i].astype(F32)
    rows = total.shape[0] - 2 * SMALL_ROWS
    high, low = split_high(total[rows : rows + SMALL_ROWS] + total[rows + SMALL_ROWS :])
    out_ref[...] = jnp.concatenate(
        [total[:rows], high.astype(F32), low.astype(F32)], 0
    ).astype(BF)


def kernel_unpack(each, per, packets, *refs):
    (gains, shifts, qkv, qv, table, proj, outs, fc1, fc1_bias, fc2, held, lines) = refs
    seqs, size, _ = packets.shape
    for s in range(seqs):
        packet = packets[s].astype(F32)
        start = size - 2 * SMALL_ROWS
        held[s * each : (s + 1) * each, :] = packet[:each]
        both = packet[start : start + SMALL_ROWS] + packet[start + SMALL_ROWS :]
        lines[s * per : (s + 1) * per, :] = both[:per]
    at = 0
    for layer in range(2):
        for target in (qkv, proj, fc1):
            rows = target.shape[1]
            for i in range(0, target.shape[2], 128):
                target[layer, :, i : i + 128] = held[at : at + rows, :]
                at += rows
        far = fc2.shape[1]
        fc2[layer] = held[at : at + far, :]
        at += far
    at = 0
    for target in (gains, shifts, qv, outs):
        for layer in range(2):
            target[layer] = lines[at : at + 2, :]
            at += 2
    for layer in range(2):
        for i in range(0, fc1_bias.shape[1], 128):
            fc1_bias[layer : layer + 1, i : i + 128] = lines[at : at + 1, :]
            at += 1
    for i in range(0, table.shape[1], 128):
        table[:, i : i + 128] = lines[at : at + table.shape[0], :]
        at += table.shape[0]


def whole_kernel(body, inputs, outputs, scratch=()):
    full = pl.BlockSpec(memory_space=pltpu.VMEM)
    return pl.pallas_call(
        body,
        in_specs=[full] * len(inputs),
        out_specs=[full] * len(outputs),
        out_shape=[jax.ShapeDtypeStruct(*out) for out in outputs],
        scratch_shapes=[pltpu.VMEM(shape, F32) for shape in scratch],
        compiler_params=pltpu.CompilerParams(vmem_limit_bytes=VMEM_LIMIT),
    )(*inputs)


def sum_everywhere(grads, smalls, depth, wide):
    seqs, parts = axis_sizes()
    rows = depth // parts
    held = 2 * (4 * depth + 2 * wide) // parts
    each = held // seqs
    size = -(-each // 16) * 16 + 2 * SMALL_ROWS
    count = 16 + 2 * (wide // 128) + 2 * HEADS * (smalls[-1].shape[1] // 128)
    per = -(-count // seqs)
    tail = (seqs * per + SMALL_ROWS, 128)

    def pack(*refs):
        kernel_pack(seqs, parts, each, *refs)

    def unpack(*refs):
        kernel_unpack(each, per, *refs)

    (packets,) = whole_kernel(
        pack,
        [*grads, *smalls],
        [((seqs * parts, size, 128), BF)],
        [(held + 16, 128), tail],
    )
    packets = lax.all_to_all(packets, ("seq", "wt"), 0, 0, tiled=True)
    (mine,) = whole_kernel(kernel_reduce, [packets], [((size, 128), BF)])
    mine = lax.all_gather(mine, "seq", axis=0)
    return whole_kernel(
        unpack,
        [mine],
        [
            ((2, 2, depth), F32), ((2, 2, depth), F32), ((2, rows, 3 * depth), F32),
            ((2, 2, depth), F32), (smalls[-1].shape, F32), ((2, rows, depth), F32),
            ((2, 2, depth), F32), ((2, rows, wide), F32), ((2, wide), F32),
            ((2, wide // parts, depth), F32),
        ],
        [(held, 128), tail],
    )


def per_device(
    tokens, region, rel_index, norm_gain, norm_bias, w_qkv, qv_bias, pos_table, w_proj, out_bias,
    w_fc1, fc1_bias, w_fc2, cotangent,
):
    images, height, width, depth = tokens.shape
    wide = w_fc1.shape[-1]
    rows, cols = height // WIN, width // WIN
    count = POS * images
    table_size = pos_table.shape[1]

    place = lax.axis_index("wt").astype(jnp.int32)[None]
    slices = [pack_slices(w_qkv[l], w_proj[l], w_fc1[l], w_fc2[l]) for l in range(2)]
    first_weights = whole_weights(place, slices[0], depth, wide)
    x = tokens.transpose(1, 2, 0, 3)
    cot = cotangent.transpose(1, 2, 0, 3)
    selector = (
        rel_index.reshape(-1)[:, None] == jnp.arange(table_size, dtype=jnp.int32)[None, :]
    ).astype(F32)
    tables = jnp.dot(
        selector,
        pos_table.transpose(1, 0, 2).reshape(table_size, 2 * HEADS) * LOG2E,
        precision=lax.Precision.HIGHEST,
    ).reshape(POS, POS, 2, HEADS)
    padded = jnp.pad(
        jnp.pad(tables.transpose(2, 0, 3, 1), ((0, 0), (0, ASKED - POS), (0, 0), (0, 0))),
        ((0, 0), (0, 0), (0, 0), (0, SLOT - POS)),
        constant_values=OFF,
    )
    biases = padded.reshape(2, ASKED, HEADS * SLOT)
    ids = region.reshape(images, rows, WIN, cols, WIN).transpose(1, 3, 0, 2, 4)
    ids = ids.reshape(rows, cols, images, POS)
    apart = (ids[..., :, None] != ids[..., None, :]).astype(BF)
    apart = jnp.pad(apart, [(0, 0)] * 3 + [(0, ASKED - POS), (0, SLOT - POS)])
    masks = jnp.concatenate([apart, apart], -1)

    first_weights, later, masks = lax.optimization_barrier((first_weights, slices[1], masks))
    weights = [first_weights, whole_weights(place, later, depth, wide)]

    field_shape = (height, width, images, depth)
    field = ((WIN, WIN, images, depth), lambda r, c: (r, c, 0, 0))
    probs_spec = ((1, 1, images, ASKED, HEADS * SLOT), lambda r, c: (r, c, 0, 0, 0))
    mask_spec = ((1, 1, images, ASKED, 2 * SLOT), lambda r, c: (r, c, 0, 0, 0))

    def flat(columns):
        return (1, 1, count, columns), lambda r, c: (r, c, 0, 0)

    def flat_type(columns, dtype):
        return jax.ShapeDtypeStruct((rows, cols, count, columns), dtype)

    probs_type = jax.ShapeDtypeStruct((rows, cols, images, ASKED, HEADS * SLOT), BF)
    rim_types = [
        jax.ShapeDtypeStruct((SHIFT, width, images, depth), BF),
        jax.ShapeDtypeStruct((height, SHIFT, images, depth), BF),
        jax.ShapeDtypeStruct((SHIFT, SHIFT, images, depth), BF),
    ]

    def run(kernel, part, inputs, outputs, slots, limit, earlier=None, held=False, group=1):
        steps, order = window_order(part, rows, cols // group)

        def spec_of(spec, shape):
            if spec is None:
                return pl.BlockSpec(tuple(shape), lambda i: (0,) * len(shape))
            block, index = spec
            block = (block[0], block[1] * group, *block[2:])
            return pl.BlockSpec(block, lambda i: index(*order(i)))

        with_rims = part != "all" and part[1]
        n_in, n_out = len(inputs), len(outputs)
        ins = [a for a, _ in inputs]
        in_specs = [spec_of(spec, a.shape) for a, spec in inputs]
        aliases = {}
        if earlier is not None:
            for n, (array, (_, spec)) in enumerate(zip(earlier, outputs)):
                if spec is not None:
                    aliases[len(ins)] = n
                ins.append(array)
                in_specs.append(
                    spec_of(None, array.shape)
                    if spec is None
                    else pl.BlockSpec(memory_space=pl.ANY)
                )
        n_all = len(ins)
        types = [t for t, _ in outputs] + (rim_types if with_rims else [])
        out_specs = [spec_of(spec, t.shape) for t, spec in outputs]
        out_specs += [spec_of(None, t.shape) for t in rim_types] if with_rims else []

        def body(*refs):
            row, col = order(pl.program_id(0))
            outs = refs[n_all : n_all + n_out]
            rims = refs[n_all + n_out : n_all + n_out + 3] if with_rims else None
            rest = refs[n_all + len(types) :]

            @pl.when(first_of_grid())
            def _():
                for n, (_, spec) in enumerate(outputs):
                    if spec is None:
                        if earlier is None:
                            outs[n][...] = jnp.zeros_like(outs[n])
                        else:
                            outs[n][...] = refs[n_in + n][...]

            def view(ref, spec, k):
                if spec is None or group == 1:
                    return ref
                size = spec[0][1]
                return ref.at[:, pl.ds(k * size, size)]

            each = len(rest) // group
            for k in range(group):
                kernel(
                    images,
                    (row, col * group + k, rows, cols),
                    rims,
                    *[view(ref, spec, k) for ref, (_, spec) in zip(refs[:n_in], inputs)],
                    *[view(ref, spec, k) for ref, (_, spec) in zip(outs, outputs)],
                    *rest[k * each : (k + 1) * each],
                )

        scratch = [pltpu.VMEM((WIN, WIN, images, depth), BF)] if held else []
        scratch += [pltpu.VMEM((SLOT * images, depth), F32)] * slots
        results = pl.pallas_call(
            body,
            grid=(steps,),
            in_specs=in_specs,
            out_specs=out_specs,
            out_shape=types,
            scratch_shapes=scratch * group,
            input_output_aliases=aliases,
            compiler_params=pltpu.CompilerParams(vmem_limit_bytes=limit * MIB),
            cost_estimate=pl.CostEstimate(
                flops=steps * 10**9, bytes_accessed=10**7, transcendentals=0
            ),
        )(*ins)
        return results[:n_out], results[n_out:]

    def run_both(kernel, edge, inputs, halos, outputs, slots, by, limits, held=False):
        lead = len(halos)
        rim_inputs = [(a, None) for halo in halos for a in halo]
        inputs_a = inputs[:lead] + rim_inputs + inputs[lead:]
        first, rims = run(
            kernel, (edge, True), inputs_a, outputs, slots, limits[0], held=held
        )
        rims = send_rims(rims, by)
        second, _ = run(
            kernel, (edge, False), inputs, outputs, slots, limits[1], first, held=held
        )
        return second, rims

    def total(*shape):
        return (jax.ShapeDtypeStruct(shape, F32), None)

    qkv0, proj0, fc10, fc20 = weights[0]
    qkv1, proj1, fc11, fc21 = weights[1]
    (stream1, hidden1, att0, share0, powers0, expanded0, *norms0), halo = run_both(
        kernel_first_layer,
        "first",
        [
            (x, field), (qkv0, None), (proj0, None), (fc10, None), (fc20, None), (norm_gain, None),
            (norm_bias, None), (out_bias, None), (qv_bias, None), (fc1_bias, None),
            (biases[0], None),
        ],
        [],
        [
            (flat_type(depth, F32), flat(depth)),
            (jax.ShapeDtypeStruct(field_shape, BF), field),
            (flat_type(depth, BF), flat(depth)),
            (flat_type(depth, F32), flat(depth)),
            (probs_type, probs_spec),
            (flat_type(wide, BF), flat(wide)),
            *[(flat_type(depth, BF), flat(depth))] * 6,
        ],
        5,
        -1,
        LIMITS[0],
    )
    (att1, share1, powers1), out_halo = run_both(
        kernel_shifted_forward,
        "last",
        [
            (hidden1, None), (qkv1, None), (qv_bias, None), (biases[1], None),
            (masks, mask_spec),
        ],
        [halo],
        [
            (jax.ShapeDtypeStruct(field_shape, BF), field),
            (flat_type(depth, F32), flat(depth)),
            (probs_type, probs_spec),
        ],
        5,
        1,
        LIMITS[1],
        held=True,
    )
    (mixed, grad1, low1, g_proj1, g_fc11, g_fc21, sums1, fc1_sums1), low_halo = run_both(
        kernel_middle,
        "first",
        [
            (att1, None), (stream1, flat(depth)), (cot, field), (proj1, None),
            (fc11, None), (fc21, None), (norm_gain, None), (norm_bias, None),
            (out_bias, None), (fc1_bias, None),
        ],
        [out_halo],
        [
            (jax.ShapeDtypeStruct(field_shape, BF), field),
            (flat_type(depth, F32), flat(depth)),
            (jax.ShapeDtypeStruct(field_shape, BF), field),
            total(depth, depth), total(depth, wide), total(depth, wide), total(4, 8, depth),
            total(8, wide),
        ],
        0,
        -1,
        LIMITS[2],
        held=True,
    )
    (hidden_grad1, g_qkv1, qv_sums1, bias_sums1), grad_halo = run_both(
        kernel_shifted_backward,
        "last",
        [
            (hidden1, None), (low1, None), (att1, field), (share1, flat(depth)),
            (powers1, probs_spec),
            (qkv1, None), (qv_bias, None),
        ],
        [halo, low_halo],
        [
            (jax.ShapeDtypeStruct(field_shape, BF), field),
            total(depth, 3 * depth), total(2, 8, depth), total(ASKED, HEADS * SLOT),
        ],
        8,
        1,
        LIMITS[3],
        held=True,
    )
    (
        tokens_grad, g_qkv0, g_proj0, g_fc10, g_fc20, sums0, fc1_sums0, qv_sums0, bias_sums0
    ), _ = run(
        kernel_first_backward,
        "all",
        [
            (hidden_grad1, None), *[(a, None) for a in grad_halo], (grad1, flat(depth)),
            *[(a, flat(depth)) for a in norms0], (expanded0, flat(wide)),
            (att0, flat(depth)), (share0, flat(depth)), (powers0, probs_spec),
            (qkv0, None), (proj0, None), (fc10, None), (fc20, None), (norm_gain, None),
            (norm_bias, None), (qv_bias, None),
        ],
        [
            (jax.ShapeDtypeStruct(field_shape, F32), field),
            total(depth, 3 * depth), total(depth, depth), total(depth, wide), total(depth, wide),
            total(8, 8, depth), total(8, wide), total(2, 8, depth), total(ASKED, HEADS * SLOT),
        ],
        8,
        LIMITS[4],
        held=True,
        group=GROUP,
    )

    bias_sums = jnp.stack([bias_sums0, bias_sums1]).reshape(2, ASKED, HEADS, SLOT)
    bias_sums = bias_sums[:, :POS, :, :POS].transpose(0, 2, 1, 3).reshape(2 * HEADS, POS * POS)
    table = jnp.dot(bias_sums, selector, precision=lax.Precision.HIGHEST)
    table = jnp.pad(table, ((0, 0), (0, -table_size % 128)))
    gains, shifts, d_qkv, d_qv, d_table, d_proj, d_out, d_fc1, d_fc1_bias, d_fc2 = sum_everywhere(
        [g_qkv0, g_proj0, g_fc10, g_fc20, g_qkv1, g_proj1, g_fc11, g_fc21],
        [sums0, sums1, qv_sums0, qv_sums1, fc1_sums0, fc1_sums1, table],
        depth,
        wide,
    )
    d_table = d_table[:, :table_size].reshape(2, HEADS, table_size).transpose(0, 2, 1)
    return (
        mixed.transpose(2, 0, 1, 3), tokens_grad.transpose(2, 0, 1, 3), gains, shifts, d_qkv,
        d_qv, d_table, d_proj, d_out, d_fc1, d_fc1_bias, d_fc2,
    )


def solution(mesh):
    field = P(None, "seq", "wt", None)
    shared = P(None, "wt", None)
    return jax.shard_map(
        per_device,
        mesh=mesh,
        in_specs=(
            field, P(None, "seq", "wt"), P(), P(), P(), shared, P(), P(), shared, P(), shared, P(),
            shared, field,
        ),
        out_specs=(
            field, field, P(), P(), shared, P(), P(), shared, P(), shared, P(), shared,
        ),
        check_vma=False,
    )
```

```python
import math

import jax
import jax.numpy as jnp
from jax import lax
from jax.experimental import pallas as pl
from jax.experimental.pallas import tpu as pltpu
from jax.sharding import PartitionSpec as P

HEADS = 4
WIN = 7
SHIFT = 3
HEAD_DIM = 32
EPSILON = 1e-05
POS = WIN * WIN
SLOT = 64
ASKED = 56
LOG2E = math.log2(math.e)
SCALE = 1.0 / math.sqrt(HEAD_DIM)
OFF = -1e30
BF = jnp.bfloat16
F32 = jnp.float32
MIB = 1024 * 1024
VMEM_LIMIT = 56 * MIB
LIMITS = ((60, 60), (16, 16), (16, 16), (16, 16), 60)


def mm(left, right):
    return lax.dot_general(left, right, (((1,), (0,)), ((), ())), preferred_element_type=F32)


def mm_nt(left, right):
    return lax.dot_general(left, right, (((1,), (1,)), ((), ())), preferred_element_type=F32)


def mm_tn(left, right):
    return lax.dot_general(left, right, (((0,), (0,)), ((), ())), preferred_element_type=F32)


def norm_parts(field):
    centred = field - jnp.mean(field, -1, keepdims=True)
    inverse = lax.rsqrt(jnp.mean(centred * centred, -1, keepdims=True) + EPSILON)
    return centred * inverse, inverse


def norm_backward(upstream, normed, inverse, gain):
    scaled = upstream * gain
    return inverse * (
        scaled
        - jnp.mean(scaled, -1, keepdims=True)
        - normed * jnp.mean(scaled * normed, -1, keepdims=True)
    )


def fold_rows(field):
    rows, cols = field.shape
    return jnp.sum(field.reshape(rows // 8, 8, cols), 0)


def tokens_of_block(block):
    return block.astype(F32).reshape(-1, block.shape[-1])


def tokens_of(ref):
    return tokens_of_block(ref[...])


def put_tokens(ref, field):
    block = field.reshape(ref.shape).astype(ref.dtype)
    ref[...] = block
    return block


def head_blocks(field):
    head = lax.broadcasted_iota(jnp.int32, field.shape, 1) >> 5
    return jnp.concatenate(
        [jnp.where(head == h, field, 0.0).astype(BF) for h in range(HEADS)], 0
    )


def gather_heads(stacked):
    head = lax.broadcasted_iota(jnp.int32, (SLOT, stacked.shape[1]), 1) >> 5
    total = stacked[:SLOT]
    for h in range(1, HEADS):
        total = jnp.where(head == h, stacked[h * SLOT : (h + 1) * SLOT], total)
    return total


def head_lanes():
    row = lax.broadcasted_iota(jnp.int32, (HEADS * SLOT, HEADS * HEAD_DIM), 0) >> 6
    col = lax.broadcasted_iota(jnp.int32, (HEADS * SLOT, HEADS * HEAD_DIM), 1) >> 5
    return jnp.where(row == col, 1.0, 0.0).astype(BF)


def segment_max(every):
    low = lax.broadcasted_iota(jnp.int32, (ASKED, 2 * SLOT), 1) < SLOT
    pairs = [s[:, start : start + 2 * SLOT] for s in every for start in (0, 2 * SLOT)]
    first = [jnp.max(jnp.where(low, pair, OFF), 1, keepdims=True) for pair in pairs]
    second = [jnp.max(jnp.where(low, OFF, pair), 1, keepdims=True) for pair in pairs]
    highest = [jnp.where(low, a, b) for a, b in zip(first, second)]
    return [jnp.concatenate(highest[n : n + 2], 1) for n in range(0, len(highest), 2)]


def zero_tails(first_step, count, *refs):
    @pl.when(first_step)
    def _():
        for ref in refs:
            ref[count:, :] = jnp.zeros((ref.shape[0] - count, ref.shape[1]), F32)


def first_of_grid():
    return pl.program_id(0) == 0


def window(ref, image, images, rows=SLOT):
    return ref[pl.ds(image, rows, stride=images), :]


def attention_forward(images, parts, bias, masks, powers_ref, out_ref, share_ref):
    sc_q, sc_k, sc_v = parts
    lanes = head_lanes()
    everything = range(images)
    scores = [
        mm_nt(window(sc_q, i, images, ASKED).astype(BF), head_blocks(window(sc_k, i, images)))
        * (SCALE * LOG2E)
        + bias
        for i in everything
    ]
    if masks is not None:
        apart = [masks[0, 0, i].astype(F32) * (-100.0 * LOG2E) for i in everything]
        scores = [scores[i] + jnp.concatenate([apart[i], apart[i]], 1) for i in everything]
    powers = [jnp.exp2(s - top) for s, top in zip(scores, segment_max(scores))]
    powers = [p.astype(BF) for p in powers]
    both = [
        mm(powers[i], jnp.concatenate([head_blocks(window(sc_v, i, images)), lanes], 1))
        for i in everything
    ]
    depth = lanes.shape[1]
    shares = [1.0 / one[:, depth:] for one in both]
    for i in everything:
        place = pl.ds(i, ASKED, stride=images)
        powers_ref[0, 0, i] = powers[i]
        out_ref[place, :] = both[i][:, :depth] * shares[i]
        share_ref[place, :] = shares[i]


def attention_backward(images, parts, sc_grad, sc_out, powers_ref, grads, bias_acc):
    sc_q, sc_k, sc_v = parts
    sc_dq, sc_dk, sc_dv = grads
    lanes = head_lanes()
    depth = lanes.shape[1]
    everything = range(images)
    upstream = [window(sc_grad, i, images, ASKED) for i in everything]
    centred = [
        mm_nt(
            jnp.concatenate([upstream[i], window(sc_out, i, images, ASKED)], 1).astype(BF),
            jnp.concatenate([head_blocks(window(sc_v, i, images)), lanes], 1),
        )
        for i in everything
    ]
    powers = [powers_ref[0, 0, i].astype(F32) for i in everything]
    score_grads = [powers[i] * centred[i] for i in everything]
    low_grads = [one.astype(BF) for one in score_grads]
    total = low_grads[0].astype(F32)
    for i in everything[1:]:
        total = total + low_grads[i].astype(F32)
    bias_acc[...] += total
    d_queries = [mm(low_grads[i], head_blocks(window(sc_k, i, images))) for i in everything]
    empty = jnp.zeros((ASKED, depth), F32)
    d_both = [
        mm_tn(
            jnp.concatenate([score_grads[i], powers[i]], 0).astype(BF),
            jnp.concatenate(
                [
                    jnp.concatenate([window(sc_q, i, images, ASKED), empty], 1),
                    jnp.concatenate([empty, upstream[i]], 1),
                ],
                0,
            ).astype(BF),
        )
        for i in everything
    ]
    for i in everything:
        place = pl.ds(i, SLOT, stride=images)
        sc_dq[pl.ds(i, ASKED, stride=images), :] = d_queries[i] * SCALE
        sc_dk[place, :] = gather_heads(d_both[i][:, :depth]) * SCALE
        sc_dv[place, :] = gather_heads(d_both[i][:, depth:])


def put_upstream(count, sc_grad, sc_out, gradient, out, share):
    shared = gradient * share
    sc_grad[:count, :] = shared
    sc_out[:count, :] = -(shared * out)


def put_norm(refs, normed, inverse):
    normed_ref, inverse_ref = refs
    normed_ref[0, 0] = normed.astype(BF)
    inverse_ref[0, 0] = jnp.broadcast_to(inverse, normed.shape).astype(BF)


def get_norm(refs):
    normed_ref, inverse_ref = refs
    return normed_ref[0, 0].astype(F32), inverse_ref[0, 0].astype(F32)


def split_projection(hidden, w_qkv, qv_ref, layer, parts, count):
    query_bias, value_bias = qv_ref[layer, 0:1], qv_ref[layer, 1:2]
    projected = mm(hidden, w_qkv) + jnp.concatenate(
        [query_bias, jnp.zeros_like(query_bias), value_bias], 1
    )
    projected = projected.astype(BF).astype(F32)
    depth = hidden.shape[1]
    for n, ref in enumerate(parts):
        ref[:count, :] = projected[:, n * depth : (n + 1) * depth]


def gelu_parts(expanded):
    cumulative = 0.5 + 0.5 * lax.erf(expanded * (1.0 / math.sqrt(2.0)))
    density = jnp.exp(expanded * expanded * -0.5) * (1.0 / math.sqrt(2.0 * math.pi))
    return expanded * cumulative, cumulative + expanded * density


def kernel_first_layer(
    images, place, rims, x_ref, w_qkv, w_proj, w_fc1, w_fc2, gains, shifts, outs, qkv_bias, fc1_bias, bias,
    stream_out, hidden_out, out_out, share_out, powers_out, expanded_out,
    n_one, r_one, n_two, r_two, n_next, r_next,
    sc_q, sc_k, sc_v, sc_out, sc_share,
):
    count = POS * images
    zero_tails(first_of_grid(), count, sc_q, sc_k, sc_v)
    stream = tokens_of(x_ref)
    normed, inverse = norm_parts(stream)
    put_norm((n_one, r_one), normed, inverse)
    hidden = (normed * gains[0, 0:1] + shifts[0, 0:1]).astype(BF)
    split_projection(hidden, w_qkv[...], qkv_bias, 0, (sc_q, sc_k, sc_v), count)
    attention_forward(images, (sc_q, sc_k, sc_v), bias[...], None, powers_out, sc_out, sc_share)
    attended = sc_out[:count, :].astype(BF)
    out_out[0, 0] = attended
    share_out[0, 0] = sc_share[:count, :]
    middle = stream + (mm(attended, w_proj[...]) + outs[0, 0:1])
    normed, inverse = norm_parts(middle)
    put_norm((n_two, r_two), normed, inverse)
    inner = (normed * gains[0, 1:2] + shifts[0, 1:2]).astype(BF)
    expanded = mm(inner, w_fc1[...]) + fc1_bias[0:1]
    expanded_out[0, 0] = expanded.astype(BF)
    activated = gelu_parts(expanded)[0].astype(BF)
    stream = middle + mm(activated, w_fc2[...]) + outs[0, 1:2]
    stream_out[0, 0] = stream
    normed, inverse = norm_parts(stream)
    put_norm((n_next, r_next), normed, inverse)
    block = put_tokens(hidden_out, normed * gains[1, 0:1] + shifts[1, 0:1])
    if rims is not None:
        put_rims(block, rims, place, "first")


def kernel_shifted_forward(
    images, place, rims, hidden_ref, *refs
):
    halo, refs = (None, refs) if rims is None else (refs[:3], refs[3:])
    (
        w_qkv, qkv_bias, bias, masks, out_out, share_out, powers_out,
        held, sc_q, sc_k, sc_v, sc_out, sc_share,
    ) = refs
    count = POS * images
    zero_tails(first_of_grid(), count, sc_q, sc_k, sc_v)
    hidden = ahead_window(hidden_ref, halo, held, place).astype(BF)
    split_projection(hidden, w_qkv[...], qkv_bias, 1, (sc_q, sc_k, sc_v), count)
    attention_forward(images, (sc_q, sc_k, sc_v), bias[...], masks, powers_out, sc_out, sc_share)
    share_out[0, 0] = sc_share[:count, :]
    block = put_tokens(out_out, sc_out[:count, :])
    if rims is not None:
        put_rims(block, rims, place, "last")


def feed_forward_backward(out_low, inner, activated, slope, w_fc1, w_fc2):
    expanded_low = (slope * mm_nt(out_low, w_fc2)).astype(BF)
    inner_grad = mm_nt(expanded_low, w_fc1)
    return expanded_low, inner_grad


def put_rims(block, rims, place, edge):
    rim_rows, rim_cols, corner = rims
    row, col, rows, cols = place
    start = 0 if edge == "first" else WIN - SHIFT
    keep = slice(start, start + SHIFT)
    row_rim = row == (0 if edge == "first" else rows - 1)
    col_rim = col == (0 if edge == "first" else cols - 1)

    @pl.when(row_rim)
    def _():
        rim_rows[:, pl.ds(col * WIN, WIN)] = block[keep]

    @pl.when(col_rim)
    def _():
        rim_cols[pl.ds(row * WIN, WIN)] = block[:, keep]

    @pl.when(row_rim & col_rim)
    def _():
        corner[...] = block[keep, keep]


def ahead_window(field, rims, held, place):
    row, col, rows, cols = place
    top, left = row * WIN + SHIFT, col * WIN + SHIFT
    if rims is None:
        return tokens_of_block(field[pl.ds(top, WIN), pl.ds(left, WIN)])
    rim_rows, rim_cols, corner = rims
    own = WIN - SHIFT
    low, far = row == rows - 1, col == cols - 1
    held[:own, :own] = field[pl.ds(top, own), pl.ds(left, own)]

    @pl.when(low)
    def _():
        held[own:, :own] = rim_rows[:, pl.ds(left, own)]

    @pl.when(jnp.logical_not(low))
    def _():
        held[own:, :own] = field[pl.ds(top + own, SHIFT), pl.ds(left, own)]

    @pl.when(far)
    def _():
        held[:own, own:] = rim_cols[pl.ds(top, own)]

    @pl.when(jnp.logical_not(far))
    def _():
        held[:own, own:] = field[pl.ds(top, own), pl.ds(left + own, SHIFT)]

    @pl.when(low & far)
    def _():
        held[own:, own:] = corner[...]

    @pl.when(low & jnp.logical_not(far))
    def _():
        held[own:, own:] = rim_rows[:, pl.ds(left + own, SHIFT)]

    @pl.when(jnp.logical_not(low) & far)
    def _():
        held[own:, own:] = rim_cols[pl.ds(top + own, SHIFT)]

    return tokens_of_block(held[...])


def behind_window(field, rims, held, place):
    row, col, _, _ = place
    top, left = row * WIN, col * WIN
    if rims is None:
        return tokens_of_block(field[pl.ds(top - SHIFT, WIN), pl.ds(left - SHIFT, WIN)])
    rim_rows, rim_cols, corner = rims
    own = WIN - SHIFT
    high, near = row == 0, col == 0
    held[SHIFT:, SHIFT:] = field[pl.ds(top, own), pl.ds(left, own)]

    @pl.when(high)
    def _():
        held[:SHIFT, SHIFT:] = rim_rows[:, pl.ds(left, own)]

    @pl.when(jnp.logical_not(high))
    def _():
        held[:SHIFT, SHIFT:] = field[pl.ds(top - SHIFT, SHIFT), pl.ds(left, own)]

    @pl.when(near)
    def _():
        held[SHIFT:, :SHIFT] = rim_cols[pl.ds(top, own)]

    @pl.when(jnp.logical_not(near))
    def _():
        held[SHIFT:, :SHIFT] = field[pl.ds(top, own), pl.ds(left - SHIFT, SHIFT)]

    @pl.when(high & near)
    def _():
        held[:SHIFT, :SHIFT] = corner[...]

    @pl.when(high & jnp.logical_not(near))
    def _():
        held[:SHIFT, :SHIFT] = rim_rows[:, pl.ds(left - SHIFT, SHIFT)]

    @pl.when(jnp.logical_not(high) & near)
    def _():
        held[:SHIFT, :SHIFT] = rim_cols[pl.ds(top - SHIFT, SHIFT)]

    @pl.when(jnp.logical_not(high) & jnp.logical_not(near))
    def _():
        held[:SHIFT, :SHIFT] = field[pl.ds(top - SHIFT, SHIFT), pl.ds(left - SHIFT, SHIFT)]

    return tokens_of_block(held[...])


def kernel_middle(images, place, rims, out_ref, *refs):
    halo, refs = (None, refs) if rims is None else (refs[:3], refs[3:])
    (
        stream_ref, cot_ref, w_proj, w_fc1, w_fc2, gains, shifts, outs, fc1_bias,
        mixed_out, grad_out, low_out, g_proj, g_fc1, g_fc2, sums, fc1_sums, held,
    ) = refs
    stream = stream_ref[0, 0]
    attended = behind_window(out_ref, halo, held, place).astype(BF)
    middle = stream + (mm(attended, w_proj[...]) + outs[1, 0:1])
    normed, inverse = norm_parts(middle)
    inner = (normed * gains[1, 1:2] + shifts[1, 1:2]).astype(BF)
    activated, slope = gelu_parts(mm(inner, w_fc1[...]) + fc1_bias[1:2])
    activated = activated.astype(BF)
    put_tokens(mixed_out, middle + mm(activated, w_fc2[...]) + outs[1, 1:2])
    gradient = tokens_of(cot_ref)
    out_low = gradient.astype(BF)
    expanded_low, inner_grad = feed_forward_backward(
        out_low, inner, activated, slope, w_fc1[...], w_fc2[...]
    )
    g_fc2[...] += mm_tn(out_low, activated)
    g_fc1[...] += mm_tn(inner, expanded_low)
    fc1_sums[...] += fold_rows(expanded_low.astype(F32))
    norm_term = norm_backward(inner_grad, normed, inverse, gains[1, 1:2])
    updated = gradient + norm_term
    grad_out[0, 0] = updated
    branch_low = updated.astype(BF)
    g_proj[...] += mm_tn(attended, branch_low)
    block = put_tokens(low_out, mm_nt(branch_low, w_proj[...]))
    if rims is not None:
        put_rims(block, rims, place, "first")
    sums[0] += fold_rows(gradient)
    sums[1] += fold_rows(inner_grad * normed)
    sums[2] += fold_rows(inner_grad)
    sums[3] += fold_rows(branch_low.astype(F32))


def joined_gradients(count, grads, qv_sums):
    pieces = [ref[:count, :].astype(BF) for ref in grads]
    qv_sums[0] += fold_rows(pieces[0].astype(F32))
    qv_sums[1] += fold_rows(pieces[2].astype(F32))
    return jnp.concatenate(pieces, 1)


def kernel_shifted_backward(images, place, rims, hidden_ref, low_ref, *refs):
    halo, low_halo, refs = (
        (None, None, refs) if rims is None else (refs[:3], refs[3:6], refs[6:])
    )
    (
        out_ref, share_ref, powers_ref, w_qkv, qkv_bias, hidden_grad_out, g_qkv, qv_sums, bias_acc,
        held, sc_q, sc_k, sc_v, sc_out, sc_grad, sc_dq, sc_dk, sc_dv,
    ) = refs
    count = POS * images
    zero_tails(first_of_grid(), count, sc_q, sc_k, sc_v, sc_out, sc_grad)
    hidden = ahead_window(hidden_ref, halo, held, place).astype(BF)
    split_projection(hidden, w_qkv[...], qkv_bias, 1, (sc_q, sc_k, sc_v), count)
    gradient = ahead_window(low_ref, low_halo, held, place)
    put_upstream(count, sc_grad, sc_out, gradient, tokens_of(out_ref), share_ref[0, 0])
    grads = (sc_dq, sc_dk, sc_dv)
    attention_backward(images, (sc_q, sc_k, sc_v), sc_grad, sc_out, powers_ref, grads, bias_acc)
    joined = joined_gradients(count, grads, qv_sums)
    g_qkv[...] += mm_tn(hidden, joined)
    block = put_tokens(hidden_grad_out, mm_nt(joined, w_qkv[...]))
    if rims is not None:
        put_rims(block, rims, place, "last")


def kernel_first_backward(
    images, place, rims, hidden_grad_ref, rim_rows, rim_cols, corner, grad_ref,
    n_one, r_one, n_two, r_two, n_next, r_next, expanded_ref, att_ref, share_ref, powers_ref,
    w_qkv, w_proj, w_fc1, w_fc2, gains, shifts, qkv_bias,
    tokens_grad_out, g_qkv, g_proj, g_fc1, g_fc2, sums, fc1_sums, qv_sums, bias_acc,
    held, sc_q, sc_k, sc_v, sc_out, sc_grad, sc_dq, sc_dk, sc_dv,
):
    count = POS * images
    zero_tails(first_of_grid(), count, sc_q, sc_k, sc_v, sc_out, sc_grad)
    upstream = behind_window(hidden_grad_ref, (rim_rows, rim_cols, corner), held, place)
    normed_one, inverse_one = get_norm((n_one, r_one))
    hidden = (normed_one * gains[0, 0:1] + shifts[0, 0:1]).astype(BF)
    normed, inverse = get_norm((n_next, r_next))
    gradient = grad_ref[0, 0] + norm_backward(upstream, normed, inverse, gains[1, 0:1])
    sums[4] += fold_rows(upstream * normed)
    sums[5] += fold_rows(upstream)
    out_low = gradient.astype(BF)
    normed, inverse = get_norm((n_two, r_two))
    inner = (normed * gains[0, 1:2] + shifts[0, 1:2]).astype(BF)
    activated, slope = gelu_parts(expanded_ref[0, 0].astype(F32))
    activated = activated.astype(BF)
    expanded_low, inner_grad = feed_forward_backward(
        out_low, inner, activated, slope, w_fc1[...], w_fc2[...]
    )
    updated = gradient + norm_backward(inner_grad, normed, inverse, gains[0, 1:2])
    branch_low = updated.astype(BF)
    low = mm_nt(branch_low, w_proj[...]).astype(BF).astype(F32)
    attended = att_ref[0, 0]
    split_projection(hidden, w_qkv[...], qkv_bias, 0, (sc_q, sc_k, sc_v), count)
    put_upstream(count, sc_grad, sc_out, low, attended.astype(F32), share_ref[0, 0])
    grads = (sc_dq, sc_dk, sc_dv)
    attention_backward(images, (sc_q, sc_k, sc_v), sc_grad, sc_out, powers_ref, grads, bias_acc)
    g_fc2[...] += mm_tn(out_low, activated)
    g_fc1[...] += mm_tn(inner, expanded_low)
    g_proj[...] += mm_tn(attended, branch_low)
    fc1_sums[...] += fold_rows(expanded_low.astype(F32))
    sums[0] += fold_rows(out_low.astype(F32))
    sums[1] += fold_rows(inner_grad * normed)
    sums[2] += fold_rows(inner_grad)
    sums[3] += fold_rows(branch_low.astype(F32))
    joined = joined_gradients(count, grads, qv_sums)
    g_qkv[...] += mm_tn(hidden, joined)
    upstream = mm_nt(joined, w_qkv[...])
    term = norm_backward(upstream, normed_one, inverse_one, gains[0, 0:1])
    put_tokens(tokens_grad_out, updated + term)
    sums[6] += fold_rows(upstream * normed_one)
    sums[7] += fold_rows(upstream)


def shift_by(array, axis, by):
    count = lax.axis_size(axis)
    return lax.ppermute(array, axis, [(i, (i + by) % count) for i in range(count)])


def shift_both(array, by):
    rows, cols = lax.axis_size("seq"), lax.axis_size("wt")
    pairs = [
        (r * cols + c, ((r + by) % rows) * cols + (c + by) % cols)
        for r in range(rows)
        for c in range(cols)
    ]
    return lax.ppermute(array, ("seq", "wt"), pairs)


def send_rims(rims, by):
    rim_rows, rim_cols, corner = rims
    return (
        shift_by(rim_rows, "seq", by),
        shift_by(rim_cols, "wt", by),
        shift_both(corner, by),
    )


def window_order(part, rows, cols):
    if part == "all":
        return rows * cols, lambda i: (i // cols, i % cols)
    edge, rim = part
    if rim:
        base = 0 if edge == "first" else rows - 1
        side = 0 if edge == "first" else cols - 1
        skip = 1 if edge == "first" else 0
        return rows + cols - 1, lambda i: (
            jnp.where(i < cols, base, i - cols + skip),
            jnp.where(i < cols, i, side),
        )
    skip = 1 if edge == "first" else 0
    return (rows - 1) * (cols - 1), lambda i: (
        i // (cols - 1) + skip,
        i % (cols - 1) + skip,
    )


def axis_sizes():
    return lax.axis_size("seq"), lax.axis_size("wt")


def blocks_of(matrix):
    return [matrix[:, i : i + 128] for i in range(0, matrix.shape[1], 128)]


def pack_slices(w_qkv, w_proj, w_fc1, w_fc2):
    return jnp.concatenate([*blocks_of(w_qkv), w_proj, *blocks_of(w_fc1), w_fc2], 0)


def kernel_weights(parts, place_ref, *refs):
    pieces, (qkv, proj, fc1, fc2), (s_qkv, s_proj, s_fc1, s_fc2) = (
        refs[:parts], refs[parts : parts + 4], refs[parts + 4 :]
    )
    rows = s_qkv.shape[0] // parts
    for k in range(parts):
        owner = lax.rem(place_ref[0] + k, parts)
        piece = pieces[k][...].astype(F32)
        near = pl.ds(pl.multiple_of(owner * rows, rows), rows)
        at = 0
        for target in (s_qkv, s_proj, s_fc1):
            for i in range(0, target.shape[1], 128):
                target[near, i : i + 128] = piece[at : at + rows]
                at += rows
        far = s_fc2.shape[0] // parts
        s_fc2[pl.ds(pl.multiple_of(owner * far, far), far), :] = piece[at : at + far]
    for out, held in ((qkv, s_qkv), (proj, s_proj), (fc1, s_fc1), (fc2, s_fc2)):
        out[...] = held[...].astype(BF)


def whole_weights(place, packed, depth, wide):
    parts = lax.axis_size("wt")
    pieces = [packed] + [shift_by(packed, "wt", -k) for k in range(1, parts)]
    shapes = [(depth, 3 * depth), (depth, depth), (depth, wide), (wide, depth)]

    def body(*refs):
        kernel_weights(parts, *refs)

    full = pl.BlockSpec(memory_space=pltpu.VMEM)
    return pl.pallas_call(
        body,
        in_specs=[pl.BlockSpec(memory_space=pltpu.SMEM)] + [full] * parts,
        out_specs=[full] * 4,
        out_shape=[jax.ShapeDtypeStruct(shape, BF) for shape in shapes],
        scratch_shapes=[pltpu.VMEM(shape, F32) for shape in shapes],
    )(place, *pieces)


SMALL_ROWS = 8


def split_high(field):
    high = field.astype(BF)
    return high, (field - high.astype(F32)).astype(BF)


def small_rows(refs):
    (sums0, sums1, qv0, qv1, fc1_0, fc1_1, table) = refs

    def one(ref, k):
        return jnp.sum(ref[k], 0, keepdims=True)

    rows = [
        one(sums0, 6), one(sums0, 1), one(sums0, 4), one(sums1, 1),
        one(sums0, 7), one(sums0, 2), one(sums0, 5), one(sums1, 2),
        one(qv0, 0), one(qv0, 1), one(qv1, 0), one(qv1, 1),
        one(sums0, 3), one(sums0, 0), one(sums1, 3), one(sums1, 0),
    ]
    for ref in (fc1_0, fc1_1):
        line = jnp.sum(ref[...], 0, keepdims=True)
        rows += [line[:, i : i + 128] for i in range(0, line.shape[1], 128)]
    size = table.shape[1]
    for i in range(0, size, 128):
        piece = table[:, i : min(i + 128, size)]
        gap = 128 - piece.shape[1]
        if gap:
            piece = jnp.concatenate([piece, jnp.zeros((piece.shape[0], gap), F32)], 1)
        rows.append(piece)
    return rows


def kernel_pack(seqs, parts, each, *refs):
    grads, smalls, out, held, lines = refs[:8], refs[8:15], refs[15], refs[16], refs[17]
    depth = grads[0].shape[0]
    rows = depth // parts
    lines[...] = jnp.zeros_like(lines)
    at = 0
    for row in small_rows(smalls):
        lines[at : at + row.shape[0], :] = row
        at += row.shape[0]
    per = -(-at // seqs)
    turned = [grads[3][...].T, grads[7][...].T]
    for w in range(parts):
        near = slice(w * rows, (w + 1) * rows)
        at = 0
        for layer in range(2):
            for grad in grads[4 * layer : 4 * layer + 3]:
                for i in range(0, grad.shape[1], 128):
                    held[at : at + rows, :] = grad[near, i : i + 128]
                    at += rows
            far = turned[layer].shape[0] // parts
            held[at : at + far, :] = turned[layer][w * far : (w + 1) * far]
            at += far
        for s in range(seqs):
            mine = held[s * each : s * each + out.shape[1] - 2 * SMALL_ROWS, :]
            high, low = split_high(lines[s * per : s * per + SMALL_ROWS, :])
            out[s * parts + w] = jnp.concatenate(
                [mine, high.astype(F32), low.astype(F32)], 0
            ).astype(BF)


def kernel_reduce(packet_ref, out_ref):
    total = packet_ref[0].astype(F32)
    for i in range(1, packet_ref.shape[0]):
        total = total + packet_ref[i].astype(F32)
    rows = total.shape[0] - 2 * SMALL_ROWS
    high, low = split_high(total[rows : rows + SMALL_ROWS] + total[rows + SMALL_ROWS :])
    out_ref[...] = jnp.concatenate(
        [total[:rows], high.astype(F32), low.astype(F32)], 0
    ).astype(BF)


def kernel_unpack(each, per, packets, *refs):
    (gains, shifts, qkv, qv, table, proj, outs, fc1, fc1_bias, fc2, held, lines) = refs
    seqs, size, _ = packets.shape
    for s in range(seqs):
        packet = packets[s].astype(F32)
        start = size - 2 * SMALL_ROWS
        held[s * each : (s + 1) * each, :] = packet[:each]
        both = packet[start : start + SMALL_ROWS] + packet[start + SMALL_ROWS :]
        lines[s * per : (s + 1) * per, :] = both[:per]
    at = 0
    for layer in range(2):
        for target in (qkv, proj, fc1):
            rows = target.shape[1]
            for i in range(0, target.shape[2], 128):
                target[layer, :, i : i + 128] = held[at : at + rows, :]
                at += rows
        far = fc2.shape[1]
        fc2[layer] = held[at : at + far, :]
        at += far
    at = 0
    for target in (gains, shifts, qv, outs):
        for layer in range(2):
            target[layer] = lines[at : at + 2, :]
            at += 2
    for layer in range(2):
        for i in range(0, fc1_bias.shape[1], 128):
            fc1_bias[layer : layer + 1, i : i + 128] = lines[at : at + 1, :]
            at += 1
    for i in range(0, table.shape[2], 128):
        wide = min(128, table.shape[2] - i)
        for layer in range(2):
            table[layer, :, i : i + wide] = lines[at : at + HEADS, :wide]
            at += HEADS


def whole_kernel(body, inputs, outputs, scratch=()):
    full = pl.BlockSpec(memory_space=pltpu.VMEM)
    return pl.pallas_call(
        body,
        in_specs=[full] * len(inputs),
        out_specs=[full] * len(outputs),
        out_shape=[jax.ShapeDtypeStruct(*out) for out in outputs],
        scratch_shapes=[pltpu.VMEM(shape, F32) for shape in scratch],
        compiler_params=pltpu.CompilerParams(vmem_limit_bytes=VMEM_LIMIT),
    )(*inputs)


def sum_everywhere(grads, smalls, depth, wide):
    seqs, parts = axis_sizes()
    rows = depth // parts
    held = 2 * (4 * depth + 2 * wide) // parts
    each = held // seqs
    size = -(-each // 16) * 16 + 2 * SMALL_ROWS
    count = 16 + 2 * (wide // 128) + 2 * HEADS * -(-smalls[-1].shape[1] // 128)
    per = -(-count // seqs)
    tail = (seqs * per + SMALL_ROWS, 128)

    def pack(*refs):
        kernel_pack(seqs, parts, each, *refs)

    def unpack(*refs):
        kernel_unpack(each, per, *refs)

    (packets,) = whole_kernel(
        pack,
        [*grads, *smalls],
        [((seqs * parts, size, 128), BF)],
        [(held + 16, 128), tail],
    )
    packets = lax.all_to_all(packets, ("seq", "wt"), 0, 0, tiled=True)
    (mine,) = whole_kernel(kernel_reduce, [packets], [((size, 128), BF)])
    mine = lax.all_gather(mine, "seq", axis=0)
    return whole_kernel(
        unpack,
        [mine],
        [
            ((2, 2, depth), F32), ((2, 2, depth), F32), ((2, rows, 3 * depth), F32),
            ((2, 2, depth), F32), ((2, HEADS, smalls[-1].shape[1]), F32),
            ((2, rows, depth), F32),
            ((2, 2, depth), F32), ((2, rows, wide), F32), ((2, wide), F32),
            ((2, wide // parts, depth), F32),
        ],
        [(held, 128), tail],
    )


def per_device(
    tokens, region, rel_index, norm_gain, norm_bias, w_qkv, qv_bias, pos_table, w_proj, out_bias,
    w_fc1, fc1_bias, w_fc2, cotangent,
):
    images, height, width, depth = tokens.shape
    wide = w_fc1.shape[-1]
    rows, cols = height // WIN, width // WIN
    count = POS * images
    table_size = pos_table.shape[1]

    place = lax.axis_index("wt").astype(jnp.int32)[None]
    slices = [pack_slices(w_qkv[l], w_proj[l], w_fc1[l], w_fc2[l]) for l in range(2)]
    first_weights = whole_weights(place, slices[0], depth, wide)
    x = tokens.transpose(1, 2, 0, 3)
    cot = cotangent.transpose(1, 2, 0, 3)
    selector = (
        rel_index.reshape(-1)[:, None] == jnp.arange(table_size, dtype=jnp.int32)[None, :]
    ).astype(F32)
    tables = jnp.dot(
        selector,
        pos_table.transpose(1, 0, 2).reshape(table_size, 2 * HEADS) * LOG2E,
        precision=lax.Precision.HIGHEST,
    ).reshape(POS, POS, 2, HEADS)
    padded = jnp.pad(
        jnp.pad(tables.transpose(2, 0, 3, 1), ((0, 0), (0, ASKED - POS), (0, 0), (0, 0))),
        ((0, 0), (0, 0), (0, 0), (0, SLOT - POS)),
        constant_values=OFF,
    )
    biases = padded.reshape(2, ASKED, HEADS * SLOT)
    ids = region.reshape(images, rows, WIN, cols, WIN).transpose(1, 3, 0, 2, 4)
    ids = ids.reshape(rows, cols, images, POS)
    apart = (ids[..., :, None] != ids[..., None, :]).astype(BF)
    apart = jnp.pad(apart, [(0, 0)] * 3 + [(0, ASKED - POS), (0, SLOT - POS)])
    masks = jnp.concatenate([apart, apart], -1)

    first_weights, masks = lax.optimization_barrier((first_weights, masks))

    field_shape = (height, width, images, depth)
    field = ((WIN, WIN, images, depth), lambda r, c: (r, c, 0, 0))
    probs_spec = ((1, 1, images, ASKED, HEADS * SLOT), lambda r, c: (r, c, 0, 0, 0))
    mask_spec = ((1, 1, images, ASKED, 2 * SLOT), lambda r, c: (r, c, 0, 0, 0))

    def flat(columns):
        return (1, 1, count, columns), lambda r, c: (r, c, 0, 0)

    def flat_type(columns, dtype):
        return jax.ShapeDtypeStruct((rows, cols, count, columns), dtype)

    probs_type = jax.ShapeDtypeStruct((rows, cols, images, ASKED, HEADS * SLOT), BF)
    rim_types = [
        jax.ShapeDtypeStruct((SHIFT, width, images, depth), BF),
        jax.ShapeDtypeStruct((height, SHIFT, images, depth), BF),
        jax.ShapeDtypeStruct((SHIFT, SHIFT, images, depth), BF),
    ]

    def run(kernel, part, inputs, outputs, slots, limit, earlier=None, held=False, group=1):
        steps, order = window_order(part, rows, cols // group)

        def spec_of(spec, shape):
            if spec is None:
                return pl.BlockSpec(tuple(shape), lambda i: (0,) * len(shape))
            block, index = spec
            block = (block[0], block[1] * group, *block[2:])
            return pl.BlockSpec(block, lambda i: index(*order(i)))

        with_rims = part != "all" and part[1]
        n_in, n_out = len(inputs), len(outputs)
        ins = [a for a, _ in inputs]
        in_specs = [spec_of(spec, a.shape) for a, spec in inputs]
        aliases = {}
        if earlier is not None:
            for n, (array, (_, spec)) in enumerate(zip(earlier, outputs)):
                if spec is not None:
                    aliases[len(ins)] = n
                ins.append(array)
                in_specs.append(
                    spec_of(None, array.shape)
                    if spec is None
                    else pl.BlockSpec(memory_space=pl.ANY)
                )
        n_all = len(ins)
        types = [t for t, _ in outputs] + (rim_types if with_rims else [])
        out_specs = [spec_of(spec, t.shape) for t, spec in outputs]
        out_specs += [spec_of(None, t.shape) for t in rim_types] if with_rims else []

        def body(*refs):
            row, col = order(pl.program_id(0))
            outs = refs[n_all : n_all + n_out]
            rims = refs[n_all + n_out : n_all + n_out + 3] if with_rims else None
            rest = refs[n_all + len(types) :]

            @pl.when(first_of_grid())
            def _():
                for n, (_, spec) in enumerate(outputs):
                    if spec is None:
                        if earlier is None:
                            outs[n][...] = jnp.zeros_like(outs[n])
                        else:
                            outs[n][...] = refs[n_in + n][...]

            def view(ref, spec, k):
                if spec is None or group == 1:
                    return ref
                size = spec[0][1]
                return ref.at[:, pl.ds(k * size, size)]

            each = len(rest) // group
            for k in range(group):
                kernel(
                    images,
                    (row, col * group + k, rows, cols),
                    rims,
                    *[view(ref, spec, k) for ref, (_, spec) in zip(refs[:n_in], inputs)],
                    *[view(ref, spec, k) for ref, (_, spec) in zip(outs, outputs)],
                    *rest[k * each : (k + 1) * each],
                )

        scratch = [pltpu.VMEM((WIN, WIN, images, depth), BF)] if held else []
        scratch += [pltpu.VMEM((SLOT * images, depth), F32)] * slots
        results = pl.pallas_call(
            body,
            grid=(steps,),
            in_specs=in_specs,
            out_specs=out_specs,
            out_shape=types,
            scratch_shapes=scratch * group,
            input_output_aliases=aliases,
            compiler_params=pltpu.CompilerParams(vmem_limit_bytes=limit * MIB),
            cost_estimate=pl.CostEstimate(
                flops=steps * 10**9, bytes_accessed=10**7, transcendentals=0
            ),
        )(*ins)
        return results[:n_out], results[n_out:]

    def run_both(kernel, edge, inputs, halos, outputs, slots, by, limits, held=False, beside=None):
        lead = len(halos)
        rim_inputs = [(a, None) for halo in halos for a in halo]
        inputs_a = inputs[:lead] + rim_inputs + inputs[lead:]
        first, rims = run(
            kernel, (edge, True), inputs_a, outputs, slots, limits[0], held=held
        )
        if beside is not None:
            rims, beside = lax.optimization_barrier((rims, beside))
            beside = whole_weights(place, beside, depth, wide)
        rims = send_rims(rims, by)
        second, _ = run(
            kernel, (edge, False), inputs, outputs, slots, limits[1], first, held=held
        )
        return (second, rims) if beside is None else (second, rims, beside)

    def total(*shape):
        return (jax.ShapeDtypeStruct(shape, F32), None)

    qkv0, proj0, fc10, fc20 = first_weights
    (
        (stream1, hidden1, att0, share0, powers0, expanded0, *norms0),
        halo,
        (qkv1, proj1, fc11, fc21),
    ) = run_both(
        kernel_first_layer,
        "first",
        [
            (x, field), (qkv0, None), (proj0, None), (fc10, None), (fc20, None), (norm_gain, None),
            (norm_bias, None), (out_bias, None), (qv_bias, None), (fc1_bias, None),
            (biases[0], None),
        ],
        [],
        [
            (flat_type(depth, F32), flat(depth)),
            (jax.ShapeDtypeStruct(field_shape, BF), field),
            (flat_type(depth, BF), flat(depth)),
            (flat_type(depth, F32), flat(depth)),
            (probs_type, probs_spec),
            (flat_type(wide, BF), flat(wide)),
            *[(flat_type(depth, BF), flat(depth))] * 6,
        ],
        5,
        -1,
        LIMITS[0],
        beside=slices[1],
    )
    (att1, share1, powers1), out_halo = run_both(
        kernel_shifted_forward,
        "last",
        [
            (hidden1, None), (qkv1, None), (qv_bias, None), (biases[1], None),
            (masks, mask_spec),
        ],
        [halo],
        [
            (jax.ShapeDtypeStruct(field_shape, BF), field),
            (flat_type(depth, F32), flat(depth)),
            (probs_type, probs_spec),
        ],
        5,
        1,
        LIMITS[1],
        held=True,
    )
    (mixed, grad1, low1, g_proj1, g_fc11, g_fc21, sums1, fc1_sums1), low_halo = run_both(
        kernel_middle,
        "first",
        [
            (att1, None), (stream1, flat(depth)), (cot, field), (proj1, None),
            (fc11, None), (fc21, None), (norm_gain, None), (norm_bias, None),
            (out_bias, None), (fc1_bias, None),
        ],
        [out_halo],
        [
            (jax.ShapeDtypeStruct(field_shape, BF), field),
            (flat_type(depth, F32), flat(depth)),
            (jax.ShapeDtypeStruct(field_shape, BF), field),
            total(depth, depth), total(depth, wide), total(depth, wide), total(4, 8, depth),
            total(8, wide),
        ],
        0,
        -1,
        LIMITS[2],
        held=True,
    )
    (hidden_grad1, g_qkv1, qv_sums1, bias_sums1), grad_halo = run_both(
        kernel_shifted_backward,
        "last",
        [
            (hidden1, None), (low1, None), (att1, field), (share1, flat(depth)),
            (powers1, probs_spec),
            (qkv1, None), (qv_bias, None),
        ],
        [halo, low_halo],
        [
            (jax.ShapeDtypeStruct(field_shape, BF), field),
            total(depth, 3 * depth), total(2, 8, depth), total(ASKED, HEADS * SLOT),
        ],
        8,
        1,
        LIMITS[3],
        held=True,
    )
    (
        tokens_grad, g_qkv0, g_proj0, g_fc10, g_fc20, sums0, fc1_sums0, qv_sums0, bias_sums0
    ), _ = run(
        kernel_first_backward,
        "all",
        [
            (hidden_grad1, None), *[(a, None) for a in grad_halo], (grad1, flat(depth)),
            *[(a, flat(depth)) for a in norms0], (expanded0, flat(wide)),
            (att0, flat(depth)), (share0, flat(depth)), (powers0, probs_spec),
            (qkv0, None), (proj0, None), (fc10, None), (fc20, None), (norm_gain, None),
            (norm_bias, None), (qv_bias, None),
        ],
        [
            (jax.ShapeDtypeStruct(field_shape, F32), field),
            total(depth, 3 * depth), total(depth, depth), total(depth, wide), total(depth, wide),
            total(8, 8, depth), total(8, wide), total(2, 8, depth), total(ASKED, HEADS * SLOT),
        ],
        8,
        LIMITS[4],
        held=True,
    )

    bias_sums = jnp.stack([bias_sums0, bias_sums1]).reshape(2, ASKED, HEADS, SLOT)
    bias_sums = bias_sums[:, :POS, :, :POS].transpose(0, 2, 1, 3).reshape(2 * HEADS, POS * POS)
    table = jnp.dot(bias_sums, selector, precision=lax.Precision.HIGHEST)
    gains, shifts, d_qkv, d_qv, d_table, d_proj, d_out, d_fc1, d_fc1_bias, d_fc2 = sum_everywhere(
        [g_qkv0, g_proj0, g_fc10, g_fc20, g_qkv1, g_proj1, g_fc11, g_fc21],
        [sums0, sums1, qv_sums0, qv_sums1, fc1_sums0, fc1_sums1, table],
        depth,
        wide,
    )
    d_table = d_table.transpose(0, 2, 1)
    return (
        mixed.transpose(2, 0, 1, 3), tokens_grad.transpose(2, 0, 1, 3), gains, shifts, d_qkv,
        d_qv, d_table, d_proj, d_out, d_fc1, d_fc1_bias, d_fc2,
    )


def solution(mesh):
    field = P(None, "seq", "wt", None)
    shared = P(None, "wt", None)
    return jax.shard_map(
        per_device,
        mesh=mesh,
        in_specs=(
            field, P(None, "seq", "wt"), P(), P(), P(), shared, P(), P(), shared, P(), shared, P(),
            shared, field,
        ),
        out_specs=(
            field, field, P(), P(), shared, P(), P(), shared, P(), shared, P(), shared,
        ),
        check_vma=False,
    )
```

```python
import math

import jax
import jax.numpy as jnp
from jax import lax
from jax.experimental import pallas as pl
from jax.experimental.pallas import tpu as pltpu
from jax.sharding import PartitionSpec as P

HEADS = 4
WIN = 7
SHIFT = 3
HEAD_DIM = 32
EPSILON = 1e-05
POS = WIN * WIN
SLOT = 64
ASKED = 56
LOG2E = math.log2(math.e)
SCALE = 1.0 / math.sqrt(HEAD_DIM)
OFF = -1e30
BF = jnp.bfloat16
F32 = jnp.float32
MIB = 1024 * 1024
VMEM_LIMIT = 56 * MIB
GROUP = 2
LIMITS = ((60, 60), (16, 16), (16, 16), (16, 16), 63)


def mm(left, right):
    return lax.dot_general(left, right, (((1,), (0,)), ((), ())), preferred_element_type=F32)


def mm_nt(left, right):
    return lax.dot_general(left, right, (((1,), (1,)), ((), ())), preferred_element_type=F32)


def mm_tn(left, right):
    return lax.dot_general(left, right, (((0,), (0,)), ((), ())), preferred_element_type=F32)


def norm_parts(field):
    centred = field - jnp.mean(field, -1, keepdims=True)
    inverse = lax.rsqrt(jnp.mean(centred * centred, -1, keepdims=True) + EPSILON)
    return centred * inverse, inverse


def norm_backward(upstream, normed, inverse, gain):
    scaled = upstream * gain
    return inverse * (
        scaled
        - jnp.mean(scaled, -1, keepdims=True)
        - normed * jnp.mean(scaled * normed, -1, keepdims=True)
    )


def fold_rows(field):
    rows, cols = field.shape
    return jnp.sum(field.reshape(rows // 8, 8, cols), 0)


def tokens_of_block(block):
    return block.astype(F32).reshape(-1, block.shape[-1])


def tokens_of(ref):
    return tokens_of_block(ref[...])


def put_tokens(ref, field):
    block = field.reshape(ref.shape).astype(ref.dtype)
    ref[...] = block
    return block


def head_blocks(field):
    head = lax.broadcasted_iota(jnp.int32, field.shape, 1) >> 5
    return jnp.concatenate(
        [jnp.where(head == h, field, 0.0).astype(BF) for h in range(HEADS)], 0
    )


def gather_heads(stacked):
    head = lax.broadcasted_iota(jnp.int32, (SLOT, stacked.shape[1]), 1) >> 5
    total = stacked[:SLOT]
    for h in range(1, HEADS):
        total = jnp.where(head == h, stacked[h * SLOT : (h + 1) * SLOT], total)
    return total


def head_lanes():
    row = lax.broadcasted_iota(jnp.int32, (HEADS * SLOT, HEADS * HEAD_DIM), 0) >> 6
    col = lax.broadcasted_iota(jnp.int32, (HEADS * SLOT, HEADS * HEAD_DIM), 1) >> 5
    return jnp.where(row == col, 1.0, 0.0).astype(BF)


def segment_max(every):
    low = lax.broadcasted_iota(jnp.int32, (ASKED, 2 * SLOT), 1) < SLOT
    pairs = [s[:, start : start + 2 * SLOT] for s in every for start in (0, 2 * SLOT)]
    first = [jnp.max(jnp.where(low, pair, OFF), 1, keepdims=True) for pair in pairs]
    second = [jnp.max(jnp.where(low, OFF, pair), 1, keepdims=True) for pair in pairs]
    highest = [jnp.where(low, a, b) for a, b in zip(first, second)]
    return [jnp.concatenate(highest[n : n + 2], 1) for n in range(0, len(highest), 2)]


def zero_tails(first_step, count, *refs):
    @pl.when(first_step)
    def _():
        for ref in refs:
            ref[count:, :] = jnp.zeros((ref.shape[0] - count, ref.shape[1]), F32)


def first_of_grid():
    return pl.program_id(0) == 0


def window(ref, image, images, rows=SLOT):
    return ref[pl.ds(image, rows, stride=images), :]


def attention_forward(images, parts, bias, masks, powers_ref, out_ref, share_ref):
    sc_q, sc_k, sc_v = parts
    lanes = head_lanes()
    everything = range(images)
    scores = [
        mm_nt(window(sc_q, i, images, ASKED).astype(BF), head_blocks(window(sc_k, i, images)))
        * (SCALE * LOG2E)
        + bias
        for i in everything
    ]
    if masks is not None:
        apart = [masks[0, 0, i].astype(F32) * (-100.0 * LOG2E) for i in everything]
        scores = [scores[i] + jnp.concatenate([apart[i], apart[i]], 1) for i in everything]
    powers = [jnp.exp2(s - top) for s, top in zip(scores, segment_max(scores))]
    powers = [p.astype(BF) for p in powers]
    both = [
        mm(powers[i], jnp.concatenate([head_blocks(window(sc_v, i, images)), lanes], 1))
        for i in everything
    ]
    depth = lanes.shape[1]
    shares = [1.0 / one[:, depth:] for one in both]
    for i in everything:
        place = pl.ds(i, ASKED, stride=images)
        powers_ref[0, 0, i] = powers[i]
        out_ref[place, :] = both[i][:, :depth] * shares[i]
        share_ref[place, :] = shares[i]


def attention_backward(images, parts, sc_grad, sc_out, powers_ref, grads, bias_acc):
    sc_q, sc_k, sc_v = parts
    sc_dq, sc_dk, sc_dv = grads
    lanes = head_lanes()
    depth = lanes.shape[1]
    everything = range(images)
    upstream = [window(sc_grad, i, images, ASKED) for i in everything]
    yield
    centred = [
        mm_nt(
            jnp.concatenate([upstream[i], window(sc_out, i, images, ASKED)], 1).astype(BF),
            jnp.concatenate([head_blocks(window(sc_v, i, images)), lanes], 1),
        )
        for i in everything
    ]
    yield
    powers = [powers_ref[0, 0, i].astype(F32) for i in everything]
    score_grads = [powers[i] * centred[i] for i in everything]
    low_grads = [one.astype(BF) for one in score_grads]
    total = low_grads[0].astype(F32)
    for i in everything[1:]:
        total = total + low_grads[i].astype(F32)
    bias_acc[...] += total
    yield
    d_queries = [mm(low_grads[i], head_blocks(window(sc_k, i, images))) for i in everything]
    yield
    empty = jnp.zeros((ASKED, depth), F32)
    d_both = [
        mm_tn(
            jnp.concatenate([score_grads[i], powers[i]], 0).astype(BF),
            jnp.concatenate(
                [
                    jnp.concatenate([window(sc_q, i, images, ASKED), empty], 1),
                    jnp.concatenate([empty, upstream[i]], 1),
                ],
                0,
            ).astype(BF),
        )
        for i in everything
    ]
    yield
    for i in everything:
        place = pl.ds(i, SLOT, stride=images)
        sc_dq[pl.ds(i, ASKED, stride=images), :] = d_queries[i] * SCALE
        sc_dk[place, :] = gather_heads(d_both[i][:, :depth]) * SCALE
        sc_dv[place, :] = gather_heads(d_both[i][:, depth:])


def put_upstream(count, sc_grad, sc_out, gradient, out, share):
    shared = gradient * share
    sc_grad[:count, :] = shared
    sc_out[:count, :] = -(shared * out)


def put_norm(refs, normed, inverse):
    normed_ref, inverse_ref = refs
    normed_ref[0, 0] = normed.astype(BF)
    inverse_ref[0, 0] = jnp.broadcast_to(inverse, normed.shape).astype(BF)


def get_norm(refs):
    normed_ref, inverse_ref = refs
    return normed_ref[0, 0].astype(F32), inverse_ref[0, 0].astype(F32)


def split_projection(hidden, w_qkv, qv_ref, layer, parts, count):
    query_bias, value_bias = qv_ref[layer, 0:1], qv_ref[layer, 1:2]
    projected = mm(hidden, w_qkv) + jnp.concatenate(
        [query_bias, jnp.zeros_like(query_bias), value_bias], 1
    )
    projected = projected.astype(BF).astype(F32)
    depth = hidden.shape[1]
    for n, ref in enumerate(parts):
        ref[:count, :] = projected[:, n * depth : (n + 1) * depth]


def gelu_parts(expanded):
    cumulative = 0.5 + 0.5 * lax.erf(expanded * (1.0 / math.sqrt(2.0)))
    density = jnp.exp(expanded * expanded * -0.5) * (1.0 / math.sqrt(2.0 * math.pi))
    return expanded * cumulative, cumulative + expanded * density


def kernel_first_layer(
    images, place, rims, x_ref, w_qkv, w_proj, w_fc1, w_fc2, gains, shifts, outs, qkv_bias, fc1_bias, bias,
    stream_out, hidden_out, out_out, share_out, powers_out, expanded_out,
    n_one, r_one, n_two, r_two, n_next, r_next,
    sc_q, sc_k, sc_v, sc_out, sc_share,
):
    count = POS * images
    zero_tails(first_of_grid(), count, sc_q, sc_k, sc_v)
    stream = tokens_of(x_ref)
    normed, inverse = norm_parts(stream)
    put_norm((n_one, r_one), normed, inverse)
    hidden = (normed * gains[0, 0:1] + shifts[0, 0:1]).astype(BF)
    split_projection(hidden, w_qkv[...], qkv_bias, 0, (sc_q, sc_k, sc_v), count)
    attention_forward(images, (sc_q, sc_k, sc_v), bias[...], None, powers_out, sc_out, sc_share)
    attended = sc_out[:count, :].astype(BF)
    out_out[0, 0] = attended
    share_out[0, 0] = sc_share[:count, :]
    middle = stream + (mm(attended, w_proj[...]) + outs[0, 0:1])
    normed, inverse = norm_parts(middle)
    put_norm((n_two, r_two), normed, inverse)
    inner = (normed * gains[0, 1:2] + shifts[0, 1:2]).astype(BF)
    expanded = mm(inner, w_fc1[...]) + fc1_bias[0:1]
    expanded_out[0, 0] = expanded.astype(BF)
    activated = gelu_parts(expanded)[0].astype(BF)
    stream = middle + mm(activated, w_fc2[...]) + outs[0, 1:2]
    stream_out[0, 0] = stream
    normed, inverse = norm_parts(stream)
    put_norm((n_next, r_next), normed, inverse)
    block = put_tokens(hidden_out, normed * gains[1, 0:1] + shifts[1, 0:1])
    if rims is not None:
        put_rims(block, rims, place, "first")


def kernel_shifted_forward(
    images, place, rims, hidden_ref, *refs
):
    halo, refs = (None, refs) if rims is None else (refs[:3], refs[3:])
    (
        w_qkv, qkv_bias, bias, masks, out_out, share_out, powers_out,
        held, sc_q, sc_k, sc_v, sc_out, sc_share,
    ) = refs
    count = POS * images
    zero_tails(first_of_grid(), count, sc_q, sc_k, sc_v)
    hidden = ahead_window(hidden_ref, halo, held, place).astype(BF)
    split_projection(hidden, w_qkv[...], qkv_bias, 1, (sc_q, sc_k, sc_v), count)
    attention_forward(images, (sc_q, sc_k, sc_v), bias[...], masks, powers_out, sc_out, sc_share)
    share_out[0, 0] = sc_share[:count, :]
    block = put_tokens(out_out, sc_out[:count, :])
    if rims is not None:
        put_rims(block, rims, place, "last")


def feed_forward_backward(out_low, inner, activated, slope, w_fc1, w_fc2):
    expanded_low = (slope * mm_nt(out_low, w_fc2)).astype(BF)
    inner_grad = mm_nt(expanded_low, w_fc1)
    return expanded_low, inner_grad


def put_rims(block, rims, place, edge):
    rim_rows, rim_cols, corner = rims
    row, col, rows, cols = place
    start = 0 if edge == "first" else WIN - SHIFT
    keep = slice(start, start + SHIFT)
    row_rim = row == (0 if edge == "first" else rows - 1)
    col_rim = col == (0 if edge == "first" else cols - 1)

    @pl.when(row_rim)
    def _():
        rim_rows[:, pl.ds(col * WIN, WIN)] = block[keep]

    @pl.when(col_rim)
    def _():
        rim_cols[pl.ds(row * WIN, WIN)] = block[:, keep]

    @pl.when(row_rim & col_rim)
    def _():
        corner[...] = block[keep, keep]


def ahead_window(field, rims, held, place):
    row, col, rows, cols = place
    top, left = row * WIN + SHIFT, col * WIN + SHIFT
    if rims is None:
        return tokens_of_block(field[pl.ds(top, WIN), pl.ds(left, WIN)])
    rim_rows, rim_cols, corner = rims
    own = WIN - SHIFT
    low, far = row == rows - 1, col == cols - 1
    held[:own, :own] = field[pl.ds(top, own), pl.ds(left, own)]

    @pl.when(low)
    def _():
        held[own:, :own] = rim_rows[:, pl.ds(left, own)]

    @pl.when(jnp.logical_not(low))
    def _():
        held[own:, :own] = field[pl.ds(top + own, SHIFT), pl.ds(left, own)]

    @pl.when(far)
    def _():
        held[:own, own:] = rim_cols[pl.ds(top, own)]

    @pl.when(jnp.logical_not(far))
    def _():
        held[:own, own:] = field[pl.ds(top, own), pl.ds(left + own, SHIFT)]

    @pl.when(low & far)
    def _():
        held[own:, own:] = corner[...]

    @pl.when(low & jnp.logical_not(far))
    def _():
        held[own:, own:] = rim_rows[:, pl.ds(left + own, SHIFT)]

    @pl.when(jnp.logical_not(low) & far)
    def _():
        held[own:, own:] = rim_cols[pl.ds(top + own, SHIFT)]

    return tokens_of_block(held[...])


def behind_window(field, rims, held, place):
    row, col, _, _ = place
    top, left = row * WIN, col * WIN
    if rims is None:
        return tokens_of_block(field[pl.ds(top - SHIFT, WIN), pl.ds(left - SHIFT, WIN)])
    rim_rows, rim_cols, corner = rims
    own = WIN - SHIFT
    high, near = row == 0, col == 0
    held[SHIFT:, SHIFT:] = field[pl.ds(top, own), pl.ds(left, own)]

    @pl.when(high)
    def _():
        held[:SHIFT, SHIFT:] = rim_rows[:, pl.ds(left, own)]

    @pl.when(jnp.logical_not(high))
    def _():
        held[:SHIFT, SHIFT:] = field[pl.ds(top - SHIFT, SHIFT), pl.ds(left, own)]

    @pl.when(near)
    def _():
        held[SHIFT:, :SHIFT] = rim_cols[pl.ds(top, own)]

    @pl.when(jnp.logical_not(near))
    def _():
        held[SHIFT:, :SHIFT] = field[pl.ds(top, own), pl.ds(left - SHIFT, SHIFT)]

    @pl.when(high & near)
    def _():
        held[:SHIFT, :SHIFT] = corner[...]

    @pl.when(high & jnp.logical_not(near))
    def _():
        held[:SHIFT, :SHIFT] = rim_rows[:, pl.ds(left - SHIFT, SHIFT)]

    @pl.when(jnp.logical_not(high) & near)
    def _():
        held[:SHIFT, :SHIFT] = rim_cols[pl.ds(top - SHIFT, SHIFT)]

    @pl.when(jnp.logical_not(high) & jnp.logical_not(near))
    def _():
        held[:SHIFT, :SHIFT] = field[pl.ds(top - SHIFT, SHIFT), pl.ds(left - SHIFT, SHIFT)]

    return tokens_of_block(held[...])


def kernel_middle(images, place, rims, out_ref, *refs):
    halo, refs = (None, refs) if rims is None else (refs[:3], refs[3:])
    (
        stream_ref, cot_ref, w_proj, w_fc1, w_fc2, gains, shifts, outs, fc1_bias,
        mixed_out, grad_out, low_out, g_proj, g_fc1, g_fc2, sums, fc1_sums, held,
    ) = refs
    stream = stream_ref[0, 0]
    attended = behind_window(out_ref, halo, held, place).astype(BF)
    middle = stream + (mm(attended, w_proj[...]) + outs[1, 0:1])
    normed, inverse = norm_parts(middle)
    inner = (normed * gains[1, 1:2] + shifts[1, 1:2]).astype(BF)
    activated, slope = gelu_parts(mm(inner, w_fc1[...]) + fc1_bias[1:2])
    activated = activated.astype(BF)
    put_tokens(mixed_out, middle + mm(activated, w_fc2[...]) + outs[1, 1:2])
    gradient = tokens_of(cot_ref)
    out_low = gradient.astype(BF)
    expanded_low, inner_grad = feed_forward_backward(
        out_low, inner, activated, slope, w_fc1[...], w_fc2[...]
    )
    g_fc2[...] += mm_tn(out_low, activated)
    g_fc1[...] += mm_tn(inner, expanded_low)
    fc1_sums[...] += fold_rows(expanded_low.astype(F32))
    norm_term = norm_backward(inner_grad, normed, inverse, gains[1, 1:2])
    updated = gradient + norm_term
    grad_out[0, 0] = updated
    branch_low = updated.astype(BF)
    g_proj[...] += mm_tn(attended, branch_low)
    block = put_tokens(low_out, mm_nt(branch_low, w_proj[...]))
    if rims is not None:
        put_rims(block, rims, place, "first")
    sums[0] += fold_rows(gradient)
    sums[1] += fold_rows(inner_grad * normed)
    sums[2] += fold_rows(inner_grad)
    sums[3] += fold_rows(branch_low.astype(F32))


def joined_gradients(count, grads, qv_sums):
    pieces = [ref[:count, :].astype(BF) for ref in grads]
    qv_sums[0] += fold_rows(pieces[0].astype(F32))
    qv_sums[1] += fold_rows(pieces[2].astype(F32))
    return jnp.concatenate(pieces, 1)


def kernel_shifted_backward(images, place, rims, hidden_ref, low_ref, *refs):
    halo, low_halo, refs = (
        (None, None, refs) if rims is None else (refs[:3], refs[3:6], refs[6:])
    )
    (
        out_ref, share_ref, powers_ref, w_qkv, qkv_bias, hidden_grad_out, g_qkv, qv_sums, bias_acc,
        held, sc_q, sc_k, sc_v, sc_out, sc_grad, sc_dq, sc_dk, sc_dv,
    ) = refs
    count = POS * images
    zero_tails(first_of_grid(), count, sc_q, sc_k, sc_v, sc_out, sc_grad)
    hidden = ahead_window(hidden_ref, halo, held, place).astype(BF)
    split_projection(hidden, w_qkv[...], qkv_bias, 1, (sc_q, sc_k, sc_v), count)
    gradient = ahead_window(low_ref, low_halo, held, place)
    put_upstream(count, sc_grad, sc_out, gradient, tokens_of(out_ref), share_ref[0, 0])
    grads = (sc_dq, sc_dk, sc_dv)
    yield from attention_backward(images, (sc_q, sc_k, sc_v), sc_grad, sc_out, powers_ref, grads, bias_acc)
    joined = joined_gradients(count, grads, qv_sums)
    g_qkv[...] += mm_tn(hidden, joined)
    block = put_tokens(hidden_grad_out, mm_nt(joined, w_qkv[...]))
    if rims is not None:
        put_rims(block, rims, place, "last")


def kernel_first_backward(
    images, place, rims, hidden_grad_ref, rim_rows, rim_cols, corner, grad_ref,
    n_one, r_one, n_two, r_two, n_next, r_next, expanded_ref, att_ref, share_ref, powers_ref,
    w_qkv, w_proj, w_fc1, w_fc2, gains, shifts, qkv_bias,
    tokens_grad_out, g_qkv, g_proj, g_fc1, g_fc2, sums, fc1_sums, qv_sums, bias_acc,
    held, sc_q, sc_k, sc_v, sc_out, sc_grad, sc_dq, sc_dk, sc_dv,
):
    count = POS * images
    zero_tails(first_of_grid(), count, sc_q, sc_k, sc_v, sc_out, sc_grad)
    upstream = behind_window(hidden_grad_ref, (rim_rows, rim_cols, corner), held, place)
    normed_one, inverse_one = get_norm((n_one, r_one))
    hidden = (normed_one * gains[0, 0:1] + shifts[0, 0:1]).astype(BF)
    normed, inverse = get_norm((n_next, r_next))
    gradient = grad_ref[0, 0] + norm_backward(upstream, normed, inverse, gains[1, 0:1])
    sums[4] += fold_rows(upstream * normed)
    sums[5] += fold_rows(upstream)
    yield
    out_low = gradient.astype(BF)
    normed, inverse = get_norm((n_two, r_two))
    inner = (normed * gains[0, 1:2] + shifts[0, 1:2]).astype(BF)
    activated, slope = gelu_parts(expanded_ref[0, 0].astype(F32))
    activated = activated.astype(BF)
    expanded_low, inner_grad = feed_forward_backward(
        out_low, inner, activated, slope, w_fc1[...], w_fc2[...]
    )
    yield
    updated = gradient + norm_backward(inner_grad, normed, inverse, gains[0, 1:2])
    branch_low = updated.astype(BF)
    yield
    low = mm_nt(branch_low, w_proj[...]).astype(BF).astype(F32)
    attended = att_ref[0, 0]
    yield
    split_projection(hidden, w_qkv[...], qkv_bias, 0, (sc_q, sc_k, sc_v), count)
    put_upstream(count, sc_grad, sc_out, low, attended.astype(F32), share_ref[0, 0])
    grads = (sc_dq, sc_dk, sc_dv)
    yield from attention_backward(images, (sc_q, sc_k, sc_v), sc_grad, sc_out, powers_ref, grads, bias_acc)
    g_fc2[...] += mm_tn(out_low, activated)
    g_fc1[...] += mm_tn(inner, expanded_low)
    g_proj[...] += mm_tn(attended, branch_low)
    fc1_sums[...] += fold_rows(expanded_low.astype(F32))
    sums[0] += fold_rows(out_low.astype(F32))
    sums[1] += fold_rows(inner_grad * normed)
    sums[2] += fold_rows(inner_grad)
    sums[3] += fold_rows(branch_low.astype(F32))
    yield
    joined = joined_gradients(count, grads, qv_sums)
    g_qkv[...] += mm_tn(hidden, joined)
    yield
    upstream = mm_nt(joined, w_qkv[...])
    term = norm_backward(upstream, normed_one, inverse_one, gains[0, 0:1])
    put_tokens(tokens_grad_out, updated + term)
    sums[6] += fold_rows(upstream * normed_one)
    sums[7] += fold_rows(upstream)


def shift_by(array, axis, by):
    count = lax.axis_size(axis)
    return lax.ppermute(array, axis, [(i, (i + by) % count) for i in range(count)])


def shift_both(array, by):
    rows, cols = lax.axis_size("seq"), lax.axis_size("wt")
    pairs = [
        (r * cols + c, ((r + by) % rows) * cols + (c + by) % cols)
        for r in range(rows)
        for c in range(cols)
    ]
    return lax.ppermute(array, ("seq", "wt"), pairs)


def send_rims(rims, by):
    rim_rows, rim_cols, corner = rims
    return (
        shift_by(rim_rows, "seq", by),
        shift_by(rim_cols, "wt", by),
        shift_both(corner, by),
    )


def window_order(part, rows, cols):
    if part == "all":
        return rows * cols, lambda i: (i // cols, i % cols)
    edge, rim = part
    if rim:
        base = 0 if edge == "first" else rows - 1
        side = 0 if edge == "first" else cols - 1
        skip = 1 if edge == "first" else 0
        return rows + cols - 1, lambda i: (
            jnp.where(i < cols, base, i - cols + skip),
            jnp.where(i < cols, i, side),
        )
    skip = 1 if edge == "first" else 0
    return (rows - 1) * (cols - 1), lambda i: (
        i // (cols - 1) + skip,
        i % (cols - 1) + skip,
    )


def axis_sizes():
    return lax.axis_size("seq"), lax.axis_size("wt")


def blocks_of(matrix):
    return [matrix[:, i : i + 128] for i in range(0, matrix.shape[1], 128)]


def pack_slices(w_qkv, w_proj, w_fc1, w_fc2):
    return jnp.concatenate([*blocks_of(w_qkv), w_proj, *blocks_of(w_fc1), w_fc2], 0)


def kernel_weights(parts, place_ref, *refs):
    pieces, (qkv, proj, fc1, fc2), (s_qkv, s_proj, s_fc1, s_fc2) = (
        refs[:parts], refs[parts : parts + 4], refs[parts + 4 :]
    )
    rows = s_qkv.shape[0] // parts
    for k in range(parts):
        owner = lax.rem(place_ref[0] + k, parts)
        piece = pieces[k][...].astype(F32)
        near = pl.ds(pl.multiple_of(owner * rows, rows), rows)
        at = 0
        for target in (s_qkv, s_proj, s_fc1):
            for i in range(0, target.shape[1], 128):
                target[near, i : i + 128] = piece[at : at + rows]
                at += rows
        far = s_fc2.shape[0] // parts
        s_fc2[pl.ds(pl.multiple_of(owner * far, far), far), :] = piece[at : at + far]
    for out, held in ((qkv, s_qkv), (proj, s_proj), (fc1, s_fc1), (fc2, s_fc2)):
        out[...] = held[...].astype(BF)


def whole_weights(place, packed, depth, wide):
    parts = lax.axis_size("wt")
    pieces = [packed] + [shift_by(packed, "wt", -k) for k in range(1, parts)]
    shapes = [(depth, 3 * depth), (depth, depth), (depth, wide), (wide, depth)]

    def body(*refs):
        kernel_weights(parts, *refs)

    full = pl.BlockSpec(memory_space=pltpu.VMEM)
    return pl.pallas_call(
        body,
        in_specs=[pl.BlockSpec(memory_space=pltpu.SMEM)] + [full] * parts,
        out_specs=[full] * 4,
        out_shape=[jax.ShapeDtypeStruct(shape, BF) for shape in shapes],
        scratch_shapes=[pltpu.VMEM(shape, F32) for shape in shapes],
    )(place, *pieces)


SMALL_ROWS = 8


def split_high(field):
    high = field.astype(BF)
    return high, (field - high.astype(F32)).astype(BF)


def small_rows(refs):
    (sums0, sums1, qv0, qv1, fc1_0, fc1_1, table) = refs

    def one(ref, k):
        return jnp.sum(ref[k], 0, keepdims=True)

    rows = [
        one(sums0, 6), one(sums0, 1), one(sums0, 4), one(sums1, 1),
        one(sums0, 7), one(sums0, 2), one(sums0, 5), one(sums1, 2),
        one(qv0, 0), one(qv0, 1), one(qv1, 0), one(qv1, 1),
        one(sums0, 3), one(sums0, 0), one(sums1, 3), one(sums1, 0),
    ]
    for ref in (fc1_0, fc1_1):
        line = jnp.sum(ref[...], 0, keepdims=True)
        rows += [line[:, i : i + 128] for i in range(0, line.shape[1], 128)]
    size = table.shape[1]
    for i in range(0, size, 128):
        piece = table[:, i : min(i + 128, size)]
        gap = 128 - piece.shape[1]
        if gap:
            piece = jnp.concatenate([piece, jnp.zeros((piece.shape[0], gap), F32)], 1)
        rows.append(piece)
    return rows


def kernel_pack(seqs, parts, each, *refs):
    grads, smalls, out, held, lines = refs[:8], refs[8:15], refs[15], refs[16], refs[17]
    depth = grads[0].shape[0]
    rows = depth // parts
    lines[...] = jnp.zeros_like(lines)
    at = 0
    for row in small_rows(smalls):
        lines[at : at + row.shape[0], :] = row
        at += row.shape[0]
    per = -(-at // seqs)
    turned = [grads[3][...].T, grads[7][...].T]
    for w in range(parts):
        near = slice(w * rows, (w + 1) * rows)
        at = 0
        for layer in range(2):
            for grad in grads[4 * layer : 4 * layer + 3]:
                for i in range(0, grad.shape[1], 128):
                    held[at : at + rows, :] = grad[near, i : i + 128]
                    at += rows
            far = turned[layer].shape[0] // parts
            held[at : at + far, :] = turned[layer][w * far : (w + 1) * far]
            at += far
        for s in range(seqs):
            mine = held[s * each : s * each + out.shape[1] - 2 * SMALL_ROWS, :]
            high, low = split_high(lines[s * per : s * per + SMALL_ROWS, :])
            out[s * parts + w] = jnp.concatenate(
                [mine, high.astype(F32), low.astype(F32)], 0
            ).astype(BF)


def kernel_reduce(packet_ref, out_ref):
    total = packet_ref[0].astype(F32)
    for i in range(1, packet_ref.shape[0]):
        total = total + packet_ref[i].astype(F32)
    rows = total.shape[0] - 2 * SMALL_ROWS
    high, low = split_high(total[rows : rows + SMALL_ROWS] + total[rows + SMALL_ROWS :])
    out_ref[...] = jnp.concatenate(
        [total[:rows], high.astype(F32), low.astype(F32)], 0
    ).astype(BF)


def kernel_unpack(each, per, packets, *refs):
    (gains, shifts, qkv, qv, table, proj, outs, fc1, fc1_bias, fc2, held, lines) = refs
    seqs, size, _ = packets.shape
    for s in range(seqs):
        packet = packets[s].astype(F32)
        start = size - 2 * SMALL_ROWS
        held[s * each : (s + 1) * each, :] = packet[:each]
        both = packet[start : start + SMALL_ROWS] + packet[start + SMALL_ROWS :]
        lines[s * per : (s + 1) * per, :] = both[:per]
    at = 0
    for layer in range(2):
        for target in (qkv, proj, fc1):
            rows = target.shape[1]
            for i in range(0, target.shape[2], 128):
                target[layer, :, i : i + 128] = held[at : at + rows, :]
                at += rows
        far = fc2.shape[1]
        fc2[layer] = held[at : at + far, :]
        at += far
    at = 0
    for target in (gains, shifts, qv, outs):
        for layer in range(2):
            target[layer] = lines[at : at + 2, :]
            at += 2
    for layer in range(2):
        for i in range(0, fc1_bias.shape[1], 128):
            fc1_bias[layer : layer + 1, i : i + 128] = lines[at : at + 1, :]
            at += 1
    for i in range(0, table.shape[2], 128):
        wide = min(128, table.shape[2] - i)
        for layer in range(2):
            table[layer, :, i : i + wide] = lines[at : at + HEADS, :wide]
            at += HEADS


def whole_kernel(body, inputs, outputs, scratch=()):
    full = pl.BlockSpec(memory_space=pltpu.VMEM)
    return pl.pallas_call(
        body,
        in_specs=[full] * len(inputs),
        out_specs=[full] * len(outputs),
        out_shape=[jax.ShapeDtypeStruct(*out) for out in outputs],
        scratch_shapes=[pltpu.VMEM(shape, F32) for shape in scratch],
        compiler_params=pltpu.CompilerParams(vmem_limit_bytes=VMEM_LIMIT),
    )(*inputs)


def sum_everywhere(grads, smalls, depth, wide):
    seqs, parts = axis_sizes()
    rows = depth // parts
    held = 2 * (4 * depth + 2 * wide) // parts
    each = held // seqs
    size = -(-each // 16) * 16 + 2 * SMALL_ROWS
    count = 16 + 2 * (wide // 128) + 2 * HEADS * -(-smalls[-1].shape[1] // 128)
    per = -(-count // seqs)
    tail = (seqs * per + SMALL_ROWS, 128)

    def pack(*refs):
        kernel_pack(seqs, parts, each, *refs)

    def unpack(*refs):
        kernel_unpack(each, per, *refs)

    (packets,) = whole_kernel(
        pack,
        [*grads, *smalls],
        [((seqs * parts, size, 128), BF)],
        [(held + 16, 128), tail],
    )
    packets = lax.all_to_all(packets, ("seq", "wt"), 0, 0, tiled=True)
    (mine,) = whole_kernel(kernel_reduce, [packets], [((size, 128), BF)])
    mine = lax.all_gather(mine, "seq", axis=0)
    return whole_kernel(
        unpack,
        [mine],
        [
            ((2, 2, depth), F32), ((2, 2, depth), F32), ((2, rows, 3 * depth), F32),
            ((2, 2, depth), F32), ((2, HEADS, smalls[-1].shape[1]), F32),
            ((2, rows, depth), F32),
            ((2, 2, depth), F32), ((2, rows, wide), F32), ((2, wide), F32),
            ((2, wide // parts, depth), F32),
        ],
        [(held, 128), tail],
    )


def per_device(
    tokens, region, rel_index, norm_gain, norm_bias, w_qkv, qv_bias, pos_table, w_proj, out_bias,
    w_fc1, fc1_bias, w_fc2, cotangent,
):
    images, height, width, depth = tokens.shape
    wide = w_fc1.shape[-1]
    rows, cols = height // WIN, width // WIN
    count = POS * images
    table_size = pos_table.shape[1]

    place = lax.axis_index("wt").astype(jnp.int32)[None]
    slices = [pack_slices(w_qkv[l], w_proj[l], w_fc1[l], w_fc2[l]) for l in range(2)]
    first_weights = whole_weights(place, slices[0], depth, wide)
    x = tokens.transpose(1, 2, 0, 3)
    cot = cotangent.transpose(1, 2, 0, 3)
    selector = (
        rel_index.reshape(-1)[:, None] == jnp.arange(table_size, dtype=jnp.int32)[None, :]
    ).astype(F32)
    tables = jnp.dot(
        selector,
        pos_table.transpose(1, 0, 2).reshape(table_size, 2 * HEADS) * LOG2E,
        precision=lax.Precision.HIGHEST,
    ).reshape(POS, POS, 2, HEADS)
    padded = jnp.pad(
        jnp.pad(tables.transpose(2, 0, 3, 1), ((0, 0), (0, ASKED - POS), (0, 0), (0, 0))),
        ((0, 0), (0, 0), (0, 0), (0, SLOT - POS)),
        constant_values=OFF,
    )
    biases = padded.reshape(2, ASKED, HEADS * SLOT)
    ids = region.reshape(images, rows, WIN, cols, WIN).transpose(1, 3, 0, 2, 4)
    ids = ids.reshape(rows, cols, images, POS)
    apart = (ids[..., :, None] != ids[..., None, :]).astype(BF)
    apart = jnp.pad(apart, [(0, 0)] * 3 + [(0, ASKED - POS), (0, SLOT - POS)])
    masks = jnp.concatenate([apart, apart], -1)

    first_weights, masks = lax.optimization_barrier((first_weights, masks))

    field_shape = (height, width, images, depth)
    field = ((WIN, WIN, images, depth), lambda r, c: (r, c, 0, 0))
    probs_spec = ((1, 1, images, ASKED, HEADS * SLOT), lambda r, c: (r, c, 0, 0, 0))
    mask_spec = ((1, 1, images, ASKED, 2 * SLOT), lambda r, c: (r, c, 0, 0, 0))

    def flat(columns):
        return (1, 1, count, columns), lambda r, c: (r, c, 0, 0)

    def flat_type(columns, dtype):
        return jax.ShapeDtypeStruct((rows, cols, count, columns), dtype)

    probs_type = jax.ShapeDtypeStruct((rows, cols, images, ASKED, HEADS * SLOT), BF)
    rim_types = [
        jax.ShapeDtypeStruct((SHIFT, width, images, depth), BF),
        jax.ShapeDtypeStruct((height, SHIFT, images, depth), BF),
        jax.ShapeDtypeStruct((SHIFT, SHIFT, images, depth), BF),
    ]

    def run(kernel, part, inputs, outputs, slots, limit, earlier=None, held=False, group=1):
        steps, order = window_order(part, rows, cols // group)

        def spec_of(spec, shape):
            if spec is None:
                return pl.BlockSpec(tuple(shape), lambda i: (0,) * len(shape))
            block, index = spec
            block = (block[0], block[1] * group, *block[2:])
            return pl.BlockSpec(block, lambda i: index(*order(i)))

        with_rims = part != "all" and part[1]
        n_in, n_out = len(inputs), len(outputs)
        ins = [a for a, _ in inputs]
        in_specs = [spec_of(spec, a.shape) for a, spec in inputs]
        aliases = {}
        if earlier is not None:
            for n, (array, (_, spec)) in enumerate(zip(earlier, outputs)):
                if spec is not None:
                    aliases[len(ins)] = n
                ins.append(array)
                in_specs.append(
                    spec_of(None, array.shape)
                    if spec is None
                    else pl.BlockSpec(memory_space=pl.ANY)
                )
        n_all = len(ins)
        types = [t for t, _ in outputs] + (rim_types if with_rims else [])
        out_specs = [spec_of(spec, t.shape) for t, spec in outputs]
        out_specs += [spec_of(None, t.shape) for t in rim_types] if with_rims else []

        def body(*refs):
            row, col = order(pl.program_id(0))
            outs = refs[n_all : n_all + n_out]
            rims = refs[n_all + n_out : n_all + n_out + 3] if with_rims else None
            rest = refs[n_all + len(types) :]

            @pl.when(first_of_grid())
            def _():
                for n, (_, spec) in enumerate(outputs):
                    if spec is None:
                        if earlier is None:
                            outs[n][...] = jnp.zeros_like(outs[n])
                        else:
                            outs[n][...] = refs[n_in + n][...]

            def view(ref, spec, k):
                if spec is None or group == 1:
                    return ref
                size = spec[0][1]
                return ref.at[:, pl.ds(k * size, size)]

            each = len(rest) // group
            runs = [
                kernel(
                    images,
                    (row, col * group + k, rows, cols),
                    rims,
                    *[view(ref, spec, k) for ref, (_, spec) in zip(refs[:n_in], inputs)],
                    *[view(ref, spec, k) for ref, (_, spec) in zip(outs, outputs)],
                    *rest[k * each : (k + 1) * each],
                )
                for k in range(group)
            ]
            done = object()
            runs = [one for one in runs if one is not None]
            while runs:
                runs = [one for one in runs if next(one, done) is not done]

        scratch = [pltpu.VMEM((WIN, WIN, images, depth), BF)] if held else []
        scratch += [pltpu.VMEM((SLOT * images, depth), F32)] * slots
        results = pl.pallas_call(
            body,
            grid=(steps,),
            in_specs=in_specs,
            out_specs=out_specs,
            out_shape=types,
            scratch_shapes=scratch * group,
            input_output_aliases=aliases,
            compiler_params=pltpu.CompilerParams(vmem_limit_bytes=limit * MIB),
            cost_estimate=pl.CostEstimate(
                flops=steps * 10**9, bytes_accessed=10**7, transcendentals=0
            ),
        )(*ins)
        return results[:n_out], results[n_out:]

    def run_both(kernel, edge, inputs, halos, outputs, slots, by, limits, held=False, beside=None):
        lead = len(halos)
        rim_inputs = [(a, None) for halo in halos for a in halo]
        inputs_a = inputs[:lead] + rim_inputs + inputs[lead:]
        first, rims = run(
            kernel, (edge, True), inputs_a, outputs, slots, limits[0], held=held
        )
        if beside is not None:
            rims, beside = lax.optimization_barrier((rims, beside))
            beside = whole_weights(place, beside, depth, wide)
        rims = send_rims(rims, by)
        second, _ = run(
            kernel, (edge, False), inputs, outputs, slots, limits[1], first, held=held
        )
        return (second, rims) if beside is None else (second, rims, beside)

    def total(*shape):
        return (jax.ShapeDtypeStruct(shape, F32), None)

    qkv0, proj0, fc10, fc20 = first_weights
    (
        (stream1, hidden1, att0, share0, powers0, expanded0, *norms0),
        halo,
        (qkv1, proj1, fc11, fc21),
    ) = run_both(
        kernel_first_layer,
        "first",
        [
            (x, field), (qkv0, None), (proj0, None), (fc10, None), (fc20, None), (norm_gain, None),
            (norm_bias, None), (out_bias, None), (qv_bias, None), (fc1_bias, None),
            (biases[0], None),
        ],
        [],
        [
            (flat_type(depth, F32), flat(depth)),
            (jax.ShapeDtypeStruct(field_shape, BF), field),
            (flat_type(depth, BF), flat(depth)),
            (flat_type(depth, F32), flat(depth)),
            (probs_type, probs_spec),
            (flat_type(wide, BF), flat(wide)),
            *[(flat_type(depth, BF), flat(depth))] * 6,
        ],
        5,
        -1,
        LIMITS[0],
        beside=slices[1],
    )
    (att1, share1, powers1), out_halo = run_both(
        kernel_shifted_forward,
        "last",
        [
            (hidden1, None), (qkv1, None), (qv_bias, None), (biases[1], None),
            (masks, mask_spec),
        ],
        [halo],
        [
            (jax.ShapeDtypeStruct(field_shape, BF), field),
            (flat_type(depth, F32), flat(depth)),
            (probs_type, probs_spec),
        ],
        5,
        1,
        LIMITS[1],
        held=True,
    )
    (mixed, grad1, low1, g_proj1, g_fc11, g_fc21, sums1, fc1_sums1), low_halo = run_both(
        kernel_middle,
        "first",
        [
            (att1, None), (stream1, flat(depth)), (cot, field), (proj1, None),
            (fc11, None), (fc21, None), (norm_gain, None), (norm_bias, None),
            (out_bias, None), (fc1_bias, None),
        ],
        [out_halo],
        [
            (jax.ShapeDtypeStruct(field_shape, BF), field),
            (flat_type(depth, F32), flat(depth)),
            (jax.ShapeDtypeStruct(field_shape, BF), field),
            total(depth, depth), total(depth, wide), total(depth, wide), total(4, 8, depth),
            total(8, wide),
        ],
        0,
        -1,
        LIMITS[2],
        held=True,
    )
    (hidden_grad1, g_qkv1, qv_sums1, bias_sums1), grad_halo = run_both(
        kernel_shifted_backward,
        "last",
        [
            (hidden1, None), (low1, None), (att1, field), (share1, flat(depth)),
            (powers1, probs_spec),
            (qkv1, None), (qv_bias, None),
        ],
        [halo, low_halo],
        [
            (jax.ShapeDtypeStruct(field_shape, BF), field),
            total(depth, 3 * depth), total(2, 8, depth), total(ASKED, HEADS * SLOT),
        ],
        8,
        1,
        LIMITS[3],
        held=True,
    )
    (
        tokens_grad, g_qkv0, g_proj0, g_fc10, g_fc20, sums0, fc1_sums0, qv_sums0, bias_sums0
    ), _ = run(
        kernel_first_backward,
        "all",
        [
            (hidden_grad1, None), *[(a, None) for a in grad_halo], (grad1, flat(depth)),
            *[(a, flat(depth)) for a in norms0], (expanded0, flat(wide)),
            (att0, flat(depth)), (share0, flat(depth)), (powers0, probs_spec),
            (qkv0, None), (proj0, None), (fc10, None), (fc20, None), (norm_gain, None),
            (norm_bias, None), (qv_bias, None),
        ],
        [
            (jax.ShapeDtypeStruct(field_shape, F32), field),
            total(depth, 3 * depth), total(depth, depth), total(depth, wide), total(depth, wide),
            total(8, 8, depth), total(8, wide), total(2, 8, depth), total(ASKED, HEADS * SLOT),
        ],
        8,
        LIMITS[4],
        held=True,
        group=GROUP,
    )

    bias_sums = jnp.stack([bias_sums0, bias_sums1]).reshape(2, ASKED, HEADS, SLOT)
    bias_sums = bias_sums[:, :POS, :, :POS].transpose(0, 2, 1, 3).reshape(2 * HEADS, POS * POS)
    table = jnp.dot(bias_sums, selector, precision=lax.Precision.HIGHEST)
    gains, shifts, d_qkv, d_qv, d_table, d_proj, d_out, d_fc1, d_fc1_bias, d_fc2 = sum_everywhere(
        [g_qkv0, g_proj0, g_fc10, g_fc20, g_qkv1, g_proj1, g_fc11, g_fc21],
        [sums0, sums1, qv_sums0, qv_sums1, fc1_sums0, fc1_sums1, table],
        depth,
        wide,
    )
    d_table = d_table.transpose(0, 2, 1)
    return (
        mixed.transpose(2, 0, 1, 3), tokens_grad.transpose(2, 0, 1, 3), gains, shifts, d_qkv,
        d_qv, d_table, d_proj, d_out, d_fc1, d_fc1_bias, d_fc2,
    )


def solution(mesh):
    field = P(None, "seq", "wt", None)
    shared = P(None, "wt", None)
    return jax.shard_map(
        per_device,
        mesh=mesh,
        in_specs=(
            field, P(None, "seq", "wt"), P(), P(), P(), shared, P(), P(), shared, P(), shared, P(),
            shared, field,
        ),
        out_specs=(
            field, field, P(), P(), shared, P(), P(), shared, P(), shared, P(), shared,
        ),
        check_vma=False,
    )
```
